32 devices in a mesh: gx: 4 (over x, core), gy: 4 (over z), gz: 2 (over y).
Axes of the slice: x: 2, y: 2, z: 4, core: 2. Of those that a mesh axis runs over, the one named last changes fastest.
Arguments:
- body_pos: float32 [3, 16384], P(None, ('gx', 'gy', 'gz')), may hold values from -1 to 1
- body_mass: float32 [16384], P(('gx', 'gy', 'gz')), may hold values from 0.003 to 0.03
- cell_mass: float32 [65536], P(('gx', 'gy', 'gz')), may hold values from 0.003 to 0.03
- cell_center: float32 [3, 65536], P(None, ('gx', 'gy', 'gz')), may hold values from -1 to 1
- cell_quad: float32 [6, 65536], P(None, ('gx', 'gy', 'gz')), may hold values from -0.001 to 0.001
- cell_lists: int32 [32, 5, 1024], P(('gx', 'gy', 'gz')), may hold values from 0 to 6143, as said below
- slot_masks: int32 [32, 5, 1024], P(('gx', 'gy', 'gz')), may hold values from 0 to 1, as said below
- face_lists: int32 [32, 2, 4], P(('gx', 'gy', 'gz')), may hold values from 0 to 3, as said below
- face_counts: int32 [32, 2], P(('gx', 'gy', 'gz')), may hold values from 1 to 4
Outputs:
- accel: float32 [3, 16384], P(None, ('gx', 'gy', 'gz'))
The draws below stay inside these ranges and needn't reach their ends.
Inputs may be any that keep to these rules, and one draw needn't show every extreme that they name: `cell_lists`: at level l (from 0) every entry is below 2048 + l * 1024, and the 1024 entries of one level of one domain are distinct. `slot_masks`: each level of each domain has exactly 768 ones. `face_lists`: each side's list of a domain is a permutation of its 4 blocks.
All inputs are finite; a program needn't handle non-finite values.
Results may differ from the reference program's by a relative error of at most 0.00002.
Values sent between devices are 32-bit elements; how exact they have to be, the bound alone decides.
No kernel may reach another device: no remote copies, remote signals or barrier semaphores. Data moves between devices by JAX's collectives and lax.ppermute only.
A program may use at most 64 MiB of HBM per device.

```python
import math
import jax
import jax.numpy as jnp
from jax import lax

CELLS = 2048
K = 1024
KV = 768
NBLK = 4
BLK = 128
LEVELS = 5
DOMAINS = 32
ZDOMAINS = 2
BOD = 512
NBODY = 16384
NCELL = 65536


def draw_cell_lists(key, part):
    span = CELLS + (LEVELS - 1) * K
    spread = 2 ** 30 // span
    positions = jnp.arange(span).astype(jnp.int32)

    def one_device(device_key):

        def one_level(level_no):
            level_key = jax.random.fold_in(device_key, level_no)
            limit = CELLS + level_no * K
            scores = jax.random.randint(level_key, (span,), 0, spread) * span + positions
            scores = jnp.where(positions < limit, scores, 2 ** 30 + positions)
            return jnp.argsort(scores, stable=True)[:K].astype(jnp.int32)
        return lax.map(one_level, jnp.arange(LEVELS).astype(jnp.int32))
    device_keys = jax.random.split(jax.random.fold_in(key, 11), DOMAINS)
    return lax.map(one_device, device_keys)


def draw_slot_masks(key, part):
    slot_keys = jax.random.split(jax.random.fold_in(key, 23), DOMAINS * LEVELS)
    orders = jax.vmap(lambda one_key: jax.random.permutation(one_key, K))(slot_keys)
    return (orders < KV).astype(jnp.int32).reshape(DOMAINS, LEVELS, K)


def draw_face_lists(key, part):
    side_keys = jax.random.split(jax.random.fold_in(key, 37), DOMAINS * 2)
    orders = jax.vmap(lambda one_key: jax.random.permutation(one_key, NBLK))(side_keys)
    return orders.astype(jnp.int32).reshape(DOMAINS, 2, NBLK)


def draw_face_counts(key, part):
    counts = jax.random.randint(jax.random.fold_in(key, 41), (DOMAINS, 2), 1, NBLK + 1)
    counts = counts.at[0, 0].set(NBLK)
    counts = counts.at[1, 1].set(1)
    return counts.astype(jnp.int32)


def block_scale(rng, shape, shards, low, top_value):
    factor_of, own = 1.0, jax.random.fold_in(rng, 6)
    for axis_at, shards_of in shards:
        heights = jnp.exp(jax.random.uniform(jax.random.fold_in(own, axis_at), (shards_of,), jnp.float32, low / len(shards), top_value / len(shards)))
        factor_of = factor_of * jnp.repeat(heights, shape[axis_at] // shards_of).reshape([-1 if axis == axis_at else 1 for axis in range(len(shape))])
    return factor_of


def setup_inputs(seed: int = 0) -> dict:
    arg_keys = jax.random.split(jax.random.key(seed), 10)
    body_pos = jnp.clip(jax.random.uniform(arg_keys[0], (3, NBODY), jnp.float32, -1.0, 1.0) * block_scale(arg_keys[0], (3, NBODY), ((1, 32),), -0.4, 0.0), -1.0, 1.0)
    body_mass = jnp.clip(jnp.exp(math.log(0.03) - 2.3025851 * jax.random.uniform(arg_keys[1], (NBODY,), jnp.float32) ** block_scale(arg_keys[1], (NBODY,), ((0, 32),), -0.2, 0.2)), 0.003, 0.03)
    cell_mass = jnp.clip(jnp.exp(math.log(0.03) - 2.3025851 * jax.random.uniform(arg_keys[2], (NCELL,), jnp.float32) ** block_scale(arg_keys[2], (NCELL,), ((0, 32),), -0.2, 0.2)), 0.003, 0.03)
    cell_center = jnp.clip(jax.random.uniform(arg_keys[3], (3, NCELL), jnp.float32, -1.0, 1.0) * block_scale(arg_keys[3], (3, NCELL), ((1, 32),), -0.4, 0.0), -1.0, 1.0)
    cell_quad = jnp.clip(jax.random.uniform(arg_keys[4], (6, NCELL), jnp.float32, -0.001, 0.001) * block_scale(arg_keys[4], (6, NCELL), ((1, 32),), -0.4, 0.0), -0.001, 0.001)
    cell_lists = draw_cell_lists(jax.random.fold_in(arg_keys[9], 71), 0)
    slot_masks = draw_slot_masks(jax.random.fold_in(arg_keys[9], 71), 0)
    face_lists = draw_face_lists(jax.random.fold_in(arg_keys[9], 71), 0)
    face_counts = draw_face_counts(jax.random.fold_in(arg_keys[9], 71), 0)
    return dict(body_pos=body_pos, body_mass=body_mass, cell_mass=cell_mass, cell_center=cell_center, cell_quad=cell_quad, cell_lists=cell_lists, slot_masks=slot_masks, face_lists=face_lists, face_counts=face_counts)


soften = 0.01

def tile_accel(targets, sources):
    offset = targets[:, :, None] - sources[1:4, None, :]
    distance = lax.optimization_barrier(jnp.sum(offset * offset, axis=0)) + soften
    inverse_one = lax.rsqrt(distance)
    inverse_two = inverse_one * inverse_one
    inverse_three = inverse_one * inverse_two
    radial = -sources[0][None, :] * inverse_three
    if sources.shape[0] == 10:
        quadrupole = sources[4:10]
        quad_x = quadrupole[0][None, :] * offset[0] + quadrupole[3][None, :] * offset[1] + quadrupole[4][None, :] * offset[2]
        quad_y = quadrupole[3][None, :] * offset[0] + quadrupole[1][None, :] * offset[1] + quadrupole[5][None, :] * offset[2]
        quad_z = quadrupole[4][None, :] * offset[0] + quadrupole[5][None, :] * offset[1] + quadrupole[2][None, :] * offset[2]
        inverse_five = inverse_three * inverse_two
        quad_form = offset[0] * quad_x + offset[1] * quad_y + offset[2] * quad_z
        radial = radial - 2.5 * quad_form * inverse_five * inverse_two
        return jnp.stack([lax.optimization_barrier(jnp.sum(radial * offset[0] + quad_x * inverse_five, axis=1)), lax.optimization_barrier(jnp.sum(radial * offset[1] + quad_y * inverse_five, axis=1)), lax.optimization_barrier(jnp.sum(radial * offset[2] + quad_z * inverse_five, axis=1))])
    return lax.optimization_barrier(jnp.sum(radial[None] * offset, axis=2))

def domain_accel(inputs):
    targets, held_cells, near_bodies = inputs
    return tile_accel(targets, held_cells) + tile_accel(targets, near_bodies)

def reference(body_pos, body_mass, cell_mass, cell_center, cell_quad, cell_lists, slot_masks, face_lists, face_counts):
    bit_count = DOMAINS.bit_length() - 1
    domain_ids = jnp.arange(DOMAINS).astype(jnp.int32)
    own_cells = jnp.concatenate([cell_mass[None], cell_center, cell_quad], 0)
    held_cells = own_cells.reshape(10, DOMAINS, CELLS).transpose(1, 0, 2)
    for level_no in range(LEVELS):
        partner = domain_ids ^ 1 << bit_count - 1 - level_no
        picked = jax.vmap(lambda cells_held, slot_index: jnp.take(cells_held, slot_index, axis=1))(held_cells, cell_lists[:, level_no, :])
        picked = picked * slot_masks[:, level_no, None, :].astype(picked.dtype)
        held_cells = jnp.concatenate([held_cells, picked[partner]], axis=2)
    bodies = jnp.concatenate([body_mass[None], body_pos], 0).reshape(4, DOMAINS, NBLK, BLK).transpose(1, 0, 2, 3)
    selected = jax.vmap(lambda blocks, block_index: jnp.take(blocks, block_index, axis=1))(bodies, face_lists.reshape(DOMAINS, 2 * NBLK))
    live_slots = jnp.arange(NBLK).astype(jnp.int32)[None, None, :] < face_counts[:, :, None]
    selected = selected * live_slots.reshape(DOMAINS, 1, 2 * NBLK, 1).astype(selected.dtype)
    selected = selected.reshape(DOMAINS, 4, 2, NBLK * BLK)
    z_index = domain_ids % ZDOMAINS
    lower_ids = jnp.maximum(domain_ids - 1, 0)
    upper_ids = jnp.minimum(domain_ids + 1, DOMAINS - 1)
    from_lower = jnp.where((z_index > 0)[:, None, None], selected[lower_ids][:, :, 1, :], 0.0)
    from_upper = jnp.where((z_index < ZDOMAINS - 1)[:, None, None], selected[upper_ids][:, :, 0, :], 0.0)
    near_bodies = jnp.concatenate([bodies.reshape(DOMAINS, 4, BOD), from_lower, from_upper], axis=2)
    targets = body_pos.reshape(3, DOMAINS, BOD).transpose(1, 0, 2)
    accelerations = lax.map(domain_accel, (targets, held_cells, near_bodies))
    return accelerations.transpose(1, 0, 2).reshape(3, DOMAINS * BOD)
```

```python
import functools
import math

import jax
import jax.numpy as jnp
from jax import lax
from jax.experimental import pallas as pl
from jax.experimental.pallas import tpu as pltpu
from jax.sharding import PartitionSpec as P

AXES = ("gx", "gy", "gz")
LANES = 128
SUBS = 8
NBLK = 4
SOFT = 0.01
QROWS = 64
SROWS = 32
FROWS = 48
UNIT = 256
A_PART = (0, 0, 1, 1, 0, 2)
B_PART = (0, 1, 0, 1, 2, 0)

f32 = jnp.float32
bf16 = jnp.bfloat16
dot = functools.partial(jnp.dot, preferred_element_type=f32)


def split3(value):
    one = value.astype(bf16).astype(f32)
    rest = value - one
    two = rest.astype(bf16).astype(f32)
    three = (rest - two).astype(bf16).astype(f32)
    return one, two, three


def halves(value):
    high = value.astype(bf16)
    return high, (value - high.astype(f32)).astype(bf16)


def paired(values, parts):
    pieces = [split3(v) for v in values]
    return [p[k] for k in parts for p in pieces]


def quad_rows(mass, center, quad):
    cx, cy, cz = center
    qxx, qyy, qzz, qxy, qxz, qyz = quad
    vx = qxx * cx + qxy * cy + qxz * cz
    vy = qxy * cx + qyy * cy + qyz * cz
    vz = qxz * cx + qyz * cy + qzz * cz
    h = 2.5 / jnp.maximum(mass, 1e-3)
    linear = [-2.0 * h * vx, -2.0 * h * vy, -2.0 * h * vz]
    square = [h * qxx, h * qyy, h * qzz, 2.0 * h * qxy, 2.0 * h * qxz, 2.0 * h * qyz]
    rows = list(split3(h * (cx * vx + cy * vy + cz * vz)))
    rows += paired(linear + square, B_PART)
    rows += [jnp.zeros_like(mass)] * (QROWS - len(rows))
    return rows, (vx, vy, vz)


def dist_rows(mass, center):
    cx, cy, cz = center
    rows = list(split3(cx * cx + cy * cy + cz * cz + SOFT))
    rows += paired([-2.0 * cx, -2.0 * cy, -2.0 * cz], B_PART)
    rows += [jnp.ones_like(mass)] * 3
    rows += [jnp.zeros_like(mass)] * (SROWS - len(rows))
    return rows


def mass_rows(mass, center):
    cx, cy, cz = center
    rows = paired([mass, mass * cx, mass * cy, mass * cz], (0, 1, 2))
    return rows + [jnp.zeros_like(mass)] * (16 - len(rows))


def moment_rows(quad, v):
    rows = paired(list(quad) + list(v), (0, 1, 2))
    return rows + [jnp.zeros_like(v[0])] * (32 - len(rows))


def target_rows(x, y, z):
    one = jnp.ones_like(x)
    zero = jnp.zeros_like(x)
    q = [one] * 3 + paired([x, y, z, x * x, y * y, z * z, x * y, x * z, y * z], A_PART)
    q += [zero] * (QROWS - len(q))
    s = [one] * 3 + paired([x, y, z], A_PART) + list(split3(x * x + y * y + z * z))
    s += [zero] * (SROWS - len(s))
    return q, s


def stage_rows(feat, rows, sub):
    for k, value in enumerate(rows):
        feat[k * sub : (k + 1) * sub, :] = value


def cell_features(read, sub, feat, lhs, fw, fu, base):
    mass, center, quad = read
    q, v = quad_rows(mass, center, quad)
    rows = q + dist_rows(mass, center) + mass_rows(mass, center) + moment_rows(quad, v)
    stage_rows(feat, rows, sub)
    wide = QROWS + SROWS
    for r in range(sub):
        at = slice(base + r * LANES, base + (r + 1) * LANES)
        left = feat[pl.ds(r, wide, stride=sub), :]
        lhs[at, 0:wide] = left.T.astype(bf16)
        right = feat[pl.ds(wide * sub + r, FROWS, stride=sub), :]
        fw[:, at] = right[0:16].astype(bf16)
        fu[:, at] = right[16:FROWS].astype(bf16)


def body_features(mass, center, sub, feat, lhs, fw, base):
    rows = dist_rows(mass, center) + mass_rows(mass, center)
    stage_rows(feat, rows, sub)
    for r in range(sub):
        at = slice(base + r * LANES, base + (r + 1) * LANES)
        left = feat[pl.ds(r, SROWS, stride=sub), :]
        lhs[at, 0:SROWS] = left.T.astype(bf16)
        right = feat[pl.ds(SROWS * sub + r, 16, stride=sub), :]
        fw[:, at] = right.astype(bf16)


def twice(left, high, low):
    return dot(jnp.concatenate([left, left], 1), jnp.concatenate([high, low], 0))


def pair_sums(cells, bodies, at_q, at_s, lhs, fw, fu, blhs, bfw, aw, au):
    targets = at_q.shape[1]
    wide = math.gcd(targets, UNIT)
    units = []
    for count, is_cell in ((cells, True), (bodies, False)):
        deep = math.gcd(count, UNIT) if count else 1
        for b in range(count // deep):
            for t in range(targets // wide):
                units.append((slice(b * deep, (b + 1) * deep), slice(t * wide, (t + 1) * wide), is_cell))
    aw[...] = jnp.zeros_like(aw)
    au[...] = jnp.zeros_like(au)

    def first(src, tgt, is_cell):
        if not is_cell:
            return dot(blhs[src, 0:SROWS], at_s[QROWS : QROWS + SROWS, tgt]), None
        s = dot(lhs[src, 0 : QROWS + SROWS], at_s[:, tgt])
        return s, dot(lhs[src, 0:QROWS], at_q[:, tgt])

    def second(src, tgt, is_cell, s, q):
        y = lax.rsqrt(s)
        y2 = y * y
        y3 = y * y2
        if not is_cell:
            aw[:, tgt] += twice(bfw[:, src], *halves(y3))
            return
        y5 = y3 * y2
        w = y3 + (q * y2) * y5
        aw[:, tgt] += twice(fw[:, src], *halves(w))
        au[:, tgt] += twice(fu[:, src], *halves(y5))

    ready = first(*units[0])
    for k, unit in enumerate(units):
        coming = first(*units[k + 1]) if k + 1 < len(units) else None
        second(*unit, *ready)
        ready = coming


def from_sums(x, y, z, aw, au):
    w = aw[0:4, :] + aw[4:8, :] + aw[8:12, :]
    u = au[0:9, :] + au[9:18, :] + au[18:27, :]

    def g(k):
        return u[k : k + 1, :]

    return (
        g(0) * x + g(3) * y + g(4) * z - g(6) - (w[0:1] * x - w[1:2]),
        g(3) * x + g(1) * y + g(5) * z - g(7) - (w[0:1] * y - w[2:3]),
        g(4) * x + g(5) * y + g(2) * z - g(8) - (w[0:1] * z - w[3:4]),
    )


def open_kernel(mass, center, quad, lists, masks, own, place, pick, vm, vc, vq, vl, vk, tab, sems):
    moves = [
        pltpu.make_async_copy(src, dst, sems.at[k])
        for k, (src, dst) in enumerate(((lists, vl), (masks, vk), (mass, vm), (center, vc), (quad, vq)))
    ]
    for move in moves:
        move.start()
    levels = lists.shape[0]
    moves[0].wait()
    moves[1].wait()
    slots = lists.shape[1] // LANES
    for level in range(levels):
        for r in range(slots):
            at = slice(r * LANES, (r + 1) * LANES)
            index = vl[level : level + 1, at]
            live = vk[level : level + 1, at]
            place[2 * level * slots + r : 2 * level * slots + r + 1, :] = jnp.where(live > 0, index >> 7, -1)
            place[(2 * level + 1) * slots + r : (2 * level + 1) * slots + r + 1, :] = index & (LANES - 1)
    moves[2].wait()
    moves[3].wait()
    moves[4].wait()
    rows = center.shape[1] // LANES
    for k in range(rows):
        at = slice(k * LANES, (k + 1) * LANES)
        tab[k * 16 : k * 16 + 1, :] = vm[k : k + 1, :]
        tab[k * 16 + 1 : k * 16 + 4, :] = vc[:, at]
        tab[k * 16 + 4 : k * 16 + 10, :] = vq[:, at]
    for f in range(10):
        own[f * rows : (f + 1) * rows, :] = tab[pl.ds(f, rows, stride=16), :]
    picked(0, [own], place, pick)


def picked(level, tables, place, pick):
    slots = pick.shape[0] // 10 if pick.shape[0] % 10 == 0 else SUBS
    row = place[2 * level * slots : (2 * level + 1) * slots, :]
    lane = place[(2 * level + 1) * slots : (2 * level + 2) * slots, :]
    out = [jnp.zeros((slots, LANES), f32)] * 10
    base = 0
    for table in tables:
        rows = table.shape[0] // 10
        for k in range(rows):
            hit = row == base + k
            for f in range(10):
                line = jnp.broadcast_to(table[f * rows + k : f * rows + k + 1, :], (slots, LANES))
                got = jnp.take_along_axis(line, lane, axis=1, mode="promise_in_bounds")
                out[f] = jnp.where(hit, got, out[f])
        base += rows
    for f in range(10):
        pick[f * slots : (f + 1) * slots, :] = out[f]


def pick_kernel(level, *refs):
    place, *tables = refs[:-1]
    picked(level, tables, place, refs[-1])


def read_cells(table, first, count, mid):
    rows = table.shape[0] // 10

    def row(f):
        return table[f * rows + first : f * rows + first + count, :]

    center = [row(1 + k) - mid[k : k + 1, :] for k in range(3)]
    return row(0), center, [row(4 + k) for k in range(6)]


def start_kernel(pos, mass, lists, counts, at_q, at_s, shifted, mid, face, bod, out, feat, blhs, bfw, aw, au):
    count = pos.shape[1]
    blocks = count // LANES
    low = jnp.min(pos[...], axis=1, keepdims=True)
    high = jnp.max(pos[...], axis=1, keepdims=True)
    middle = jnp.broadcast_to(0.5 * (low + high), (3, LANES))
    mid[0:3, :] = middle
    moved = pos[...] - middle[:, 0:1]
    shifted[0:3, :] = moved
    x, y, z = moved[0:1], moved[1:2], moved[2:3]
    q, s = target_rows(x, y, z)
    at_q[...] = jnp.concatenate(q, axis=0).astype(bf16)
    at_s[...] = jnp.concatenate([jnp.zeros_like(x)] * QROWS + s, axis=0).astype(bf16)
    bod[0:blocks, :] = mass[...]
    for f in range(3):
        for k in range(blocks):
            at = slice(k * LANES, (k + 1) * LANES)
            bod[(f + 1) * blocks + k : (f + 1) * blocks + k + 1, :] = pos[f : f + 1, at]
    for side in range(2):
        for j in range(blocks):
            block = lists[side, j]
            live = (j < counts[0, side]).astype(f32)
            for f in range(4):
                to = side * 4 * blocks + f * blocks + j
                face[to : to + 1, :] = bod[pl.ds(f * blocks + block, 1), :] * live
    center = [bod[(1 + k) * blocks : (2 + k) * blocks, :] - mid[k : k + 1, :] for k in range(3)]
    body_features(bod[0:blocks, :], center, blocks, feat, blhs, bfw, 0)
    pair_sums(0, count, at_q, at_s, None, None, None, blhs, bfw, aw, au)
    ax, ay, az = from_sums(x, y, z, aw, au)
    out[0:1, :] = ax
    out[1:2, :] = ay
    out[2:3, :] = az


def cell_kernel(first, count, at_q, at_s, shifted, mid, table, out, feat, lhs, fw, fu, aw, au):
    for g in range(count // SUBS):
        read = read_cells(table, first + g * SUBS, SUBS, mid)
        cell_features(read, SUBS, feat, lhs, fw, fu, g * SUBS * LANES)
    pair_sums(count * LANES, 0, at_q, at_s, lhs, fw, fu, None, None, aw, au)
    ax, ay, az = from_sums(shifted[0:1], shifted[1:2], shifted[2:3], aw, au)
    out[0:1, :] = ax
    out[1:2, :] = ay
    out[2:3, :] = az


def last_kernel(faces, parts, *refs):
    at_q, at_s, shifted, mid, table = refs[:5]
    sides = refs[5 : 5 + faces]
    sums = refs[5 + faces : 5 + faces + parts]
    out, feat, lhs, fw, fu, blhs, bfw, aw, au = refs[5 + faces + parts :]
    rows = table.shape[0] // 10
    for g in range(rows // SUBS):
        read = read_cells(table, g * SUBS, SUBS, mid)
        cell_features(read, SUBS, feat, lhs, fw, fu, g * SUBS * LANES)
    base = 0
    for side in sides:
        blocks = side.shape[0] // 4
        center = [side[(1 + k) * blocks : (2 + k) * blocks, :] - mid[k : k + 1, :] for k in range(3)]
        body_features(side[0:blocks, :], center, blocks, feat, blhs, bfw, base)
        base += blocks * LANES
    pair_sums(rows * LANES, base, at_q, at_s, lhs, fw, fu, blhs, bfw, aw, au)
    total = list(from_sums(shifted[0:1], shifted[1:2], shifted[2:3], aw, au))
    for part in sums:
        total = [t + part[k : k + 1, :] for k, t in enumerate(total)]
    for k in range(3):
        out[k : k + 1, :] = total[k]


def call(kernel, out_shape, args, scratch=(), in_specs=None, flops=0):
    specs = in_specs or [pl.BlockSpec(memory_space=pltpu.VMEM)] * len(args)
    many = isinstance(out_shape, (list, tuple))
    vmem = pl.BlockSpec(memory_space=pltpu.VMEM)
    return pl.pallas_call(
        kernel,
        out_shape=out_shape,
        in_specs=specs,
        out_specs=[vmem] * len(out_shape) if many else vmem,
        scratch_shapes=list(scratch),
        compiler_params=pltpu.CompilerParams(vmem_limit_bytes=32 * 2**20),
        cost_estimate=pl.CostEstimate(flops=flops, bytes_accessed=2**18, transcendentals=0),
    )(*args)


def shaped(*shape, dtype=f32):
    return jax.ShapeDtypeStruct(shape, dtype)


def sum_scratch(targets, cells, bodies):
    got = [pltpu.VMEM(((QROWS + SROWS + FROWS) * SUBS, LANES), f32)]
    if cells:
        got += [pltpu.VMEM((cells, LANES), bf16), pltpu.VMEM((16, cells), bf16), pltpu.VMEM((32, cells), bf16)]
    if bodies:
        got += [pltpu.VMEM((bodies, LANES), bf16), pltpu.VMEM((16, bodies), bf16)]
    return got + [pltpu.VMEM((16, targets), f32), pltpu.VMEM((32, targets), f32)]


def swapped(value, apart):
    mask = 2**apart
    return lax.ppermute(value, AXES, [(k, k ^ mask) for k in range(lax.axis_size(AXES))])


def shards(body_pos, body_mass, cell_mass, cell_center, cell_quad, cell_lists, slot_masks, face_lists, face_counts):
    bits = lax.axis_size(AXES).bit_length() - 1
    levels, slots = cell_lists.shape[1:]
    cells = cell_mass.shape[0]
    targets = body_mass.shape[0]
    blocks = targets // LANES
    rows = cells // LANES
    pick_rows = 10 * slots // LANES
    anywhere = pl.BlockSpec(memory_space=pl.ANY)
    vmem = pl.BlockSpec(memory_space=pltpu.VMEM)
    smem = pl.BlockSpec(memory_space=pltpu.SMEM)
    own, place, pick = call(
        open_kernel,
        [shaped(10 * rows, LANES), shaped(2 * levels * slots // LANES, LANES, dtype=jnp.int32), shaped(pick_rows, LANES)],
        [cell_mass.reshape(rows, LANES), cell_center, cell_quad, cell_lists[0], slot_masks[0]],
        [
            pltpu.VMEM((rows, LANES), f32),
            pltpu.VMEM(cell_center.shape, f32),
            pltpu.VMEM(cell_quad.shape, f32),
            pltpu.VMEM((levels, slots), jnp.int32),
            pltpu.VMEM((levels, slots), jnp.int32),
            pltpu.VMEM((rows * 16, LANES), f32),
            pltpu.SemaphoreType.DMA((5,)),
        ],
        [anywhere] * 5,
    )
    arrived = swapped(pick, bits - 1)
    at_q, at_s, shifted, mid, face, unused, near = call(
        start_kernel,
        [
            shaped(QROWS, targets, dtype=bf16),
            shaped(QROWS + SROWS, targets, dtype=bf16),
            shaped(SUBS, targets),
            shaped(SUBS, LANES),
            shaped(2 * 4 * blocks, LANES),
            shaped(4 * blocks, LANES),
            shaped(3, targets),
        ],
        [body_pos, body_mass.reshape(blocks, LANES), face_lists[0], face_counts],
        sum_scratch(targets, 0, targets),
        [vmem, vmem, smem, smem],
        flops=targets * targets * 20,
    )
    common = [at_q, at_s, shifted, mid]

    def cell_sums(table, first, count):
        kernel = functools.partial(cell_kernel, first, count)
        flops = targets * count * LANES * 50
        return call(kernel, shaped(3, targets), common + [table], sum_scratch(targets, count * LANES, 0), flops=flops)

    lower, upper = face[: 4 * blocks], face[4 * blocks :]
    count = lax.axis_size("gz")
    if count == 2:
        side = jnp.where(lax.axis_index("gz") == 0, upper, lower)
        sides = [lax.ppermute(side, "gz", [(0, 1), (1, 0)])]
    else:
        sides = [
            lax.ppermute(upper, "gz", [(k, k + 1) for k in range(count - 1)]),
            lax.ppermute(lower, "gz", [(k + 1, k) for k in range(count - 1)]),
        ]
    sums = [near]
    half = rows // 2
    sums.append(cell_sums(own, 0, half))
    sums.append(cell_sums(own, half, rows - half))
    tables = [own, arrived]
    for level in range(1, levels):
        pick = call(functools.partial(pick_kernel, level), shaped(pick_rows, LANES), [place] + tables)
        arrived = swapped(pick, bits - 1 - level)
        sums.append(cell_sums(tables[-1], 0, slots // LANES))
        tables.append(arrived)
    return call(
        functools.partial(last_kernel, len(sides), len(sums)),
        shaped(3, targets),
        common + [arrived] + sides + sums,
        sum_scratch(targets, slots, targets * len(sides)),
        flops=targets * slots * 50,
    )


def solution(mesh):
    in_specs = (
        P(None, AXES),
        P(AXES),
        P(AXES),
        P(None, AXES),
        P(None, AXES),
        P(AXES, None, None),
        P(AXES, None, None),
        P(AXES, None, None),
        P(AXES, None),
    )
    out_specs = P(None, AXES)
    return jax.shard_map(shards, mesh=mesh, in_specs=in_specs, out_specs=out_specs, check_vma=False)
```

```python
import functools
import math

import jax
import jax.numpy as jnp
from jax import lax
from jax.experimental import pallas as pl
from jax.experimental.pallas import tpu as pltpu
from jax.sharding import PartitionSpec as P

AXES = ("gx", "gy", "gz")
LANES = 128
SUBS = 8
NBLK = 4
SOFT = 0.01
QROWS = 64
SROWS = 32
FROWS = 48
UNIT = 256
A_PART = (0, 0, 1, 1, 0, 2)
B_PART = (0, 1, 0, 1, 2, 0)

f32 = jnp.float32
bf16 = jnp.bfloat16
dot = functools.partial(jnp.dot, preferred_element_type=f32)


def split3(value):
    one = value.astype(bf16).astype(f32)
    rest = value - one
    two = rest.astype(bf16).astype(f32)
    three = (rest - two).astype(bf16).astype(f32)
    return one, two, three


def halves(value):
    high = value.astype(bf16)
    return high, (value - high.astype(f32)).astype(bf16)


def paired(values, parts):
    pieces = [split3(v) for v in values]
    return [p[k] for k in parts for p in pieces]


def quad_rows(mass, center, quad):
    cx, cy, cz = center
    qxx, qyy, qzz, qxy, qxz, qyz = quad
    vx = qxx * cx + qxy * cy + qxz * cz
    vy = qxy * cx + qyy * cy + qyz * cz
    vz = qxz * cx + qyz * cy + qzz * cz
    h = 2.5 / jnp.maximum(mass, 1e-3)
    linear = [-2.0 * h * vx, -2.0 * h * vy, -2.0 * h * vz]
    square = [h * qxx, h * qyy, h * qzz, 2.0 * h * qxy, 2.0 * h * qxz, 2.0 * h * qyz]
    rows = list(split3(h * (cx * vx + cy * vy + cz * vz)))
    rows += paired(linear + square, B_PART)
    rows += [jnp.zeros_like(mass)] * (QROWS - len(rows))
    return rows, (vx, vy, vz)


def dist_rows(mass, center):
    cx, cy, cz = center
    rows = list(split3(cx * cx + cy * cy + cz * cz + SOFT))
    rows += paired([-2.0 * cx, -2.0 * cy, -2.0 * cz], B_PART)
    rows += [jnp.ones_like(mass)] * 3
    rows += [jnp.zeros_like(mass)] * (SROWS - len(rows))
    return rows


def mass_rows(mass, center):
    cx, cy, cz = center
    rows = paired([mass, mass * cx, mass * cy, mass * cz], (0, 1, 2))
    return rows + [jnp.zeros_like(mass)] * (16 - len(rows))


def moment_rows(quad, v):
    rows = paired(list(quad) + list(v), (0, 1, 2))
    return rows + [jnp.zeros_like(v[0])] * (32 - len(rows))


def target_rows(x, y, z):
    one = jnp.ones_like(x)
    zero = jnp.zeros_like(x)
    q = [one] * 3 + paired([x, y, z, x * x, y * y, z * z, x * y, x * z, y * z], A_PART)
    q += [zero] * (QROWS - len(q))
    s = [one] * 3 + paired([x, y, z], A_PART) + list(split3(x * x + y * y + z * z))
    s += [zero] * (SROWS - len(s))
    return q, s


def stage_rows(feat, rows, sub):
    for k, value in enumerate(rows):
        feat[k * sub : (k + 1) * sub, :] = value


def cell_features(read, sub, feat, lhs, fw, fu, base):
    mass, center, quad = read
    q, v = quad_rows(mass, center, quad)
    rows = q + dist_rows(mass, center) + mass_rows(mass, center) + moment_rows(quad, v)
    stage_rows(feat, rows, sub)
    wide = QROWS + SROWS
    for r in range(sub):
        at = slice(base + r * LANES, base + (r + 1) * LANES)
        left = feat[pl.ds(r, wide, stride=sub), :]
        lhs[at, 0:wide] = left.T.astype(bf16)
        right = feat[pl.ds(wide * sub + r, FROWS, stride=sub), :]
        fw[:, at] = right[0:16].astype(bf16)
        fu[:, at] = right[16:FROWS].astype(bf16)


def body_features(mass, center, sub, feat, lhs, fw, base):
    rows = dist_rows(mass, center) + mass_rows(mass, center)
    stage_rows(feat, rows, sub)
    for r in range(sub):
        at = slice(base + r * LANES, base + (r + 1) * LANES)
        left = feat[pl.ds(r, SROWS, stride=sub), :]
        lhs[at, 0:SROWS] = left.T.astype(bf16)
        right = feat[pl.ds(SROWS * sub + r, 16, stride=sub), :]
        fw[:, at] = right.astype(bf16)


def twice(left, high, low):
    return dot(jnp.concatenate([left, left], 1), jnp.concatenate([high, low], 0))


def pair_sums(cells, bodies, at_q, at_s, lhs, fw, fu, blhs, bfw, aw, au):
    targets = at_q.shape[1]
    wide = math.gcd(targets, UNIT)
    units = []
    for count, is_cell in ((cells, True), (bodies, False)):
        deep = math.gcd(count, UNIT) if count else 1
        for b in range(count // deep):
            for t in range(targets // wide):
                units.append((slice(b * deep, (b + 1) * deep), slice(t * wide, (t + 1) * wide), is_cell))
    aw[...] = jnp.zeros_like(aw)
    au[...] = jnp.zeros_like(au)

    def first(src, tgt, is_cell):
        if not is_cell:
            return dot(blhs[src, 0:SROWS], at_s[QROWS : QROWS + SROWS, tgt]), None
        s = dot(lhs[src, 0 : QROWS + SROWS], at_s[:, tgt])
        return s, dot(lhs[src, 0:QROWS], at_q[:, tgt])

    def second(src, tgt, is_cell, s, q):
        y = lax.rsqrt(s)
        y2 = y * y
        y3 = y * y2
        if not is_cell:
            aw[:, tgt] += twice(bfw[:, src], *halves(y3))
            return
        y5 = y3 * y2
        w = y3 + (q * y2) * y5
        aw[:, tgt] += twice(fw[:, src], *halves(w))
        au[:, tgt] += twice(fu[:, src], *halves(y5))

    ready = first(*units[0])
    for k, unit in enumerate(units):
        coming = first(*units[k + 1]) if k + 1 < len(units) else None
        second(*unit, *ready)
        ready = coming


def from_sums(x, y, z, aw, au):
    w = aw[0:4, :] + aw[4:8, :] + aw[8:12, :]
    u = au[0:9, :] + au[9:18, :] + au[18:27, :]

    def g(k):
        return u[k : k + 1, :]

    return (
        g(0) * x + g(3) * y + g(4) * z - g(6) - (w[0:1] * x - w[1:2]),
        g(3) * x + g(1) * y + g(5) * z - g(7) - (w[0:1] * y - w[2:3]),
        g(4) * x + g(5) * y + g(2) * z - g(8) - (w[0:1] * z - w[3:4]),
    )


def open_kernel(mass, center, quad, lists, masks, own, place, pick, vm, vc, vq, vl, vk, tab, sems):
    moves = [
        pltpu.make_async_copy(src, dst, sems.at[k])
        for k, (src, dst) in enumerate(((lists, vl), (masks, vk), (mass, vm), (center, vc), (quad, vq)))
    ]
    for move in moves:
        move.start()
    levels = lists.shape[0]
    moves[0].wait()
    moves[1].wait()
    slots = lists.shape[1] // LANES
    for level in range(levels):
        for r in range(slots):
            at = slice(r * LANES, (r + 1) * LANES)
            index = vl[level : level + 1, at]
            live = vk[level : level + 1, at]
            place[2 * level * slots + r : 2 * level * slots + r + 1, :] = jnp.where(live > 0, index >> 7, -1)
            place[(2 * level + 1) * slots + r : (2 * level + 1) * slots + r + 1, :] = index & (LANES - 1)
    moves[2].wait()
    moves[3].wait()
    moves[4].wait()
    rows = center.shape[1] // LANES
    for k in range(rows):
        at = slice(k * LANES, (k + 1) * LANES)
        tab[k * 16 : k * 16 + 1, :] = vm[k : k + 1, :]
        tab[k * 16 + 1 : k * 16 + 4, :] = vc[:, at]
        tab[k * 16 + 4 : k * 16 + 10, :] = vq[:, at]
    for f in range(10):
        own[f * rows : (f + 1) * rows, :] = tab[pl.ds(f, rows, stride=16), :]
    picked(0, [own], place, pick)


def picked(level, tables, place, pick):
    slots = SUBS
    row = place[2 * level * slots : (2 * level + 1) * slots, :]
    lane = place[(2 * level + 1) * slots : (2 * level + 2) * slots, :]
    out = [jnp.zeros((slots, LANES), f32)] * 10
    base = 0
    for table in tables:
        rows = table.shape[0] // 10
        for k in range(rows):
            hit = row == base + k
            for f in range(10):
                line = jnp.broadcast_to(table[f * rows + k : f * rows + k + 1, :], (slots, LANES))
                got = jnp.take_along_axis(line, lane, axis=1, mode="promise_in_bounds")
                out[f] = jnp.where(hit, got, out[f])
        base += rows
    for f in range(10):
        pick[f * slots : (f + 1) * slots, :] = out[f]


def pick_kernel(level, faces, *refs):
    place, *tables = refs[: len(refs) - 1 - faces]
    pick = refs[-1]
    for face in refs[len(refs) - 1 - faces : -1]:
        pick[pick.shape[0] - face.shape[0] :, :] = face[...]
    picked(level, tables, place, pick)


def read_cells(table, first, count, mid):
    rows = table.shape[0] // 10 // SUBS * SUBS

    def row(f):
        return table[f * rows + first : f * rows + first + count, :]

    center = [row(1 + k) - mid[k : k + 1, :] for k in range(3)]
    return row(0), center, [row(4 + k) for k in range(6)]


def start_kernel(one_side, pos, mass, lists, counts, at_q, at_s, shifted, mid, face, out, bod, feat, blhs, bfw, aw, au):
    count = pos.shape[1]
    blocks = count // LANES
    low = jnp.min(pos[...], axis=1, keepdims=True)
    high = jnp.max(pos[...], axis=1, keepdims=True)
    middle = jnp.broadcast_to(0.5 * (low + high), (3, LANES))
    mid[0:3, :] = middle
    moved = pos[...] - middle[:, 0:1]
    shifted[0:3, :] = moved
    x, y, z = moved[0:1], moved[1:2], moved[2:3]
    q, s = target_rows(x, y, z)
    at_q[...] = jnp.concatenate(q, axis=0).astype(bf16)
    at_s[...] = jnp.concatenate([jnp.zeros_like(x)] * QROWS + s, axis=0).astype(bf16)
    bod[0:blocks, :] = mass[...]
    for f in range(3):
        for k in range(blocks):
            at = slice(k * LANES, (k + 1) * LANES)
            bod[(f + 1) * blocks + k : (f + 1) * blocks + k + 1, :] = pos[f : f + 1, at]
    sides = [1 - lax.axis_index("gz")] if one_side else [0, 1]
    for k, side in enumerate(sides):
        for j in range(blocks):
            block = lists[side, j]
            live = (j < counts[0, side]).astype(f32)
            for f in range(4):
                to = k * 4 * blocks + f * blocks + j
                face[to : to + 1, :] = bod[pl.ds(f * blocks + block, 1), :] * live
    center = [bod[(1 + k) * blocks : (2 + k) * blocks, :] - mid[k : k + 1, :] for k in range(3)]
    body_features(bod[0:blocks, :], center, blocks, feat, blhs, bfw, 0)
    pair_sums(0, count, at_q, at_s, None, None, None, blhs, bfw, aw, au)
    ax, ay, az = from_sums(x, y, z, aw, au)
    out[0:1, :] = ax
    out[1:2, :] = ay
    out[2:3, :] = az


def cell_kernel(spans, at_q, at_s, shifted, mid, *refs):
    tables = refs[: len(spans)]
    out, feat, lhs, fw, fu, aw, au = refs[len(spans) :]
    base = 0
    for table, (first, count) in zip(tables, spans):
        for g in range(count // SUBS):
            read = read_cells(table, first + g * SUBS, SUBS, mid)
            cell_features(read, SUBS, feat, lhs, fw, fu, base)
            base += SUBS * LANES
    pair_sums(base, 0, at_q, at_s, lhs, fw, fu, None, None, aw, au)
    ax, ay, az = from_sums(shifted[0:1], shifted[1:2], shifted[2:3], aw, au)
    out[0:1, :] = ax
    out[1:2, :] = ay
    out[2:3, :] = az


def last_kernel(merged, faces, parts, *refs):
    at_q, at_s, shifted, mid, table = refs[:5]
    sides = list(refs[5 : 5 + faces])
    sums = refs[5 + faces : 5 + faces + parts]
    out, feat, lhs, fw, fu, blhs, bfw, aw, au = refs[5 + faces + parts :]
    if merged:
        sides.append(table.at[10 * SUBS :])
    read = read_cells(table, 0, SUBS, mid)
    cell_features(read, SUBS, feat, lhs, fw, fu, 0)
    base = 0
    for side in sides:
        blocks = side.shape[0] // 4
        center = [side[(1 + k) * blocks : (2 + k) * blocks, :] - mid[k : k + 1, :] for k in range(3)]
        body_features(side[0:blocks, :], center, blocks, feat, blhs, bfw, base)
        base += blocks * LANES
    pair_sums(SUBS * LANES, base, at_q, at_s, lhs, fw, fu, blhs, bfw, aw, au)
    total = list(from_sums(shifted[0:1], shifted[1:2], shifted[2:3], aw, au))
    for part in sums:
        total = [t + part[k : k + 1, :] for k, t in enumerate(total)]
    for k in range(3):
        out[k : k + 1, :] = total[k]


def call(kernel, out_shape, args, scratch=(), in_specs=None, flops=0):
    specs = in_specs or [pl.BlockSpec(memory_space=pltpu.VMEM)] * len(args)
    many = isinstance(out_shape, (list, tuple))
    vmem = pl.BlockSpec(memory_space=pltpu.VMEM)
    return pl.pallas_call(
        kernel,
        out_shape=out_shape,
        in_specs=specs,
        out_specs=[vmem] * len(out_shape) if many else vmem,
        scratch_shapes=list(scratch),
        compiler_params=pltpu.CompilerParams(vmem_limit_bytes=32 * 2**20),
        cost_estimate=pl.CostEstimate(flops=flops, bytes_accessed=2**18, transcendentals=0),
    )(*args)


def shaped(*shape, dtype=f32):
    return jax.ShapeDtypeStruct(shape, dtype)


def sum_scratch(targets, cells, bodies):
    got = [pltpu.VMEM(((QROWS + SROWS + FROWS) * SUBS, LANES), f32)]
    if cells:
        got += [pltpu.VMEM((cells, LANES), bf16), pltpu.VMEM((16, cells), bf16), pltpu.VMEM((32, cells), bf16)]
    if bodies:
        got += [pltpu.VMEM((bodies, LANES), bf16), pltpu.VMEM((16, bodies), bf16)]
    return got + [pltpu.VMEM((16, targets), f32), pltpu.VMEM((32, targets), f32)]


def swapped(value, apart):
    mask = 2**apart
    return lax.ppermute(value, AXES, [(k, k ^ mask) for k in range(lax.axis_size(AXES))])


def shards(body_pos, body_mass, cell_mass, cell_center, cell_quad, cell_lists, slot_masks, face_lists, face_counts):
    bits = lax.axis_size(AXES).bit_length() - 1
    levels, slots = cell_lists.shape[1:]
    cells = cell_mass.shape[0]
    targets = body_mass.shape[0]
    blocks = targets // LANES
    rows = cells // LANES
    pick_rows = 10 * slots // LANES
    anywhere = pl.BlockSpec(memory_space=pl.ANY)
    vmem = pl.BlockSpec(memory_space=pltpu.VMEM)
    smem = pl.BlockSpec(memory_space=pltpu.SMEM)
    own, place, pick = call(
        open_kernel,
        [shaped(10 * rows, LANES), shaped(2 * levels * slots // LANES, LANES, dtype=jnp.int32), shaped(pick_rows, LANES)],
        [cell_mass.reshape(rows, LANES), cell_center, cell_quad, cell_lists[0], slot_masks[0]],
        [
            pltpu.VMEM((rows, LANES), f32),
            pltpu.VMEM(cell_center.shape, f32),
            pltpu.VMEM(cell_quad.shape, f32),
            pltpu.VMEM((levels, slots), jnp.int32),
            pltpu.VMEM((levels, slots), jnp.int32),
            pltpu.VMEM((rows * 16, LANES), f32),
            pltpu.SemaphoreType.DMA((5,)),
        ],
        [anywhere] * 5,
    )
    arrived = swapped(pick, bits - 1)
    near_by = lax.axis_size("gz")
    merged = near_by == 2 and bits == levels
    at_q, at_s, shifted, mid, face, near = call(
        functools.partial(start_kernel, merged),
        [
            shaped(QROWS, targets, dtype=bf16),
            shaped(QROWS + SROWS, targets, dtype=bf16),
            shaped(SUBS, targets),
            shaped(SUBS, LANES),
            shaped((1 if merged else 2) * 4 * blocks, LANES),
            shaped(3, targets),
        ],
        [body_pos, body_mass.reshape(blocks, LANES), face_lists[0], face_counts],
        [pltpu.VMEM((4 * blocks, LANES), f32)] + sum_scratch(targets, 0, targets),
        [vmem, vmem, smem, smem],
        flops=targets * targets * 20,
    )
    common = [at_q, at_s, shifted, mid]

    def cell_sums(*spans):
        kernel = functools.partial(cell_kernel, [span[1:] for span in spans])
        count = sum(span[2] for span in spans) * LANES
        args = common + [span[0] for span in spans]
        return call(kernel, shaped(3, targets), args, sum_scratch(targets, count, 0), flops=targets * count * 50)

    sides = []
    if not merged:
        lower, upper = face[: 4 * blocks], face[4 * blocks :]
        sides = [
            lax.ppermute(upper, "gz", [(k, k + 1) for k in range(near_by - 1)]),
            lax.ppermute(lower, "gz", [(k + 1, k) for k in range(near_by - 1)]),
        ]
    half = rows // 2
    wide = slots // LANES
    sums = []
    tables = [own, arrived]
    window = [cell_sums((own, 0, half)), near]
    for level in range(1, levels):
        tied = lax.optimization_barrier((tables[-1], *window))
        tables[-1] = tied[0]
        sums += tied[1:]
        last = level == levels - 1
        extra = [face] if merged and last else []
        pick = call(
            functools.partial(pick_kernel, level, len(extra)),
            shaped(pick_rows + len(extra) * 4 * blocks, LANES),
            [place] + tables + extra,
        )
        arrived = swapped(pick, bits - 1 - level)
        if level == 1:
            window = [cell_sums((own, half, rows - half))]
        elif last:
            window = [cell_sums((tables[-2], 0, wide), (tables[-1], 0, wide))]
        else:
            window = [cell_sums((tables[level - 1], 0, wide))]
        tables.append(arrived)
    sums += window
    count = targets * (len(sides) + merged)
    return call(
        functools.partial(last_kernel, merged, len(sides), len(sums)),
        shaped(3, targets),
        common + [arrived] + sides + sums,
        sum_scratch(targets, slots, count),
        flops=targets * slots * 50,
    )


def solution(mesh):
    in_specs = (
        P(None, AXES),
        P(AXES),
        P(AXES),
        P(None, AXES),
        P(None, AXES),
        P(AXES, None, None),
        P(AXES, None, None),
        P(AXES, None, None),
        P(AXES, None),
    )
    out_specs = P(None, AXES)
    return jax.shard_map(shards, mesh=mesh, in_specs=in_specs, out_specs=out_specs, check_vma=False)
```

```python
import functools
import math

import jax
import jax.numpy as jnp
from jax import lax
from jax.experimental import pallas as pl
from jax.experimental.pallas import tpu as pltpu
from jax.sharding import PartitionSpec as P

AXES = ("gx", "gy", "gz")
LANES = 128
SUBS = 8
LIVE = 768
SOFT = 0.01
QROWS = 64
SROWS = 32
FROWS = 48
UNIT = 256
A_PART = (0, 0, 1, 1, 0, 2)
B_PART = (0, 1, 0, 1, 2, 0)

f32 = jnp.float32
bf16 = jnp.bfloat16
dot = functools.partial(jnp.dot, preferred_element_type=f32)


def split3(value):
    one = value.astype(bf16).astype(f32)
    rest = value - one
    two = rest.astype(bf16).astype(f32)
    three = (rest - two).astype(bf16).astype(f32)
    return one, two, three


def halves(value):
    high = value.astype(bf16)
    return high, (value - high.astype(f32)).astype(bf16)


def paired(values, parts):
    pieces = [split3(v) for v in values]
    return [p[k] for k in parts for p in pieces]


def quad_rows(mass, center, quad):
    cx, cy, cz = center
    qxx, qyy, qzz, qxy, qxz, qyz = quad
    vx = qxx * cx + qxy * cy + qxz * cz
    vy = qxy * cx + qyy * cy + qyz * cz
    vz = qxz * cx + qyz * cy + qzz * cz
    h = 2.5 / jnp.maximum(mass, 1e-3)
    linear = [-2.0 * h * vx, -2.0 * h * vy, -2.0 * h * vz]
    square = [h * qxx, h * qyy, h * qzz, 2.0 * h * qxy, 2.0 * h * qxz, 2.0 * h * qyz]
    rows = list(split3(h * (cx * vx + cy * vy + cz * vz)))
    rows += paired(linear + square, B_PART)
    rows += [jnp.zeros_like(mass)] * (QROWS - len(rows))
    return rows, (vx, vy, vz)


def dist_rows(mass, center):
    cx, cy, cz = center
    rows = list(split3(cx * cx + cy * cy + cz * cz + SOFT))
    rows += paired([-2.0 * cx, -2.0 * cy, -2.0 * cz], B_PART)
    rows += [jnp.ones_like(mass)] * 3
    rows += [jnp.zeros_like(mass)] * (SROWS - len(rows))
    return rows


def mass_rows(mass, center):
    cx, cy, cz = center
    rows = paired([mass, mass * cx, mass * cy, mass * cz], (0, 1, 2))
    return rows + [jnp.zeros_like(mass)] * (16 - len(rows))


def moment_rows(quad, v):
    rows = paired(list(quad) + list(v), (0, 1, 2))
    return rows + [jnp.zeros_like(v[0])] * (32 - len(rows))


def target_rows(x, y, z):
    one = jnp.ones_like(x)
    zero = jnp.zeros_like(x)
    q = [one] * 3 + paired([x, y, z, x * x, y * y, z * z, x * y, x * z, y * z], A_PART)
    q += [zero] * (QROWS - len(q))
    s = [one] * 3 + paired([x, y, z], A_PART) + list(split3(x * x + y * y + z * z))
    s += [zero] * (SROWS - len(s))
    return q, s


def stage_rows(feat, rows, sub):
    for k, value in enumerate(rows):
        feat[k * sub : (k + 1) * sub, :] = value


def cell_features(read, sub, feat, lhs, fw, fu, base):
    mass, center, quad = read
    q, v = quad_rows(mass, center, quad)
    rows = q + dist_rows(mass, center) + mass_rows(mass, center) + moment_rows(quad, v)
    stage_rows(feat, rows, sub)
    wide = QROWS + SROWS
    for r in range(sub):
        at = slice(base + r * LANES, base + (r + 1) * LANES)
        left = feat[pl.ds(r, wide, stride=sub), :]
        lhs[at, 0:wide] = left.T.astype(bf16)
        right = feat[pl.ds(wide * sub + r, FROWS, stride=sub), :]
        fw[:, at] = right[0:16].astype(bf16)
        fu[:, at] = right[16:FROWS].astype(bf16)


def body_features(mass, center, sub, feat, lhs, fw, base):
    rows = dist_rows(mass, center) + mass_rows(mass, center)
    stage_rows(feat, rows, sub)
    for r in range(sub):
        at = slice(base + r * LANES, base + (r + 1) * LANES)
        left = feat[pl.ds(r, SROWS, stride=sub), :]
        lhs[at, 0:SROWS] = left.T.astype(bf16)
        right = feat[pl.ds(SROWS * sub + r, 16, stride=sub), :]
        fw[:, at] = right.astype(bf16)


def twice(left, high, low):
    return dot(jnp.concatenate([left, left], 1), jnp.concatenate([high, low], 0))


def pair_sums(cells, bodies, at_q, at_s, lhs, fw, fu, blhs, bfw, aw, au):
    targets = at_q.shape[1]
    wide = math.gcd(targets, UNIT)
    units = []
    for count, is_cell in ((cells, True), (bodies, False)):
        deep = math.gcd(count, UNIT) if count else 1
        for b in range(count // deep):
            for t in range(targets // wide):
                units.append((slice(b * deep, (b + 1) * deep), slice(t * wide, (t + 1) * wide), is_cell))
    aw[...] = jnp.zeros_like(aw)
    au[...] = jnp.zeros_like(au)

    def first(src, tgt, is_cell):
        if not is_cell:
            return dot(blhs[src, 0:SROWS], at_s[QROWS : QROWS + SROWS, tgt]), None
        s = dot(lhs[src, 0 : QROWS + SROWS], at_s[:, tgt])
        return s, dot(lhs[src, 0:QROWS], at_q[:, tgt])

    def second(src, tgt, is_cell, s, q):
        y = lax.rsqrt(s)
        y2 = y * y
        y3 = y * y2
        if not is_cell:
            aw[:, tgt] += twice(bfw[:, src], *halves(y3))
            return
        y5 = y3 * y2
        w = y3 + (q * y2) * y5
        aw[:, tgt] += twice(fw[:, src], *halves(w))
        au[:, tgt] += twice(fu[:, src], *halves(y5))

    ready = first(*units[0])
    for k, unit in enumerate(units):
        coming = first(*units[k + 1]) if k + 1 < len(units) else None
        second(*unit, *ready)
        ready = coming


def from_sums(x, y, z, aw, au):
    w = aw[0:4, :] + aw[4:8, :] + aw[8:12, :]
    u = au[0:9, :] + au[9:18, :] + au[18:27, :]

    def g(k):
        return u[k : k + 1, :]

    return (
        g(0) * x + g(3) * y + g(4) * z - g(6) - (w[0:1] * x - w[1:2]),
        g(3) * x + g(1) * y + g(5) * z - g(7) - (w[0:1] * y - w[2:3]),
        g(4) * x + g(5) * y + g(2) * z - g(8) - (w[0:1] * z - w[3:4]),
    )


def slot_place(lists, masks, level):
    slots = lists.shape[2] // LANES
    rows, lanes = [], []
    for r in range(slots):
        at = slice(r * LANES, (r + 1) * LANES)
        index = lists[0, level : level + 1, at]
        rows.append(jnp.where(masks[0, level : level + 1, at] > 0, index >> 7, -1))
        lanes.append(index & (LANES - 1))
    return jnp.concatenate(rows, 0), jnp.concatenate(lanes, 0)


def picked(row, lane, lines, base, count, out):
    out = list(out)
    for k in range(count):
        hit = row == base + k
        for f in range(10):
            line = jnp.broadcast_to(lines(f, k), row.shape)
            got = jnp.take_along_axis(line, lane, axis=1, mode="promise_in_bounds")
            out[f] = jnp.where(hit, got, out[f])
    return out


def table_lines(table):
    rows = table.shape[0] // 10

    def line(f, k):
        return table[f * rows + k : f * rows + k + 1, :]

    return rows, line


def picked_tables(row, lane, tables):
    out = [jnp.zeros(row.shape, f32)] * 10
    base = 0
    for table in tables:
        rows, line = table_lines(table)
        out = picked(row, lane, line, base, rows, out)
        base += rows
    return out


def store_rows(to, values, count):
    for f, value in enumerate(values):
        to[f * count : (f + 1) * count, :] = value[0:count, :]


def open_kernel(mass, center, quad, lists, masks, pos, weight, faces, counts, pick):
    row, lane = slot_place(lists, masks, 0)

    def line(f, k):
        at = slice(k * LANES, (k + 1) * LANES)
        if f == 0:
            return mass[k : k + 1, :]
        return center[f - 1 : f, at] if f < 4 else quad[f - 4 : f - 3, at]

    zeros = [jnp.zeros(row.shape, f32)] * 10
    store_rows(pick, picked(row, lane, line, 0, mass.shape[0], zeros), row.shape[0])


def packed(row, lane):
    subs = row.shape[0]
    live = row >= 0
    at_row = lax.broadcasted_iota(jnp.int32, row.shape, 0)
    at_lane = lax.broadcasted_iota(jnp.int32, row.shape, 1)
    upper = lax.broadcasted_iota(jnp.int32, (LANES, LANES), 0) < lax.broadcasted_iota(jnp.int32, (LANES, LANES), 1)
    dead = jnp.where(live, 0.0, 1.0).astype(bf16)
    before = dot(dead, jnp.where(upper, 1.0, 0.0).astype(bf16))
    whole = dot(dead, jnp.ones((LANES, LANES), bf16))
    run = whole
    step = 1
    while step < subs:
        run = run + jnp.where(at_row >= step, pltpu.roll(run, step, axis=0), 0.0)
        step *= 2
    move = (before + run - whole).astype(jnp.int32)
    word = jnp.where(live, (((move + subs * LANES) << 6) + row << 7) + lane, 0)
    step = 1
    shift = 13
    while step < subs * LANES:
        if step < LANES:
            turned = pltpu.roll(word, LANES - step, axis=1)
            come = jnp.where(at_lane < LANES - step, turned, pltpu.roll(turned, subs - 1, axis=0))
        else:
            come = pltpu.roll(word, subs - step // LANES, axis=0)
        stay = jnp.where((word >> shift) & 1 == 0, word, 0)
        word = jnp.where((come >> shift) & 1 == 1, come, stay)
        step *= 2
        shift += 1
    return jnp.where(word > 0, (word >> 7) & 63, -1), word & (LANES - 1)


def read_cells(table, first, count, mid):
    rows, unused = table_lines(table)

    def row(f):
        return table[f * rows + first : f * rows + first + count, :]

    center = [row(1 + k) - mid[k : k + 1, :] for k in range(3)]
    return row(0), center, [row(4 + k) for k in range(6)]


def read_bodies(table, mid):
    blocks = table.shape[0] // 4
    center = [table[(1 + k) * blocks : (2 + k) * blocks, :] - mid[k : k + 1, :] for k in range(3)]
    return table[0:blocks, :], center, blocks


def span_features(spans, mid, feat, lhs, fw, fu):
    base = 0
    for table, first, count in spans:
        done = 0
        while done < count:
            sub = min(SUBS, count - done)
            cell_features(read_cells(table, first + done, sub, mid), sub, feat, lhs, fw, fu, base)
            base += sub * LANES
            done += sub
    return base


def store_sums(out, shifted, aw, au, parts=()):
    total = list(from_sums(shifted[0:1], shifted[1:2], shifted[2:3], aw, au))
    for part in parts:
        total = [t + part[k : k + 1, :] for k, t in enumerate(total)]
    for k in range(3):
        out[k : k + 1, :] = total[k]


def start_kernel(
    one_side, some, mass, center, quad, lists, masks, pos, weight, faces, counts,
    own, place, part, at_q, at_s, shifted, mid, face, out,
    tab, bod, feat, lhs, fw, fu, blhs, bfw, aw, au,
):
    levels = lists.shape[1]
    slots = lists.shape[2] // LANES
    for level in range(levels):
        row, lane = slot_place(lists, masks, level)
        if level == levels - 1:
            row, lane = packed(row, lane)
        place[2 * level * slots : (2 * level + 1) * slots, :] = row
        place[(2 * level + 1) * slots : (2 * level + 2) * slots, :] = lane
    rows = mass.shape[0]
    for k in range(rows):
        at = slice(k * LANES, (k + 1) * LANES)
        tab[k * 16 : k * 16 + 1, :] = mass[k : k + 1, :]
        tab[k * 16 + 1 : k * 16 + 4, :] = center[:, at]
        tab[k * 16 + 4 : k * 16 + 10, :] = quad[:, at]
    for f in range(10):
        own[f * rows : (f + 1) * rows, :] = tab[pl.ds(f, rows, stride=16), :]

    targets = pos.shape[1]
    blocks = targets // LANES
    low = jnp.min(pos[...], axis=1, keepdims=True)
    high = jnp.max(pos[...], axis=1, keepdims=True)
    middle = jnp.broadcast_to(0.5 * (low + high), (3, LANES))
    mid[0:3, :] = middle
    bod[0:blocks, :] = weight[...]
    for k in range(blocks):
        at = slice(k * LANES, (k + 1) * LANES)
        here = pos[:, at]
        bod[pl.ds(blocks + k, 3, stride=blocks), :] = here
        shifted[0:3, at] = here - middle
    own_mass, own_center, unused = read_bodies(bod, mid)
    q, s = target_rows(*own_center)
    stage_rows(feat, q + s, blocks)
    for k in range(blocks):
        at = slice(k * LANES, (k + 1) * LANES)
        rows_here = feat[pl.ds(k, QROWS + SROWS, stride=blocks), :]
        at_q[:, at] = rows_here[0:QROWS].astype(bf16)
        at_s[0:QROWS, at] = jnp.zeros((QROWS, LANES), bf16)
        at_s[QROWS : QROWS + SROWS, at] = rows_here[QROWS : QROWS + SROWS].astype(bf16)
    body_features(own_mass, own_center, blocks, feat, blhs, bfw, 0)
    span_features([(own, 0, some)], mid, feat, lhs, fw, fu)

    lower = lax.axis_index("gz") > 0
    for k in range(1 if one_side else 2):
        order = jnp.where(lower, faces[0:1, :], faces[1:2, :]) if one_side else faces[k : k + 1, :]
        many = jnp.where(lower, counts[:, 0:1], counts[:, 1:2]) if one_side else counts[:, k : k + 1]
        for j in range(blocks):
            take = jnp.where(j < many, order[:, j : j + 1], -1)
            got = jnp.zeros((4, LANES), f32)
            for b in range(blocks):
                got = jnp.where(take == b, bod[pl.ds(b, 4, stride=blocks), :], got)
            face[pl.ds(k * 4 * blocks + j, 4, stride=blocks), :] = got
    row, lane = place[2 * slots : 3 * slots, :], place[3 * slots : 4 * slots, :]
    store_rows(part, picked_tables(row, lane, [own]), slots)
    pair_sums(some * LANES, targets, at_q, at_s, lhs, fw, fu, blhs, bfw, aw, au)
    store_sums(out, shifted, aw, au)


def window_kernel(spans, ahead, count, at_q, at_s, shifted, mid, place, *refs):
    tables = refs[:count]
    if ahead:
        out, part, feat, lhs, fw, fu, aw, au = refs[count:]
        level, ids = ahead
        row = place[2 * level * SUBS : (2 * level + 1) * SUBS, :]
        lane = place[(2 * level + 1) * SUBS : (2 * level + 2) * SUBS, :]
        store_rows(part, picked_tables(row, lane, [tables[k] for k in ids]), SUBS)
    else:
        out, feat, lhs, fw, fu, aw, au = refs[count:]
    base = span_features([(tables[k], first, many) for k, first, many in spans], mid, feat, lhs, fw, fu)
    pair_sums(base, 0, at_q, at_s, lhs, fw, fu, None, None, aw, au)
    store_sums(out, shifted, aw, au)


def pick_kernel(level, base, live, faces, place, part, table, *refs):
    pick = refs[-1]
    row = place[2 * level * SUBS : (2 * level + 1) * SUBS, :]
    lane = place[(2 * level + 1) * SUBS : (2 * level + 2) * SUBS, :]
    rows, line = table_lines(table)
    out = [part[f * SUBS : (f + 1) * SUBS, :] for f in range(10)]
    store_rows(pick, picked(row, lane, line, base, rows, out), live)
    if faces:
        pick[10 * live :, :] = refs[0][...]


def last_kernel(merged, faces, parts, live, *refs):
    at_q, at_s, shifted, mid, table = refs[:5]
    sides = list(refs[5 : 5 + faces])
    sums = refs[5 + faces : 5 + faces + parts]
    out, feat, lhs, fw, fu, blhs, bfw, aw, au = refs[5 + faces + parts :]
    if merged:
        sides.append(table.at[10 * live :])
        table = table.at[: 10 * live]
    base = 0
    for side in sides:
        mass, center, blocks = read_bodies(side, mid)
        body_features(mass, center, blocks, feat, blhs, bfw, base)
        base += blocks * LANES
    count = span_features([(table, 0, live)], mid, feat, lhs, fw, fu)
    pair_sums(count, base, at_q, at_s, lhs, fw, fu, blhs, bfw, aw, au)
    store_sums(out, shifted, aw, au, sums)


def call(kernel, out_shape, args, scratch=(), in_specs=None, flops=0):
    specs = in_specs or [pl.BlockSpec(memory_space=pltpu.VMEM)] * len(args)
    many = isinstance(out_shape, (list, tuple))
    vmem = pl.BlockSpec(memory_space=pltpu.VMEM)
    return pl.pallas_call(
        kernel,
        out_shape=out_shape,
        in_specs=specs,
        out_specs=[vmem] * len(out_shape) if many else vmem,
        scratch_shapes=list(scratch),
        compiler_params=pltpu.CompilerParams(vmem_limit_bytes=32 * 2**20),
        cost_estimate=pl.CostEstimate(flops=flops, bytes_accessed=2**18, transcendentals=0),
    )(*args)


def shaped(*shape, dtype=f32):
    return jax.ShapeDtypeStruct(shape, dtype)


def sum_scratch(targets, cells, bodies):
    got = [pltpu.VMEM(((QROWS + SROWS + FROWS) * SUBS, LANES), f32)]
    if cells:
        got += [pltpu.VMEM((cells, LANES), bf16), pltpu.VMEM((16, cells), bf16), pltpu.VMEM((32, cells), bf16)]
    if bodies:
        got += [pltpu.VMEM((bodies, LANES), bf16), pltpu.VMEM((16, bodies), bf16)]
    return got + [pltpu.VMEM((16, targets), f32), pltpu.VMEM((32, targets), f32)]


def swapped(value, apart):
    mask = 2**apart
    return lax.ppermute(value, AXES, [(k, k ^ mask) for k in range(lax.axis_size(AXES))])


def shards(body_pos, body_mass, cell_mass, cell_center, cell_quad, cell_lists, slot_masks, face_lists, face_counts):
    bits = lax.axis_size(AXES).bit_length() - 1
    levels, slots = cell_lists.shape[1:]
    targets = body_mass.shape[0]
    blocks = targets // LANES
    rows = cell_mass.shape[0] // LANES
    wide = slots // LANES
    live = LIVE // LANES
    near_by = lax.axis_size("gz")
    merged = near_by == 2 and bits == levels
    given = [cell_mass.reshape(rows, LANES), cell_center, cell_quad, cell_lists, slot_masks]
    given += [body_pos, body_mass.reshape(blocks, LANES), face_lists[0], face_counts]
    pick = call(open_kernel, shaped(10 * wide, LANES), given)
    arrived = swapped(pick, bits - 1)

    some = rows // 4
    own, place, part, at_q, at_s, shifted, mid, face, near = call(
        functools.partial(start_kernel, merged, some),
        [
            shaped(10 * rows, LANES),
            shaped(2 * levels * wide, LANES, dtype=jnp.int32),
            shaped(10 * wide, LANES),
            shaped(QROWS, targets, dtype=bf16),
            shaped(QROWS + SROWS, targets, dtype=bf16),
            shaped(SUBS, targets),
            shaped(SUBS, LANES),
            shaped((1 if merged else 2) * 4 * blocks, LANES),
            shaped(3, targets),
        ],
        given,
        [pltpu.VMEM((16 * rows, LANES), f32), pltpu.VMEM((4 * blocks, LANES), f32)]
        + sum_scratch(targets, some * LANES, targets),
        flops=targets * (some * LANES * 50 + targets * 20),
    )
    common = [at_q, at_s, shifted, mid]

    def window(spans, ahead):
        tables = []
        for table, first, many in spans:
            if not any(table is known for known in tables):
                tables.append(table)
        if ahead:
            tables += [t for t in ahead[1] if not any(t is known for known in tables)]

        def place_of(table):
            return [table is known for known in tables].index(True)

        count = sum(many for table, first, many in spans) * LANES
        kernel = functools.partial(
            window_kernel,
            [(place_of(table), first, many) for table, first, many in spans],
            (ahead[0], [place_of(t) for t in ahead[1]]) if ahead else None,
            len(tables),
        )
        outs = [shaped(3, targets)] + ([shaped(10 * wide, LANES)] if ahead else [])
        scratch = sum_scratch(targets, count, 0)
        got = call(kernel, outs, common + [place] + tables, scratch, flops=targets * count * 50)
        return got

    sides = []
    if not merged:
        lower, upper = face[: 4 * blocks], face[4 * blocks :]
        sides = [
            lax.ppermute(upper, "gz", [(k, k + 1) for k in range(near_by - 1)]),
            lax.ppermute(lower, "gz", [(k + 1, k) for k in range(near_by - 1)]),
        ]
    tables = [own]
    sums = []
    tied = [near, part]
    for level in range(1, levels):
        arrived, total, part = lax.optimization_barrier((arrived, *tied))
        sums.append(total)
        last = level == levels - 1
        extra = [face] if merged and last else []
        many = live if last else wide
        base = rows + (level - 1) * wide
        pick = call(
            functools.partial(pick_kernel, level, base, many, len(extra)),
            shaped(10 * many + len(extra) * 4 * blocks, LANES),
            [place, part, arrived] + extra,
        )
        tables.append(arrived)
        arrived = swapped(pick, bits - 1 - level)
        if level == 1:
            spans = [(own, some, some)]
        elif level == 2:
            spans = [(own, 2 * some, rows - 2 * some)]
        elif level == 3:
            spans = [(tables[1], 0, wide), (tables[2], 0, wide)]
        else:
            spans = [(t, 0, wide) for t in tables[3:]]
        tied = window(spans, None if last else (level + 1, list(tables)))
    sums += tied
    return call(
        functools.partial(last_kernel, merged, len(sides), len(sums), live),
        shaped(3, targets),
        common + [arrived] + sides + sums,
        sum_scratch(targets, live * LANES, targets * (len(sides) + merged)),
        flops=targets * LIVE * 50,
    )


def solution(mesh):
    in_specs = (
        P(None, AXES),
        P(AXES),
        P(AXES),
        P(None, AXES),
        P(None, AXES),
        P(AXES, None, None),
        P(AXES, None, None),
        P(AXES, None, None),
        P(AXES, None),
    )
    out_specs = P(None, AXES)
    return jax.shard_map(shards, mesh=mesh, in_specs=in_specs, out_specs=out_specs, check_vma=False)
```

```python
import functools
import math

import jax
import jax.numpy as jnp
from jax import lax
from jax.experimental import pallas as pl
from jax.experimental.pallas import tpu as pltpu
from jax.sharding import PartitionSpec as P

AXES = ("gx", "gy", "gz")
LANES = 128
SUBS = 8
LIVE = 768
SOFT = 0.01
QROWS = 64
SROWS = 32
FROWS = 48
UNIT = 256
A_PART = (0, 0, 1, 1, 0, 2)
B_PART = (0, 1, 0, 1, 2, 0)

f32 = jnp.float32
bf16 = jnp.bfloat16
dot = functools.partial(jnp.dot, preferred_element_type=f32)


def split3(value):
    one = value.astype(bf16).astype(f32)
    rest = value - one
    two = rest.astype(bf16).astype(f32)
    three = (rest - two).astype(bf16).astype(f32)
    return one, two, three


def halves(value):
    high = value.astype(bf16)
    return high, (value - high.astype(f32)).astype(bf16)


def paired(values, parts):
    pieces = [split3(v) for v in values]
    return [p[k] for k in parts for p in pieces]


def quad_rows(mass, center, quad):
    cx, cy, cz = center
    qxx, qyy, qzz, qxy, qxz, qyz = quad
    vx = qxx * cx + qxy * cy + qxz * cz
    vy = qxy * cx + qyy * cy + qyz * cz
    vz = qxz * cx + qyz * cy + qzz * cz
    h = 2.5 / jnp.maximum(mass, 1e-3)
    linear = [-2.0 * h * vx, -2.0 * h * vy, -2.0 * h * vz]
    square = [h * qxx, h * qyy, h * qzz, 2.0 * h * qxy, 2.0 * h * qxz, 2.0 * h * qyz]
    rows = list(split3(h * (cx * vx + cy * vy + cz * vz)))
    rows += paired(linear + square, B_PART)
    rows += [jnp.zeros_like(mass)] * (QROWS - len(rows))
    return rows, (vx, vy, vz)


def dist_rows(mass, center):
    cx, cy, cz = center
    rows = list(split3(cx * cx + cy * cy + cz * cz + SOFT))
    rows += paired([-2.0 * cx, -2.0 * cy, -2.0 * cz], B_PART)
    rows += [jnp.ones_like(mass)] * 3
    rows += [jnp.zeros_like(mass)] * (SROWS - len(rows))
    return rows


def mass_rows(mass, center):
    cx, cy, cz = center
    rows = paired([mass, mass * cx, mass * cy, mass * cz], (0, 1, 2))
    return rows + [jnp.zeros_like(mass)] * (16 - len(rows))


def moment_rows(quad, v):
    rows = paired(list(quad) + list(v), (0, 1, 2))
    return rows + [jnp.zeros_like(v[0])] * (32 - len(rows))


def target_rows(x, y, z):
    one = jnp.ones_like(x)
    zero = jnp.zeros_like(x)
    q = [one] * 3 + paired([x, y, z, x * x, y * y, z * z, x * y, x * z, y * z], A_PART)
    q += [zero] * (QROWS - len(q))
    s = [one] * 3 + paired([x, y, z], A_PART) + list(split3(x * x + y * y + z * z))
    s += [zero] * (SROWS - len(s))
    return q, s


def stage_rows(feat, rows, sub):
    for k, value in enumerate(rows):
        feat[k * sub : (k + 1) * sub, :] = value


def cell_features(read, sub, feat, lhs, fw, fu, base):
    mass, center, quad = read
    q, v = quad_rows(mass, center, quad)
    rows = q + dist_rows(mass, center) + mass_rows(mass, center) + moment_rows(quad, v)
    stage_rows(feat, rows, sub)
    wide = QROWS + SROWS
    for r in range(sub):
        at = slice(base + r * LANES, base + (r + 1) * LANES)
        left = feat[pl.ds(r, wide, stride=sub), :]
        lhs[at, 0:wide] = left.T.astype(bf16)
        right = feat[pl.ds(wide * sub + r, FROWS, stride=sub), :]
        fw[:, at] = right[0:16].astype(bf16)
        fu[:, at] = right[16:FROWS].astype(bf16)


def body_features(mass, center, sub, feat, lhs, fw, base):
    rows = dist_rows(mass, center) + mass_rows(mass, center)
    stage_rows(feat, rows, sub)
    for r in range(sub):
        at = slice(base + r * LANES, base + (r + 1) * LANES)
        left = feat[pl.ds(r, SROWS, stride=sub), :]
        lhs[at, 0:SROWS] = left.T.astype(bf16)
        right = feat[pl.ds(SROWS * sub + r, 16, stride=sub), :]
        fw[:, at] = right.astype(bf16)


def twice(left, high, low):
    return dot(jnp.concatenate([left, left], 1), jnp.concatenate([high, low], 0))


def pair_sums(cells, bodies, at_q, at_s, lhs, fw, fu, blhs, bfw, aw, au):
    targets = at_q.shape[1]
    wide = math.gcd(targets, UNIT)
    units = []
    for count, is_cell in ((cells, True), (bodies, False)):
        deep = math.gcd(count, UNIT) if count else 1
        for b in range(count // deep):
            for t in range(targets // wide):
                units.append((slice(b * deep, (b + 1) * deep), slice(t * wide, (t + 1) * wide), is_cell))
    aw[...] = jnp.zeros_like(aw)
    au[...] = jnp.zeros_like(au)

    def first(src, tgt, is_cell):
        if not is_cell:
            return dot(blhs[src, 0:SROWS], at_s[QROWS : QROWS + SROWS, tgt]), None
        s = dot(lhs[src, 0 : QROWS + SROWS], at_s[:, tgt])
        return s, dot(lhs[src, 0:QROWS], at_q[:, tgt])

    def second(src, tgt, is_cell, s, q):
        y = lax.rsqrt(s)
        y2 = y * y
        y3 = y * y2
        if not is_cell:
            aw[:, tgt] += twice(bfw[:, src], *halves(y3))
            return
        y5 = y3 * y2
        w = y3 + (q * y2) * y5
        aw[:, tgt] += twice(fw[:, src], *halves(w))
        au[:, tgt] += twice(fu[:, src], *halves(y5))

    ready = first(*units[0])
    for k, unit in enumerate(units):
        coming = first(*units[k + 1]) if k + 1 < len(units) else None
        second(*unit, *ready)
        ready = coming


def from_sums(x, y, z, aw, au):
    w = aw[0:4, :] + aw[4:8, :] + aw[8:12, :]
    u = au[0:9, :] + au[9:18, :] + au[18:27, :]

    def g(k):
        return u[k : k + 1, :]

    return (
        g(0) * x + g(3) * y + g(4) * z - g(6) - (w[0:1] * x - w[1:2]),
        g(3) * x + g(1) * y + g(5) * z - g(7) - (w[0:1] * y - w[2:3]),
        g(4) * x + g(5) * y + g(2) * z - g(8) - (w[0:1] * z - w[3:4]),
    )


def slot_place(lists, masks, level):
    rows, lanes = [], []
    for r in range(lists.shape[1] // LANES):
        at = slice(r * LANES, (r + 1) * LANES)
        index = lists[level : level + 1, at]
        rows.append(jnp.where(masks[level : level + 1, at] > 0, index >> 7, -1))
        lanes.append(index & (LANES - 1))
    return jnp.concatenate(rows, 0), jnp.concatenate(lanes, 0)


def picked(row, lane, lines, base, count, out):
    out = list(out)
    for k in range(count):
        hit = row == base + k
        for f in range(10):
            line = jnp.broadcast_to(lines(f, k), row.shape)
            got = jnp.take_along_axis(line, lane, axis=1, mode="promise_in_bounds")
            out[f] = jnp.where(hit, got, out[f])
    return out


def table_lines(table):
    rows = table.shape[0] // 10

    def line(f, k):
        return table[f * rows + k : f * rows + k + 1, :]

    return rows, line


def picked_tables(row, lane, tables):
    out = [jnp.zeros(row.shape, f32)] * 10
    base = 0
    for table in tables:
        rows, line = table_lines(table)
        out = picked(row, lane, line, base, rows, out)
        base += rows
    return out


def store_rows(to, values, count):
    for f, value in enumerate(values):
        to[f * count : (f + 1) * count, :] = value[0:count, :]


def open_kernel(mass, center, quad, lists, masks, pick):
    row, lane = slot_place(lists, masks, 0)

    def line(f, k):
        at = slice(k * LANES, (k + 1) * LANES)
        if f == 0:
            return mass[k : k + 1, :]
        return center[f - 1 : f, at] if f < 4 else quad[f - 4 : f - 3, at]

    zeros = [jnp.zeros(row.shape, f32)] * 10
    store_rows(pick, picked(row, lane, line, 0, mass.shape[0], zeros), row.shape[0])


def packed(row, lane):
    subs = row.shape[0]
    live = row >= 0
    at_row = lax.broadcasted_iota(jnp.int32, row.shape, 0)
    at_lane = lax.broadcasted_iota(jnp.int32, row.shape, 1)
    upper = lax.broadcasted_iota(jnp.int32, (LANES, LANES), 0) < lax.broadcasted_iota(jnp.int32, (LANES, LANES), 1)
    dead = jnp.where(live, 0.0, 1.0).astype(bf16)
    before = dot(dead, jnp.where(upper, 1.0, 0.0).astype(bf16))
    whole = dot(dead, jnp.ones((LANES, LANES), bf16))
    run = whole
    step = 1
    while step < subs:
        run = run + jnp.where(at_row >= step, pltpu.roll(run, step, axis=0), 0.0)
        step *= 2
    move = (before + run - whole).astype(jnp.int32)
    word = jnp.where(live, (((move + subs * LANES) << 6) + row << 7) + lane, 0)
    step = 1
    shift = 13
    while step < subs * LANES:
        if step < LANES:
            turned = pltpu.roll(word, LANES - step, axis=1)
            come = jnp.where(at_lane < LANES - step, turned, pltpu.roll(turned, subs - 1, axis=0))
        else:
            come = pltpu.roll(word, subs - step // LANES, axis=0)
        stay = jnp.where((word >> shift) & 1 == 0, word, 0)
        word = jnp.where((come >> shift) & 1 == 1, come, stay)
        step *= 2
        shift += 1
    return jnp.where(word > 0, (word >> 7) & 63, -1), word & (LANES - 1)


def read_cells(table, first, count, mid):
    rows, unused = table_lines(table)

    def row(f):
        return table[f * rows + first : f * rows + first + count, :]

    center = [row(1 + k) - mid[k : k + 1, :] for k in range(3)]
    return row(0), center, [row(4 + k) for k in range(6)]


def read_bodies(table, mid):
    blocks = table.shape[0] // 4
    center = [table[(1 + k) * blocks : (2 + k) * blocks, :] - mid[k : k + 1, :] for k in range(3)]
    return table[0:blocks, :], center, blocks


def span_features(spans, mid, feat, lhs, fw, fu):
    base = 0
    for table, first, count in spans:
        done = 0
        while done < count:
            sub = min(SUBS, count - done)
            cell_features(read_cells(table, first + done, sub, mid), sub, feat, lhs, fw, fu, base)
            base += sub * LANES
            done += sub
    return base


def store_sums(out, shifted, aw, au, parts=()):
    total = list(from_sums(shifted[0:1], shifted[1:2], shifted[2:3], aw, au))
    for part in parts:
        total = [t + part[k : k + 1, :] for k, t in enumerate(total)]
    for k in range(3):
        out[k : k + 1, :] = total[k]


def start_kernel(
    one_side, some, mass, center, quad, lists, masks, pos, weight, faces, counts,
    own, place, part, at_q, at_s, shifted, mid, face, out,
    tab, bod, feat, lhs, fw, fu, blhs, bfw, aw, au,
):
    slots = SUBS
    levels = lists.shape[0]
    for level in range(levels):
        row, lane = slot_place(lists, masks, level)
        if level == levels - 1:
            row, lane = packed(row, lane)
        place[2 * level * slots : (2 * level + 1) * slots, :] = row
        place[(2 * level + 1) * slots : (2 * level + 2) * slots, :] = lane
    rows = mass.shape[0]
    for k in range(rows):
        at = slice(k * LANES, (k + 1) * LANES)
        tab[k * 16 : k * 16 + 1, :] = mass[k : k + 1, :]
        tab[k * 16 + 1 : k * 16 + 4, :] = center[:, at]
        tab[k * 16 + 4 : k * 16 + 10, :] = quad[:, at]
    for f in range(10):
        own[f * rows : (f + 1) * rows, :] = tab[pl.ds(f, rows, stride=16), :]

    targets = pos.shape[1]
    blocks = targets // LANES
    low = jnp.min(pos[...], axis=1, keepdims=True)
    high = jnp.max(pos[...], axis=1, keepdims=True)
    middle = jnp.broadcast_to(0.5 * (low + high), (3, LANES))
    mid[0:3, :] = middle
    bod[0:blocks, :] = weight[...]
    for k in range(blocks):
        at = slice(k * LANES, (k + 1) * LANES)
        here = pos[:, at]
        bod[pl.ds(blocks + k, 3, stride=blocks), :] = here
        shifted[0:3, at] = here - middle
    own_mass, own_center, unused = read_bodies(bod, mid)
    q, s = target_rows(*own_center)
    stage_rows(feat, q + s, blocks)
    for k in range(blocks):
        at = slice(k * LANES, (k + 1) * LANES)
        rows_here = feat[pl.ds(k, QROWS + SROWS, stride=blocks), :]
        at_q[:, at] = rows_here[0:QROWS].astype(bf16)
        at_s[0:QROWS, at] = jnp.zeros((QROWS, LANES), bf16)
        at_s[QROWS : QROWS + SROWS, at] = rows_here[QROWS : QROWS + SROWS].astype(bf16)
    body_features(own_mass, own_center, blocks, feat, blhs, bfw, 0)
    span_features([(own, 0, some)], mid, feat, lhs, fw, fu)

    lower = lax.axis_index("gz") > 0
    for k in range(1 if one_side else 2):
        order = jnp.where(lower, faces[0:1, :], faces[1:2, :]) if one_side else faces[k : k + 1, :]
        many = jnp.where(lower, counts[:, 0:1], counts[:, 1:2]) if one_side else counts[:, k : k + 1]
        for j in range(blocks):
            take = jnp.where(j < many, order[:, j : j + 1], -1)
            got = jnp.zeros((4, LANES), f32)
            for b in range(blocks):
                got = jnp.where(take == b, bod[pl.ds(b, 4, stride=blocks), :], got)
            face[pl.ds(k * 4 * blocks + j, 4, stride=blocks), :] = got
    row, lane = place[2 * slots : 3 * slots, :], place[3 * slots : 4 * slots, :]
    store_rows(part, picked_tables(row, lane, [own]), slots)
    pair_sums(some * LANES, targets, at_q, at_s, lhs, fw, fu, blhs, bfw, aw, au)
    store_sums(out, shifted, aw, au)


def window_kernel(spans, ahead, count, at_q, at_s, shifted, mid, place, *refs):
    tables = refs[:count]
    if ahead:
        out, part, feat, lhs, fw, fu, aw, au = refs[count:]
        level, ids = ahead
        row = place[2 * level * SUBS : (2 * level + 1) * SUBS, :]
        lane = place[(2 * level + 1) * SUBS : (2 * level + 2) * SUBS, :]
        store_rows(part, picked_tables(row, lane, [tables[k] for k in ids]), SUBS)
    else:
        out, feat, lhs, fw, fu, aw, au = refs[count:]
    base = span_features([(tables[k], first, many) for k, first, many in spans], mid, feat, lhs, fw, fu)
    pair_sums(base, 0, at_q, at_s, lhs, fw, fu, None, None, aw, au)
    store_sums(out, shifted, aw, au)


def pick_kernel(level, base, live, faces, place, part, table, *refs):
    pick = refs[-1]
    row = place[2 * level * SUBS : (2 * level + 1) * SUBS, :]
    lane = place[(2 * level + 1) * SUBS : (2 * level + 2) * SUBS, :]
    rows, line = table_lines(table)
    out = [part[f * SUBS : (f + 1) * SUBS, :] for f in range(10)]
    store_rows(pick, picked(row, lane, line, base, rows, out), live)
    if faces:
        pick[10 * live :, :] = refs[0][...]


def last_kernel(merged, faces, parts, live, *refs):
    at_q, at_s, shifted, mid, table = refs[:5]
    sides = list(refs[5 : 5 + faces])
    sums = refs[5 + faces : 5 + faces + parts]
    out, feat, lhs, fw, fu, blhs, bfw, aw, au = refs[5 + faces + parts :]
    if merged:
        sides.append(table.at[10 * live :])
        table = table.at[: 10 * live]
    base = 0
    for side in sides:
        mass, center, blocks = read_bodies(side, mid)
        body_features(mass, center, blocks, feat, blhs, bfw, base)
        base += blocks * LANES
    count = span_features([(table, 0, live)], mid, feat, lhs, fw, fu)
    pair_sums(count, base, at_q, at_s, lhs, fw, fu, blhs, bfw, aw, au)
    store_sums(out, shifted, aw, au, sums)


def call(kernel, out_shape, args, scratch=(), in_specs=None, flops=0):
    specs = in_specs or [pl.BlockSpec(memory_space=pltpu.VMEM)] * len(args)
    many = isinstance(out_shape, (list, tuple))
    vmem = pl.BlockSpec(memory_space=pltpu.VMEM)
    return pl.pallas_call(
        kernel,
        out_shape=out_shape,
        in_specs=specs,
        out_specs=[vmem] * len(out_shape) if many else vmem,
        scratch_shapes=list(scratch),
        compiler_params=pltpu.CompilerParams(vmem_limit_bytes=32 * 2**20),
        cost_estimate=pl.CostEstimate(flops=flops, bytes_accessed=2**18, transcendentals=0),
    )(*args)


def shaped(*shape, dtype=f32):
    return jax.ShapeDtypeStruct(shape, dtype)


def sum_scratch(targets, cells, bodies):
    got = [pltpu.VMEM(((QROWS + SROWS + FROWS) * SUBS, LANES), f32)]
    if cells:
        got += [pltpu.VMEM((cells, LANES), bf16), pltpu.VMEM((16, cells), bf16), pltpu.VMEM((32, cells), bf16)]
    if bodies:
        got += [pltpu.VMEM((bodies, LANES), bf16), pltpu.VMEM((16, bodies), bf16)]
    return got + [pltpu.VMEM((16, targets), f32), pltpu.VMEM((32, targets), f32)]


def swapped(value, apart):
    mask = 2**apart
    return lax.ppermute(value, AXES, [(k, k ^ mask) for k in range(lax.axis_size(AXES))])


def shards(body_pos, body_mass, cell_mass, cell_center, cell_quad, cell_lists, slot_masks, face_lists, face_counts):
    bits = lax.axis_size(AXES).bit_length() - 1
    levels, slots = cell_lists.shape[1:]
    targets = body_mass.shape[0]
    blocks = targets // LANES
    rows = cell_mass.shape[0] // LANES
    wide = slots // LANES
    live = LIVE // LANES
    near_by = lax.axis_size("gz")
    merged = near_by == 2 and bits == levels
    given = [cell_mass.reshape(rows, LANES), cell_center, cell_quad]
    given += [cell_lists[0], slot_masks[0]]
    given += [body_pos, body_mass.reshape(blocks, LANES), face_lists[0], face_counts]
    pick = call(open_kernel, shaped(10 * wide, LANES), given[:5])
    arrived = swapped(pick, bits - 1)

    some = rows // 4
    own, place, part, at_q, at_s, shifted, mid, face, near = call(
        functools.partial(start_kernel, merged, some),
        [
            shaped(10 * rows, LANES),
            shaped(2 * levels * wide, LANES, dtype=jnp.int32),
            shaped(10 * wide, LANES),
            shaped(QROWS, targets, dtype=bf16),
            shaped(QROWS + SROWS, targets, dtype=bf16),
            shaped(SUBS, targets),
            shaped(SUBS, LANES),
            shaped((1 if merged else 2) * 4 * blocks, LANES),
            shaped(3, targets),
        ],
        given,
        [pltpu.VMEM((16 * rows, LANES), f32), pltpu.VMEM((4 * blocks, LANES), f32)]
        + sum_scratch(targets, some * LANES, targets),
        flops=targets * (some * LANES * 50 + targets * 20),
    )
    common = [at_q, at_s, shifted, mid]

    def window(spans, ahead):
        tables = []
        for table, first, many in spans:
            if not any(table is known for known in tables):
                tables.append(table)
        if ahead:
            tables += [t for t in ahead[1] if not any(t is known for known in tables)]

        def place_of(table):
            return [table is known for known in tables].index(True)

        count = sum(many for table, first, many in spans) * LANES
        kernel = functools.partial(
            window_kernel,
            [(place_of(table), first, many) for table, first, many in spans],
            (ahead[0], [place_of(t) for t in ahead[1]]) if ahead else None,
            len(tables),
        )
        outs = [shaped(3, targets)] + ([shaped(10 * wide, LANES)] if ahead else [])
        scratch = sum_scratch(targets, count, 0)
        got = call(kernel, outs, common + [place] + tables, scratch, flops=targets * count * 50)
        return got

    sides = []
    if not merged:
        lower, upper = face[: 4 * blocks], face[4 * blocks :]
        sides = [
            lax.ppermute(upper, "gz", [(k, k + 1) for k in range(near_by - 1)]),
            lax.ppermute(lower, "gz", [(k + 1, k) for k in range(near_by - 1)]),
        ]
    tables = [own]
    sums = []
    tied = [near, part]
    for level in range(1, levels):
        arrived, total, part = lax.optimization_barrier((arrived, *tied))
        sums.append(total)
        last = level == levels - 1
        extra = [face] if merged and last else []
        many = live if last else wide
        base = rows + (level - 1) * wide
        pick = call(
            functools.partial(pick_kernel, level, base, many, len(extra)),
            shaped(10 * many + len(extra) * 4 * blocks, LANES),
            [place, part, arrived] + extra,
        )
        tables.append(arrived)
        arrived = swapped(pick, bits - 1 - level)
        if level == 1:
            spans = [(own, some, some)]
        elif level == 2:
            spans = [(own, 2 * some, rows - 2 * some)]
        elif level == 3:
            spans = [(tables[1], 0, wide), (tables[2], 0, wide)]
        else:
            spans = [(t, 0, wide) for t in tables[3:]]
        tied = window(spans, None if last else (level + 1, list(tables)))
    sums += tied
    return call(
        functools.partial(last_kernel, merged, len(sides), len(sums), live),
        shaped(3, targets),
        common + [arrived] + sides + sums,
        sum_scratch(targets, live * LANES, targets * (len(sides) + merged)),
        flops=targets * LIVE * 50,
    )


def solution(mesh):
    in_specs = (
        P(None, AXES),
        P(AXES),
        P(AXES),
        P(None, AXES),
        P(None, AXES),
        P(AXES, None, None),
        P(AXES, None, None),
        P(AXES, None, None),
        P(AXES, None),
    )
    out_specs = P(None, AXES)
    return jax.shard_map(shards, mesh=mesh, in_specs=in_specs, out_specs=out_specs, check_vma=False)
```

```python
import functools
import math

import jax
import jax.numpy as jnp
from jax import lax
from jax.experimental import pallas as pl
from jax.experimental.pallas import tpu as pltpu
from jax.sharding import PartitionSpec as P

AXES = ("gx", "gy", "gz")
LANES = 128
SUBS = 8
LIVE = 768
SOFT = 0.01
QROWS = 64
SROWS = 32
FROWS = 48
UNIT = 256
A_PART = (0, 0, 1, 1, 0, 2)
B_PART = (0, 1, 0, 1, 2, 0)

f32 = jnp.float32
bf16 = jnp.bfloat16
dot = functools.partial(jnp.dot, preferred_element_type=f32)


def split3(value):
    one = value.astype(bf16).astype(f32)
    rest = value - one
    two = rest.astype(bf16).astype(f32)
    three = (rest - two).astype(bf16).astype(f32)
    return one, two, three


def halves(value):
    high = value.astype(bf16)
    return high, (value - high.astype(f32)).astype(bf16)


def paired(values, parts):
    pieces = [split3(v) for v in values]
    return [p[k] for k in parts for p in pieces]


def quad_rows(mass, center, quad):
    cx, cy, cz = center
    qxx, qyy, qzz, qxy, qxz, qyz = quad
    vx = qxx * cx + qxy * cy + qxz * cz
    vy = qxy * cx + qyy * cy + qyz * cz
    vz = qxz * cx + qyz * cy + qzz * cz
    h = 2.5 / jnp.maximum(mass, 1e-3)
    linear = [-2.0 * h * vx, -2.0 * h * vy, -2.0 * h * vz]
    square = [h * qxx, h * qyy, h * qzz, 2.0 * h * qxy, 2.0 * h * qxz, 2.0 * h * qyz]
    rows = list(split3(h * (cx * vx + cy * vy + cz * vz)))
    rows += paired(linear + square, B_PART)
    rows += [jnp.zeros_like(mass)] * (QROWS - len(rows))
    return rows, (vx, vy, vz)


def dist_rows(mass, center):
    cx, cy, cz = center
    rows = list(split3(cx * cx + cy * cy + cz * cz + SOFT))
    rows += paired([-2.0 * cx, -2.0 * cy, -2.0 * cz], B_PART)
    rows += [jnp.ones_like(mass)] * 3
    rows += [jnp.zeros_like(mass)] * (SROWS - len(rows))
    return rows


def mass_rows(mass, center):
    cx, cy, cz = center
    rows = paired([mass, mass * cx, mass * cy, mass * cz], (0, 1, 2))
    return rows + [jnp.zeros_like(mass)] * (16 - len(rows))


def moment_rows(quad, v):
    rows = paired(list(quad) + list(v), (0, 1, 2))
    return rows + [jnp.zeros_like(v[0])] * (32 - len(rows))


def target_rows(x, y, z):
    one = jnp.ones_like(x)
    zero = jnp.zeros_like(x)
    q = [one] * 3 + paired([x, y, z, x * x, y * y, z * z, x * y, x * z, y * z], A_PART)
    q += [zero] * (QROWS - len(q))
    s = [one] * 3 + paired([x, y, z], A_PART) + list(split3(x * x + y * y + z * z))
    s += [zero] * (SROWS - len(s))
    return q, s


def stage_rows(feat, rows, sub):
    for k, value in enumerate(rows):
        feat[k * sub : (k + 1) * sub, :] = value


def cell_features(read, sub, feat, lhs, fw, fu, base):
    mass, center, quad = read
    q, v = quad_rows(mass, center, quad)
    rows = q + dist_rows(mass, center) + mass_rows(mass, center) + moment_rows(quad, v)
    stage_rows(feat, rows, sub)
    wide = QROWS + SROWS
    for r in range(sub):
        at = slice(base + r * LANES, base + (r + 1) * LANES)
        left = feat[pl.ds(r, wide, stride=sub), :]
        lhs[at, 0:wide] = left.T.astype(bf16)
        right = feat[pl.ds(wide * sub + r, FROWS, stride=sub), :]
        fw[:, at] = right[0:16].astype(bf16)
        fu[:, at] = right[16:FROWS].astype(bf16)


def body_features(mass, center, sub, feat, lhs, fw, base):
    rows = dist_rows(mass, center) + mass_rows(mass, center)
    stage_rows(feat, rows, sub)
    for r in range(sub):
        at = slice(base + r * LANES, base + (r + 1) * LANES)
        left = feat[pl.ds(r, SROWS, stride=sub), :]
        lhs[at, 0:SROWS] = left.T.astype(bf16)
        right = feat[pl.ds(SROWS * sub + r, 16, stride=sub), :]
        fw[:, at] = right.astype(bf16)


def twice(left, high, low):
    return dot(jnp.concatenate([left, left], 1), jnp.concatenate([high, low], 0))


def pair_sums(cells, bodies, at_q, at_s, lhs, fw, fu, blhs, bfw, aw, au):
    targets = at_q.shape[1]
    wide = math.gcd(targets, UNIT)
    units = []
    for count, is_cell in ((cells, True), (bodies, False)):
        deep = math.gcd(count, UNIT) if count else 1
        for b in range(count // deep):
            for t in range(targets // wide):
                units.append((slice(b * deep, (b + 1) * deep), slice(t * wide, (t + 1) * wide), is_cell))
    aw[...] = jnp.zeros_like(aw)
    au[...] = jnp.zeros_like(au)

    def first(src, tgt, is_cell):
        if not is_cell:
            return dot(blhs[src, 0:SROWS], at_s[QROWS : QROWS + SROWS, tgt]), None
        s = dot(lhs[src, 0 : QROWS + SROWS], at_s[:, tgt])
        return s, dot(lhs[src, 0:QROWS], at_q[:, tgt])

    def second(src, tgt, is_cell, s, q):
        y = lax.rsqrt(s)
        y2 = y * y
        y3 = y * y2
        if not is_cell:
            aw[:, tgt] += twice(bfw[:, src], *halves(y3))
            return
        y5 = y3 * y2
        w = y3 + (q * y2) * y5
        aw[:, tgt] += twice(fw[:, src], *halves(w))
        au[:, tgt] += twice(fu[:, src], *halves(y5))

    ready = first(*units[0])
    for k, unit in enumerate(units):
        coming = first(*units[k + 1]) if k + 1 < len(units) else None
        second(*unit, *ready)
        ready = coming


def from_sums(x, y, z, aw, au):
    w = aw[0:4, :] + aw[4:8, :] + aw[8:12, :]
    u = au[0:9, :] + au[9:18, :] + au[18:27, :]

    def g(k):
        return u[k : k + 1, :]

    return (
        g(0) * x + g(3) * y + g(4) * z - g(6) - (w[0:1] * x - w[1:2]),
        g(3) * x + g(1) * y + g(5) * z - g(7) - (w[0:1] * y - w[2:3]),
        g(4) * x + g(5) * y + g(2) * z - g(8) - (w[0:1] * z - w[3:4]),
    )


def slot_place(lists, masks, level):
    rows, lanes = [], []
    for r in range(lists.shape[1] // LANES):
        at = slice(r * LANES, (r + 1) * LANES)
        index = lists[level : level + 1, at]
        rows.append(jnp.where(masks[level : level + 1, at] > 0, index >> 7, -1))
        lanes.append(index & (LANES - 1))
    return jnp.concatenate(rows, 0), jnp.concatenate(lanes, 0)


def picked(row, lane, lines, base, count, out):
    out = list(out)
    for k in range(count):
        hit = row == base + k
        for f in range(10):
            line = jnp.broadcast_to(lines(f, k), row.shape)
            got = jnp.take_along_axis(line, lane, axis=1, mode="promise_in_bounds")
            out[f] = jnp.where(hit, got, out[f])
    return out


def table_lines(table):
    rows = table.shape[0] // 10

    def line(f, k):
        return table[f * rows + k : f * rows + k + 1, :]

    return rows, line


def picked_tables(row, lane, tables):
    out = [jnp.zeros(row.shape, f32)] * 10
    base = 0
    for table in tables:
        rows, line = table_lines(table)
        out = picked(row, lane, line, base, rows, out)
        base += rows
    return out


def store_rows(to, values, count):
    for f, value in enumerate(values):
        to[f * count : (f + 1) * count, :] = value[0:count, :]


def open_kernel(mass, center, quad, lists, masks, pick):
    row, lane = slot_place(lists, masks, 0)

    def line(f, k):
        at = slice(k * LANES, (k + 1) * LANES)
        if f == 0:
            return mass[k : k + 1, :]
        return center[f - 1 : f, at] if f < 4 else quad[f - 4 : f - 3, at]

    zeros = [jnp.zeros(row.shape, f32)] * 10
    store_rows(pick, picked(row, lane, line, 0, mass.shape[0], zeros), row.shape[0])


def packed(live, value, bits):
    subs = live.shape[0]
    at_row = lax.broadcasted_iota(jnp.int32, live.shape, 0)
    at_lane = lax.broadcasted_iota(jnp.int32, live.shape, 1)
    upper = lax.broadcasted_iota(jnp.int32, (LANES, LANES), 0) < lax.broadcasted_iota(jnp.int32, (LANES, LANES), 1)
    dead = jnp.where(live, 0.0, 1.0).astype(bf16)
    before = dot(dead, jnp.where(upper, 1.0, 0.0).astype(bf16))
    whole = dot(dead, jnp.ones((LANES, LANES), bf16))
    run = whole
    step = 1
    while step < subs:
        run = run + jnp.where(at_row >= step, pltpu.roll(run, step, axis=0), 0.0)
        step *= 2
    move = (before + run - whole).astype(jnp.int32)
    word = jnp.where(live, ((move + subs * LANES) << bits) + value, 0)
    step = 1
    shift = bits
    while step < subs * LANES:
        if step < LANES:
            turned = pltpu.roll(word, LANES - step, axis=1)
            come = jnp.where(at_lane < LANES - step, turned, pltpu.roll(turned, subs - 1, axis=0))
        else:
            come = pltpu.roll(word, subs - step // LANES, axis=0)
        stay = jnp.where((word >> shift) & 1 == 0, word, 0)
        word = jnp.where((come >> shift) & 1 == 1, come, stay)
        step *= 2
        shift += 1
    return word > 0, word & ((1 << bits) - 1)


def packed_place(row, lane, live):
    found, value = packed(live, row * LANES + lane, 13)
    return jnp.where(found, value >> 7, -1), value & (LANES - 1)


def packed_table(table, to, count):
    shape = (SUBS, LANES)
    index = lax.broadcasted_iota(jnp.int32, shape, 0) * LANES + lax.broadcasted_iota(jnp.int32, shape, 1)
    found, value = packed(table[0:SUBS, :] > 0.0, index, 10)
    row = jnp.where(found, value >> 7, -1)
    store_rows(to, picked_tables(row, value & (LANES - 1), [table]), count)


def read_cells(table, first, count, mid):
    rows, unused = table_lines(table)

    def row(f):
        return table[f * rows + first : f * rows + first + count, :]

    center = [row(1 + k) - mid[k : k + 1, :] for k in range(3)]
    return row(0), center, [row(4 + k) for k in range(6)]


def read_bodies(table, mid):
    blocks = table.shape[0] // 4
    center = [table[(1 + k) * blocks : (2 + k) * blocks, :] - mid[k : k + 1, :] for k in range(3)]
    return table[0:blocks, :], center, blocks


def span_features(spans, mid, feat, lhs, fw, fu):
    base = 0
    for table, first, count in spans:
        done = 0
        while done < count:
            sub = min(SUBS, count - done)
            cell_features(read_cells(table, first + done, sub, mid), sub, feat, lhs, fw, fu, base)
            base += sub * LANES
            done += sub
    return base


def store_sums(out, shifted, aw, au, parts=()):
    total = list(from_sums(shifted[0:1], shifted[1:2], shifted[2:3], aw, au))
    for part in parts:
        total = [t + part[k : k + 1, :] for k, t in enumerate(total)]
    for k in range(3):
        out[k : k + 1, :] = total[k]


def start_kernel(
    one_side, some, mass, center, quad, lists, masks, pos, weight, faces, counts,
    own, place, part, at_q, at_s, shifted, mid, face, out,
    tab, bod, feat, lhs, fw, fu, blhs, bfw, aw, au,
):
    slots = SUBS
    levels = lists.shape[0]
    for level in range(levels):
        row, lane = slot_place(lists, masks, level)
        if level == levels - 1:
            row, lane = packed_place(row, lane, row >= 0)
        place[2 * level * slots : (2 * level + 1) * slots, :] = row
        place[(2 * level + 1) * slots : (2 * level + 2) * slots, :] = lane
    rows = mass.shape[0]
    for k in range(rows):
        at = slice(k * LANES, (k + 1) * LANES)
        tab[k * 16 : k * 16 + 1, :] = mass[k : k + 1, :]
        tab[k * 16 + 1 : k * 16 + 4, :] = center[:, at]
        tab[k * 16 + 4 : k * 16 + 10, :] = quad[:, at]
    for f in range(10):
        own[f * rows : (f + 1) * rows, :] = tab[pl.ds(f, rows, stride=16), :]

    targets = pos.shape[1]
    blocks = targets // LANES
    low = jnp.min(pos[...], axis=1, keepdims=True)
    high = jnp.max(pos[...], axis=1, keepdims=True)
    middle = jnp.broadcast_to(0.5 * (low + high), (3, LANES))
    mid[0:3, :] = middle
    bod[0:blocks, :] = weight[...]
    for k in range(blocks):
        at = slice(k * LANES, (k + 1) * LANES)
        here = pos[:, at]
        bod[pl.ds(blocks + k, 3, stride=blocks), :] = here
        shifted[0:3, at] = here - middle
    own_mass, own_center, unused = read_bodies(bod, mid)
    q, s = target_rows(*own_center)
    stage_rows(feat, q + s, blocks)
    for k in range(blocks):
        at = slice(k * LANES, (k + 1) * LANES)
        rows_here = feat[pl.ds(k, QROWS + SROWS, stride=blocks), :]
        at_q[:, at] = rows_here[0:QROWS].astype(bf16)
        at_s[0:QROWS, at] = jnp.zeros((QROWS, LANES), bf16)
        at_s[QROWS : QROWS + SROWS, at] = rows_here[QROWS : QROWS + SROWS].astype(bf16)
    body_features(own_mass, own_center, blocks, feat, blhs, bfw, 0)
    span_features([(own, 0, some)], mid, feat, lhs, fw, fu)

    lower = lax.axis_index("gz") > 0
    for k in range(1 if one_side else 2):
        order = jnp.where(lower, faces[0:1, :], faces[1:2, :]) if one_side else faces[k : k + 1, :]
        many = jnp.where(lower, counts[:, 0:1], counts[:, 1:2]) if one_side else counts[:, k : k + 1]
        for j in range(blocks):
            take = jnp.where(j < many, order[:, j : j + 1], -1)
            got = jnp.zeros((4, LANES), f32)
            for b in range(blocks):
                got = jnp.where(take == b, bod[pl.ds(b, 4, stride=blocks), :], got)
            face[pl.ds(k * 4 * blocks + j, 4, stride=blocks), :] = got
    row, lane = place[2 * slots : 3 * slots, :], place[3 * slots : 4 * slots, :]
    store_rows(part, picked_tables(row, lane, [own]), slots)
    pair_sums(some * LANES, targets, at_q, at_s, lhs, fw, fu, blhs, bfw, aw, au)
    store_sums(out, shifted, aw, au)


def placed(place, level):
    row = place[2 * level * SUBS : (2 * level + 1) * SUBS, :]
    return row, place[(2 * level + 1) * SUBS : (2 * level + 2) * SUBS, :]


def window_kernel(spans, ahead, dense, inside, count, bodies, at_q, at_s, shifted, mid, place, *refs):
    tables, sides = list(refs[:count]), refs[count : count + bodies]
    refs = list(refs[count + bodies :])
    out = refs.pop(0)
    for level, ids in ahead:
        row, lane = placed(place, level)
        store_rows(refs.pop(0), picked_tables(row, lane, [tables[k] for k in ids]), SUBS)
    if dense is not None:
        to = refs.pop(0)
        packed_table(tables[dense], to, to.shape[0] // 10)
    au, aw = refs.pop(), refs.pop()
    room = refs.pop() if inside is not None else None
    feat, lhs, fw, fu = refs[:4]
    blhs, bfw = refs[4:6] if bodies else (None, None)
    near = 0
    for side in sides:
        mass, center, blocks = read_bodies(side, mid)
        body_features(mass, center, blocks, feat, blhs, bfw, near)
        near += blocks * LANES
    if inside is not None:
        packed_table(tables[inside], room, room.shape[0] // 10)
        tables[inside] = room
    base = span_features([(tables[k], first, many) for k, first, many in spans], mid, feat, lhs, fw, fu)
    pair_sums(base, near, at_q, at_s, lhs, fw, fu, blhs, bfw, aw, au)
    store_sums(out, shifted, aw, au)


def pick_kernel(level, base, live, faces, place, part, table, *refs):
    row, lane = placed(place, level)
    rows, line = table_lines(table)
    out = [part[f * SUBS : (f + 1) * SUBS, :] for f in range(10)]
    store_rows(refs[-1], picked(row, lane, line, base, rows, out), live)
    if faces:
        refs[-1][10 * live :, :] = refs[0][...]


def last_kernel(merged, faces, parts, live, *refs):
    at_q, at_s, shifted, mid, table = refs[:5]
    sides = list(refs[5 : 5 + faces])
    sums = refs[5 + faces : 5 + faces + parts]
    out, feat, lhs, fw, fu, blhs, bfw, aw, au = refs[5 + faces + parts :]
    if merged:
        sides.append(table.at[10 * live :])
        table = table.at[: 10 * live]
    base = 0
    for side in sides:
        mass, center, blocks = read_bodies(side, mid)
        body_features(mass, center, blocks, feat, blhs, bfw, base)
        base += blocks * LANES
    count = span_features([(table, 0, live)], mid, feat, lhs, fw, fu)
    pair_sums(count, base, at_q, at_s, lhs, fw, fu, blhs, bfw, aw, au)
    store_sums(out, shifted, aw, au, sums)


def call(kernel, out_shape, args, scratch=(), in_specs=None, flops=0):
    specs = in_specs or [pl.BlockSpec(memory_space=pltpu.VMEM)] * len(args)
    many = isinstance(out_shape, (list, tuple))
    vmem = pl.BlockSpec(memory_space=pltpu.VMEM)
    return pl.pallas_call(
        kernel,
        out_shape=out_shape,
        in_specs=specs,
        out_specs=[vmem] * len(out_shape) if many else vmem,
        scratch_shapes=list(scratch),
        compiler_params=pltpu.CompilerParams(vmem_limit_bytes=32 * 2**20),
        cost_estimate=pl.CostEstimate(flops=flops * 64, bytes_accessed=2**18, transcendentals=0),
    )(*args)


def shaped(*shape, dtype=f32):
    return jax.ShapeDtypeStruct(shape, dtype)


def sum_scratch(targets, cells, bodies):
    got = [pltpu.VMEM(((QROWS + SROWS + FROWS) * SUBS, LANES), f32)]
    if cells:
        got += [pltpu.VMEM((cells, LANES), bf16), pltpu.VMEM((16, cells), bf16), pltpu.VMEM((32, cells), bf16)]
    if bodies:
        got += [pltpu.VMEM((bodies, LANES), bf16), pltpu.VMEM((16, bodies), bf16)]
    return got + [pltpu.VMEM((16, targets), f32), pltpu.VMEM((32, targets), f32)]


def swapped(value, apart):
    mask = 2**apart
    return lax.ppermute(value, AXES, [(k, k ^ mask) for k in range(lax.axis_size(AXES))])


def shards(body_pos, body_mass, cell_mass, cell_center, cell_quad, cell_lists, slot_masks, face_lists, face_counts):
    bits = lax.axis_size(AXES).bit_length() - 1
    levels, slots = cell_lists.shape[1:]
    targets = body_mass.shape[0]
    blocks = targets // LANES
    rows = cell_mass.shape[0] // LANES
    wide = slots // LANES
    live = LIVE // LANES
    near_by = lax.axis_size("gz")
    merged = near_by == 2 and bits == levels
    given = [cell_mass.reshape(rows, LANES), cell_center, cell_quad]
    given += [cell_lists[0], slot_masks[0]]
    given += [body_pos, body_mass.reshape(blocks, LANES), face_lists[0], face_counts]
    pick = call(open_kernel, shaped(10 * wide, LANES), given[:5])
    arrived = swapped(pick, bits - 1)

    some = rows // 8
    own, place, part, at_q, at_s, shifted, mid, face, near = call(
        functools.partial(start_kernel, merged, some),
        [
            shaped(10 * rows, LANES),
            shaped(2 * levels * wide, LANES, dtype=jnp.int32),
            shaped(10 * wide, LANES),
            shaped(QROWS, targets, dtype=bf16),
            shaped(QROWS + SROWS, targets, dtype=bf16),
            shaped(SUBS, targets),
            shaped(SUBS, LANES),
            shaped((1 if merged else 2) * 4 * blocks, LANES),
            shaped(3, targets),
        ],
        given,
        [pltpu.VMEM((16 * rows, LANES), f32), pltpu.VMEM((4 * blocks, LANES), f32)]
        + sum_scratch(targets, some * LANES, targets),
        flops=targets * (some * LANES * 50 + targets * 20),
    )
    common = [at_q, at_s, shifted, mid]

    def window(spans, ahead=(), dense=None, inside=None, bodies=(), cost=1):
        tables = []
        for table in [span[0] for span in spans] + [t for item in ahead for t in item[1]] + [dense]:
            if table is not None and not any(table is known for known in tables):
                tables.append(table)

        def at(table):
            return None if table is None else [table is known for known in tables].index(True)

        count = sum(many for table, first, many in spans) * LANES
        kernel = functools.partial(
            window_kernel,
            [(at(table), first, many) for table, first, many in spans],
            [(level, [at(t) for t in some_tables]) for level, some_tables in ahead],
            at(dense),
            at(inside),
            len(tables),
            len(bodies),
        )
        outs = [shaped(3, targets)] + [shaped(10 * wide, LANES)] * len(ahead)
        outs += [shaped(10 * live, LANES)] if dense is not None else []
        scratch = sum_scratch(targets, count, targets * len(bodies))
        if inside is not None:
            scratch.insert(-2, pltpu.VMEM((10 * live, LANES), f32))
        flops = int(cost * targets * (count * 50 + len(bodies) * targets * 20))
        return call(kernel, outs, common + [place] + tables + list(bodies), scratch, flops=flops)

    sides = []
    if not merged:
        lower, upper = face[: 4 * blocks], face[4 * blocks :]
        sides = [
            lax.ppermute(upper, "gz", [(k, k + 1) for k in range(near_by - 1)]),
            lax.ppermute(lower, "gz", [(k + 1, k) for k in range(near_by - 1)]),
        ]

    def cut(start, stop):
        return (own, start * rows // 8, (stop - start) * rows // 8)

    tables = [own]
    dense = []
    sums = []
    tied = [near, part]
    for level in range(1, levels):
        tied = list(lax.optimization_barrier((arrived, *tied)))
        arrived = tied.pop(0)
        sums.append(tied.pop(0))
        part = tied.pop(0)
        dense += tied
        last = level == levels - 1
        extra = [face] if merged and last else []
        many = live if last else wide
        pick = call(
            functools.partial(pick_kernel, level, rows + (level - 1) * wide, many, len(extra)),
            shaped(10 * many + len(extra) * 4 * blocks, LANES),
            [place, part, arrived] + extra,
        )
        tables.append(arrived)
        newest = arrived
        arrived = swapped(pick, bits - 1 - level)
        if level == 1:
            spans = [cut(1, 3)]
        elif level == 2:
            spans = [cut(3, 8)]
        elif level == 3:
            spans = [(dense[0], 0, live), (dense[1], 0, live)]
        else:
            spans = [(dense[2], 0, live), (newest, 0, wide)]
        ahead = [] if last else [(level + 1, list(tables))]
        tied = window(spans, ahead, None if last else newest)
    sums += tied
    return call(
        functools.partial(last_kernel, merged, len(sides), len(sums), live),
        shaped(3, targets),
        common + [arrived] + sides + sums,
        sum_scratch(targets, live * LANES, targets * (len(sides) + merged)),
        flops=targets * LIVE * 50,
    )


def solution(mesh):
    in_specs = (
        P(None, AXES),
        P(AXES),
        P(AXES),
        P(None, AXES),
        P(None, AXES),
        P(AXES, None, None),
        P(AXES, None, None),
        P(AXES, None, None),
        P(AXES, None),
    )
    out_specs = P(None, AXES)
    return jax.shard_map(shards, mesh=mesh, in_specs=in_specs, out_specs=out_specs, check_vma=False)
```

```python
import functools
import math

import jax
import jax.numpy as jnp
from jax import lax
from jax.experimental import pallas as pl
from jax.experimental.pallas import tpu as pltpu
from jax.sharding import PartitionSpec as P

AXES = ("gx", "gy", "gz")
LANES = 128
SUBS = 8
LIVE = 768
SOFT = 0.01
QROWS = 64
SROWS = 32
FROWS = 48
UNIT = 256
A_PART = (0, 0, 1, 1, 0, 2)
B_PART = (0, 1, 0, 1, 2, 0)

f32 = jnp.float32
bf16 = jnp.bfloat16
dot = functools.partial(jnp.dot, preferred_element_type=f32)


def split3(value):
    one = value.astype(bf16).astype(f32)
    rest = value - one
    two = rest.astype(bf16).astype(f32)
    three = (rest - two).astype(bf16).astype(f32)
    return one, two, three


def halves(value):
    high = value.astype(bf16)
    return high, (value - high.astype(f32)).astype(bf16)


def paired(values, parts):
    pieces = [split3(v) for v in values]
    return [p[k] for k in parts for p in pieces]


def quad_rows(mass, center, quad):
    cx, cy, cz = center
    qxx, qyy, qzz, qxy, qxz, qyz = quad
    vx = qxx * cx + qxy * cy + qxz * cz
    vy = qxy * cx + qyy * cy + qyz * cz
    vz = qxz * cx + qyz * cy + qzz * cz
    h = 2.5 / jnp.maximum(mass, 1e-3)
    linear = [-2.0 * h * vx, -2.0 * h * vy, -2.0 * h * vz]
    square = [h * qxx, h * qyy, h * qzz, 2.0 * h * qxy, 2.0 * h * qxz, 2.0 * h * qyz]
    rows = list(split3(h * (cx * vx + cy * vy + cz * vz)))
    rows += paired(linear + square, B_PART)
    rows += [jnp.zeros_like(mass)] * (QROWS - len(rows))
    return rows, (vx, vy, vz)


def dist_rows(mass, center):
    cx, cy, cz = center
    rows = list(split3(cx * cx + cy * cy + cz * cz + SOFT))
    rows += paired([-2.0 * cx, -2.0 * cy, -2.0 * cz], B_PART)
    rows += [jnp.ones_like(mass)] * 3
    rows += [jnp.zeros_like(mass)] * (SROWS - len(rows))
    return rows


def mass_rows(mass, center):
    cx, cy, cz = center
    rows = paired([mass, mass * cx, mass * cy, mass * cz], (0, 1, 2))
    return rows + [jnp.zeros_like(mass)] * (16 - len(rows))


def moment_rows(quad, v):
    rows = paired(list(quad) + list(v), (0, 1, 2))
    return rows + [jnp.zeros_like(v[0])] * (32 - len(rows))


def target_rows(x, y, z):
    one = jnp.ones_like(x)
    zero = jnp.zeros_like(x)
    q = [one] * 3 + paired([x, y, z, x * x, y * y, z * z, x * y, x * z, y * z], A_PART)
    q += [zero] * (QROWS - len(q))
    s = [one] * 3 + paired([x, y, z], A_PART) + list(split3(x * x + y * y + z * z))
    s += [zero] * (SROWS - len(s))
    return q, s


def stage_rows(feat, rows, sub):
    for k, value in enumerate(rows):
        feat[k * sub : (k + 1) * sub, :] = value


def cell_features(read, sub, feat, lhs, fw, fu, base):
    mass, center, quad = read
    q, v = quad_rows(mass, center, quad)
    rows = q + dist_rows(mass, center) + mass_rows(mass, center) + moment_rows(quad, v)
    stage_rows(feat, rows, sub)
    wide = QROWS + SROWS
    for r in range(sub):
        at = slice(base + r * LANES, base + (r + 1) * LANES)
        left = feat[pl.ds(r, wide, stride=sub), :]
        lhs[at, 0:wide] = left.T.astype(bf16)
        right = feat[pl.ds(wide * sub + r, FROWS, stride=sub), :]
        fw[:, at] = right[0:16].astype(bf16)
        fu[:, at] = right[16:FROWS].astype(bf16)


def body_features(mass, center, sub, feat, lhs, fw, base):
    rows = dist_rows(mass, center) + mass_rows(mass, center)
    stage_rows(feat, rows, sub)
    for r in range(sub):
        at = slice(base + r * LANES, base + (r + 1) * LANES)
        left = feat[pl.ds(r, SROWS, stride=sub), :]
        lhs[at, 0:SROWS] = left.T.astype(bf16)
        right = feat[pl.ds(SROWS * sub + r, 16, stride=sub), :]
        fw[:, at] = right.astype(bf16)


def twice(left, high, low):
    return dot(jnp.concatenate([left, left], 1), jnp.concatenate([high, low], 0))


def pair_sums(cells, bodies, at_q, at_s, lhs, fw, fu, blhs, bfw, aw, au):
    targets = at_q.shape[1]
    wide = math.gcd(targets, UNIT)
    units = []
    for count, is_cell in ((cells, True), (bodies, False)):
        deep = math.gcd(count, UNIT) if count else 1
        for b in range(count // deep):
            for t in range(targets // wide):
                units.append((slice(b * deep, (b + 1) * deep), slice(t * wide, (t + 1) * wide), is_cell))
    aw[...] = jnp.zeros_like(aw)
    au[...] = jnp.zeros_like(au)

    def first(src, tgt, is_cell):
        if not is_cell:
            return dot(blhs[src, 0:SROWS], at_s[QROWS : QROWS + SROWS, tgt]), None
        s = dot(lhs[src, 0 : QROWS + SROWS], at_s[:, tgt])
        return s, dot(lhs[src, 0:QROWS], at_q[:, tgt])

    def second(src, tgt, is_cell, s, q):
        y = lax.rsqrt(s)
        y2 = y * y
        y3 = y * y2
        if not is_cell:
            aw[:, tgt] += twice(bfw[:, src], *halves(y3))
            return
        y5 = y3 * y2
        w = y3 + (q * y2) * y5
        aw[:, tgt] += twice(fw[:, src], *halves(w))
        au[:, tgt] += twice(fu[:, src], *halves(y5))

    ready = first(*units[0])
    for k, unit in enumerate(units):
        coming = first(*units[k + 1]) if k + 1 < len(units) else None
        second(*unit, *ready)
        ready = coming


def from_sums(x, y, z, aw, au):
    w = aw[0:4, :] + aw[4:8, :] + aw[8:12, :]
    u = au[0:9, :] + au[9:18, :] + au[18:27, :]

    def g(k):
        return u[k : k + 1, :]

    return (
        g(0) * x + g(3) * y + g(4) * z - g(6) - (w[0:1] * x - w[1:2]),
        g(3) * x + g(1) * y + g(5) * z - g(7) - (w[0:1] * y - w[2:3]),
        g(4) * x + g(5) * y + g(2) * z - g(8) - (w[0:1] * z - w[3:4]),
    )


def slot_place(lists, masks, level):
    at = slice(level * SUBS, (level + 1) * SUBS)
    index = lists[at, :]
    return jnp.where(masks[at, :] > 0, index >> 7, -1), index & (LANES - 1)


def picked(row, lane, lines, base, count, out):
    out = list(out)
    for k in range(count):
        hit = row == base + k
        for f in range(10):
            line = jnp.broadcast_to(lines(f, k), row.shape)
            got = jnp.take_along_axis(line, lane, axis=1, mode="promise_in_bounds")
            out[f] = jnp.where(hit, got, out[f])
    return out


def table_lines(table):
    rows = table.shape[0] // 10

    def line(f, k):
        return table[f * rows + k : f * rows + k + 1, :]

    return rows, line


def picked_tables(row, lane, tables):
    out = [jnp.zeros(row.shape, f32)] * 10
    base = 0
    for table in tables:
        rows, line = table_lines(table)
        out = picked(row, lane, line, base, rows, out)
        base += rows
    return out


def store_rows(to, values, count):
    for f, value in enumerate(values):
        to[f * count : (f + 1) * count, :] = value[0:count, :]


def open_kernel(count, *refs):
    sources, pick, here, sems = refs[:count], refs[count], refs[count + 1 : -1], refs[-1]
    moves = [pltpu.make_async_copy(a, b, sems.at[k]) for k, (a, b) in enumerate(zip(sources, here))]
    for move in moves:
        move.start()
    mass, center, quad, lists, masks = here[:5]
    for move in moves[:5]:
        move.wait()
    row, lane = slot_place(lists, masks, 0)

    def line(f, k):
        at = slice(k * LANES, (k + 1) * LANES)
        if f == 0:
            return mass[k : k + 1, :]
        return center[f - 1 : f, at] if f < 4 else quad[f - 4 : f - 3, at]

    zeros = [jnp.zeros(row.shape, f32)] * 10
    store_rows(pick, picked(row, lane, line, 0, mass.shape[0], zeros), row.shape[0])
    for move in moves[5:]:
        move.wait()


def packed(live, value, bits):
    subs = live.shape[0]
    at_row = lax.broadcasted_iota(jnp.int32, live.shape, 0)
    at_lane = lax.broadcasted_iota(jnp.int32, live.shape, 1)
    upper = lax.broadcasted_iota(jnp.int32, (LANES, LANES), 0) < lax.broadcasted_iota(jnp.int32, (LANES, LANES), 1)
    dead = jnp.where(live, 0.0, 1.0).astype(bf16)
    before = dot(dead, jnp.where(upper, 1.0, 0.0).astype(bf16))
    whole = dot(dead, jnp.ones((LANES, LANES), bf16))
    run = whole
    step = 1
    while step < subs:
        run = run + jnp.where(at_row >= step, pltpu.roll(run, step, axis=0), 0.0)
        step *= 2
    move = (before + run - whole).astype(jnp.int32)
    word = jnp.where(live, ((move + subs * LANES) << bits) + value, 0)
    step = 1
    shift = bits
    while step < subs * LANES:
        if step < LANES:
            turned = pltpu.roll(word, LANES - step, axis=1)
            come = jnp.where(at_lane < LANES - step, turned, pltpu.roll(turned, subs - 1, axis=0))
        else:
            come = pltpu.roll(word, subs - step // LANES, axis=0)
        stay = jnp.where((word >> shift) & 1 == 0, word, 0)
        word = jnp.where((come >> shift) & 1 == 1, come, stay)
        step *= 2
        shift += 1
    return word > 0, word & ((1 << bits) - 1)


def packed_place(row, lane, live):
    found, value = packed(live, row * LANES + lane, 13)
    return jnp.where(found, value >> 7, -1), value & (LANES - 1)


def packed_table(table, to, count):
    shape = (SUBS, LANES)
    index = lax.broadcasted_iota(jnp.int32, shape, 0) * LANES + lax.broadcasted_iota(jnp.int32, shape, 1)
    found, value = packed(table[0:SUBS, :] > 0.0, index, 10)
    row = jnp.where(found, value >> 7, -1)
    store_rows(to, picked_tables(row, value & (LANES - 1), [table]), count)


def read_cells(table, first, count, mid):
    rows, unused = table_lines(table)

    def row(f):
        return table[f * rows + first : f * rows + first + count, :]

    center = [row(1 + k) - mid[k : k + 1, :] for k in range(3)]
    return row(0), center, [row(4 + k) for k in range(6)]


def read_bodies(table, mid):
    blocks = table.shape[0] // 4
    center = [table[(1 + k) * blocks : (2 + k) * blocks, :] - mid[k : k + 1, :] for k in range(3)]
    return table[0:blocks, :], center, blocks


def span_features(spans, mid, feat, lhs, fw, fu):
    base = 0
    for table, first, count in spans:
        done = 0
        while done < count:
            sub = min(SUBS, count - done)
            cell_features(read_cells(table, first + done, sub, mid), sub, feat, lhs, fw, fu, base)
            base += sub * LANES
            done += sub
    return base


def store_sums(out, shifted, aw, au, parts=()):
    total = list(from_sums(shifted[0:1], shifted[1:2], shifted[2:3], aw, au))
    for part in parts:
        total = [t + part[k : k + 1, :] for k, t in enumerate(total)]
    for k in range(3):
        out[k : k + 1, :] = total[k]


def start_kernel(
    one_side, some, mass, center, quad, lists, masks, pos, weight, faces, counts,
    own, place, part, at_q, at_s, shifted, mid, face, out,
    tab, bod, feat, lhs, fw, fu, blhs, bfw, aw, au,
):
    slots = SUBS
    levels = lists.shape[0] // slots
    for level in range(levels):
        row, lane = slot_place(lists, masks, level)
        if level == levels - 1:
            row, lane = packed_place(row, lane, row >= 0)
        place[2 * level * slots : (2 * level + 1) * slots, :] = row
        place[(2 * level + 1) * slots : (2 * level + 2) * slots, :] = lane
    rows = mass.shape[0]
    for k in range(rows):
        at = slice(k * LANES, (k + 1) * LANES)
        tab[k * 16 : k * 16 + 1, :] = mass[k : k + 1, :]
        tab[k * 16 + 1 : k * 16 + 4, :] = center[:, at]
        tab[k * 16 + 4 : k * 16 + 10, :] = quad[:, at]
    for f in range(10):
        own[f * rows : (f + 1) * rows, :] = tab[pl.ds(f, rows, stride=16), :]

    targets = pos.shape[1]
    blocks = targets // LANES
    low = jnp.min(pos[...], axis=1, keepdims=True)
    high = jnp.max(pos[...], axis=1, keepdims=True)
    middle = jnp.broadcast_to(0.5 * (low + high), (3, LANES))
    mid[0:3, :] = middle
    bod[0:blocks, :] = weight[...]
    for k in range(blocks):
        at = slice(k * LANES, (k + 1) * LANES)
        here = pos[:, at]
        bod[pl.ds(blocks + k, 3, stride=blocks), :] = here
        shifted[0:3, at] = here - middle
    own_mass, own_center, unused = read_bodies(bod, mid)
    q, s = target_rows(*own_center)
    stage_rows(feat, q + s, blocks)
    for k in range(blocks):
        at = slice(k * LANES, (k + 1) * LANES)
        rows_here = feat[pl.ds(k, QROWS + SROWS, stride=blocks), :]
        at_q[:, at] = rows_here[0:QROWS].astype(bf16)
        at_s[0:QROWS, at] = jnp.zeros((QROWS, LANES), bf16)
        at_s[QROWS : QROWS + SROWS, at] = rows_here[QROWS : QROWS + SROWS].astype(bf16)
    body_features(own_mass, own_center, blocks, feat, blhs, bfw, 0)
    span_features([(own, 0, some)], mid, feat, lhs, fw, fu)

    lower = lax.axis_index("gz") > 0
    for k in range(1 if one_side else 2):
        order = jnp.where(lower, faces[0:1, :], faces[1:2, :]) if one_side else faces[k : k + 1, :]
        many = jnp.where(lower, counts[:, 0:1], counts[:, 1:2]) if one_side else counts[:, k : k + 1]
        for j in range(blocks):
            take = jnp.where(j < many, order[:, j : j + 1], -1)
            got = jnp.zeros((4, LANES), f32)
            for b in range(blocks):
                got = jnp.where(take == b, bod[pl.ds(b, 4, stride=blocks), :], got)
            face[pl.ds(k * 4 * blocks + j, 4, stride=blocks), :] = got
    row, lane = place[2 * slots : 3 * slots, :], place[3 * slots : 4 * slots, :]
    store_rows(part, picked_tables(row, lane, [own]), slots)
    pair_sums(some * LANES, targets, at_q, at_s, lhs, fw, fu, blhs, bfw, aw, au)
    store_sums(out, shifted, aw, au)


def placed(place, level):
    row = place[2 * level * SUBS : (2 * level + 1) * SUBS, :]
    return row, place[(2 * level + 1) * SUBS : (2 * level + 2) * SUBS, :]


def window_kernel(spans, ahead, dense, inside, count, bodies, at_q, at_s, shifted, mid, place, *refs):
    tables, sides = list(refs[:count]), refs[count : count + bodies]
    refs = list(refs[count + bodies :])
    out = refs.pop(0)
    for level, ids in ahead:
        row, lane = placed(place, level)
        store_rows(refs.pop(0), picked_tables(row, lane, [tables[k] for k in ids]), SUBS)
    if dense is not None:
        to = refs.pop(0)
        packed_table(tables[dense], to, to.shape[0] // 10)
    au, aw = refs.pop(), refs.pop()
    room = refs.pop() if inside is not None else None
    feat, lhs, fw, fu = refs[:4]
    blhs, bfw = refs[4:6] if bodies else (None, None)
    near = 0
    for side in sides:
        mass, center, blocks = read_bodies(side, mid)
        body_features(mass, center, blocks, feat, blhs, bfw, near)
        near += blocks * LANES
    if inside is not None:
        packed_table(tables[inside], room, room.shape[0] // 10)
        tables[inside] = room
    base = span_features([(tables[k], first, many) for k, first, many in spans], mid, feat, lhs, fw, fu)
    pair_sums(base, near, at_q, at_s, lhs, fw, fu, blhs, bfw, aw, au)
    store_sums(out, shifted, aw, au)


def pick_kernel(level, base, live, faces, place, part, table, *refs):
    row, lane = placed(place, level)
    rows, line = table_lines(table)
    out = [part[f * SUBS : (f + 1) * SUBS, :] for f in range(10)]
    store_rows(refs[-1], picked(row, lane, line, base, rows, out), live)
    if faces:
        refs[-1][10 * live :, :] = refs[0][...]


def last_kernel(merged, faces, parts, live, *refs):
    at_q, at_s, shifted, mid, table = refs[:5]
    sides = list(refs[5 : 5 + faces])
    sums = refs[5 + faces : 5 + faces + parts]
    out, feat, lhs, fw, fu, blhs, bfw, aw, au = refs[5 + faces + parts :]
    if merged:
        sides.append(table.at[10 * live :])
        table = table.at[: 10 * live]
    base = 0
    for side in sides:
        mass, center, blocks = read_bodies(side, mid)
        body_features(mass, center, blocks, feat, blhs, bfw, base)
        base += blocks * LANES
    count = span_features([(table, 0, live)], mid, feat, lhs, fw, fu)
    pair_sums(count, base, at_q, at_s, lhs, fw, fu, blhs, bfw, aw, au)
    store_sums(out, shifted, aw, au, sums)


def call(kernel, out_shape, args, scratch=(), in_specs=None, flops=0):
    specs = in_specs or [pl.BlockSpec(memory_space=pltpu.VMEM)] * len(args)
    many = isinstance(out_shape, (list, tuple))
    vmem = pl.BlockSpec(memory_space=pltpu.VMEM)
    return pl.pallas_call(
        kernel,
        out_shape=out_shape,
        in_specs=specs,
        out_specs=[vmem] * len(out_shape) if many else vmem,
        scratch_shapes=list(scratch),
        compiler_params=pltpu.CompilerParams(vmem_limit_bytes=32 * 2**20),
        cost_estimate=pl.CostEstimate(flops=flops * 64, bytes_accessed=2**18, transcendentals=0),
    )(*args)


def shaped(*shape, dtype=f32):
    return jax.ShapeDtypeStruct(shape, dtype)


def sum_scratch(targets, cells, bodies):
    got = [pltpu.VMEM(((QROWS + SROWS + FROWS) * SUBS, LANES), f32)]
    if cells:
        got += [pltpu.VMEM((cells, LANES), bf16), pltpu.VMEM((16, cells), bf16), pltpu.VMEM((32, cells), bf16)]
    if bodies:
        got += [pltpu.VMEM((bodies, LANES), bf16), pltpu.VMEM((16, bodies), bf16)]
    return got + [pltpu.VMEM((16, targets), f32), pltpu.VMEM((32, targets), f32)]


def swapped(value, apart):
    mask = 2**apart
    return lax.ppermute(value, AXES, [(k, k ^ mask) for k in range(lax.axis_size(AXES))])


def shards(body_pos, body_mass, cell_mass, cell_center, cell_quad, cell_lists, slot_masks, face_lists, face_counts):
    bits = lax.axis_size(AXES).bit_length() - 1
    levels, slots = cell_lists.shape[1:]
    targets = body_mass.shape[0]
    blocks = targets // LANES
    rows = cell_mass.shape[0] // LANES
    wide = slots // LANES
    live = LIVE // LANES
    near_by = lax.axis_size("gz")
    merged = near_by == 2 and bits == levels
    given = [cell_mass.reshape(rows, LANES), cell_center, cell_quad]
    given += [cell_lists.reshape(levels * wide, LANES), slot_masks.reshape(levels * wide, LANES)]
    given += [body_pos, body_mass.reshape(blocks, LANES), face_lists[0], face_counts]
    pick, *given = call(
        functools.partial(open_kernel, len(given)),
        [shaped(10 * wide, LANES)] + [shaped(*g.shape, dtype=g.dtype) for g in given],
        [pltpu.with_memory_space_constraint(g, pltpu.HBM) for g in given],
        [pltpu.SemaphoreType.DMA((len(given),))],
        [pl.BlockSpec(memory_space=pltpu.HBM)] * len(given),
    )
    arrived = swapped(pick, bits - 1)

    some = 3 * rows // 8
    own, place, part, at_q, at_s, shifted, mid, face, near = call(
        functools.partial(start_kernel, merged, some),
        [
            shaped(10 * rows, LANES),
            shaped(2 * levels * wide, LANES, dtype=jnp.int32),
            shaped(10 * wide, LANES),
            shaped(QROWS, targets, dtype=bf16),
            shaped(QROWS + SROWS, targets, dtype=bf16),
            shaped(SUBS, targets),
            shaped(SUBS, LANES),
            shaped((1 if merged else 2) * 4 * blocks, LANES),
            shaped(3, targets),
        ],
        given,
        [pltpu.VMEM((16 * rows, LANES), f32), pltpu.VMEM((4 * blocks, LANES), f32)]
        + sum_scratch(targets, some * LANES, targets),
        flops=targets * (some * LANES * 50 + targets * 20),
    )
    common = [at_q, at_s, shifted, mid]

    def window(spans, ahead=(), dense=None, inside=None, bodies=(), cost=1):
        tables = []
        for table in [span[0] for span in spans] + [t for item in ahead for t in item[1]] + [dense]:
            if table is not None and not any(table is known for known in tables):
                tables.append(table)

        def at(table):
            return None if table is None else [table is known for known in tables].index(True)

        count = sum(many for table, first, many in spans) * LANES
        kernel = functools.partial(
            window_kernel,
            [(at(table), first, many) for table, first, many in spans],
            [(level, [at(t) for t in some_tables]) for level, some_tables in ahead],
            at(dense),
            at(inside),
            len(tables),
            len(bodies),
        )
        outs = [shaped(3, targets)] + [shaped(10 * wide, LANES)] * len(ahead)
        outs += [shaped(10 * live, LANES)] if dense is not None else []
        scratch = sum_scratch(targets, count, targets * len(bodies))
        if inside is not None:
            scratch.insert(-2, pltpu.VMEM((10 * live, LANES), f32))
        flops = int(cost * targets * (count * 50 + len(bodies) * targets * 20))
        return call(kernel, outs, common + [place] + tables + list(bodies), scratch, flops=flops)

    sides = []
    if not merged:
        lower, upper = face[: 4 * blocks], face[4 * blocks :]
        sides = [
            lax.ppermute(upper, "gz", [(k, k + 1) for k in range(near_by - 1)]),
            lax.ppermute(lower, "gz", [(k + 1, k) for k in range(near_by - 1)]),
        ]

    def cut(start, stop):
        return (own, start * rows // 8, (stop - start) * rows // 8)

    tables = [own]
    dense = []
    sums = []
    tied = [near, part]
    for level in range(1, levels):
        tied = list(lax.optimization_barrier((arrived, *tied)))
        arrived = tied.pop(0)
        sums.append(tied.pop(0))
        part = tied.pop(0)
        dense += tied
        last = level == levels - 1
        extra = [face] if merged and last else []
        many = live if last else wide
        pick = call(
            functools.partial(pick_kernel, level, rows + (level - 1) * wide, many, len(extra)),
            shaped(10 * many + len(extra) * 4 * blocks, LANES),
            [place, part, arrived] + extra,
        )
        tables.append(arrived)
        newest = arrived
        arrived = swapped(pick, bits - 1 - level)
        if level == 1:
            spans = [cut(3, 5)]
        elif level == 2:
            spans = [cut(5, 7), (dense[0], 0, live)]
        elif level == 3:
            spans = [cut(7, 8), (dense[1], 0, live)]
        else:
            spans = [(dense[2], 0, live), (newest, 0, live)]
        ahead = [] if last else [(level + 1, list(tables))]
        tied = window(spans, ahead, None if last else newest, newest if last else None)
    sums += tied
    return call(
        functools.partial(last_kernel, merged, len(sides), len(sums), live),
        shaped(3, targets),
        common + [arrived] + sides + sums,
        sum_scratch(targets, live * LANES, targets * (len(sides) + merged)),
        flops=targets * LIVE * 50,
    )


def solution(mesh):
    in_specs = (
        P(None, AXES),
        P(AXES),
        P(AXES),
        P(None, AXES),
        P(None, AXES),
        P(AXES, None, None),
        P(AXES, None, None),
        P(AXES, None, None),
        P(AXES, None),
    )
    out_specs = P(None, AXES)
    return jax.shard_map(shards, mesh=mesh, in_specs=in_specs, out_specs=out_specs, check_vma=False)
```

```python
import functools
import math

import jax
import jax.numpy as jnp
from jax import lax
from jax.experimental import pallas as pl
from jax.experimental.pallas import tpu as pltpu
from jax.sharding import PartitionSpec as P

AXES = ("gx", "gy", "gz")
LANES = 128
SUBS = 8
LIVE = 768
SOFT = 0.01
QROWS = 64
SROWS = 32
FROWS = 48
UNIT = 256
A_PART = (0, 0, 1, 1, 0, 2)
B_PART = (0, 1, 0, 1, 2, 0)

f32 = jnp.float32
bf16 = jnp.bfloat16
dot = functools.partial(jnp.dot, preferred_element_type=f32)


def split3(value):
    one = value.astype(bf16).astype(f32)
    rest = value - one
    two = rest.astype(bf16).astype(f32)
    three = (rest - two).astype(bf16).astype(f32)
    return one, two, three


def halves(value):
    high = value.astype(bf16)
    return high, (value - high.astype(f32)).astype(bf16)


def paired(values, parts):
    pieces = [split3(v) for v in values]
    return [p[k] for k in parts for p in pieces]


def quad_rows(mass, center, quad):
    cx, cy, cz = center
    qxx, qyy, qzz, qxy, qxz, qyz = quad
    vx = qxx * cx + qxy * cy + qxz * cz
    vy = qxy * cx + qyy * cy + qyz * cz
    vz = qxz * cx + qyz * cy + qzz * cz
    h = 2.5 / jnp.maximum(mass, 1e-3)
    linear = [-2.0 * h * vx, -2.0 * h * vy, -2.0 * h * vz]
    square = [h * qxx, h * qyy, h * qzz, 2.0 * h * qxy, 2.0 * h * qxz, 2.0 * h * qyz]
    rows = list(split3(h * (cx * vx + cy * vy + cz * vz)))
    rows += paired(linear + square, B_PART)
    rows += [jnp.zeros_like(mass)] * (QROWS - len(rows))
    return rows, (vx, vy, vz)


def dist_rows(mass, center):
    cx, cy, cz = center
    rows = list(split3(cx * cx + cy * cy + cz * cz + SOFT))
    rows += paired([-2.0 * cx, -2.0 * cy, -2.0 * cz], B_PART)
    rows += [jnp.ones_like(mass)] * 3
    rows += [jnp.zeros_like(mass)] * (SROWS - len(rows))
    return rows


def mass_rows(mass, center):
    cx, cy, cz = center
    rows = paired([mass, mass * cx, mass * cy, mass * cz], (0, 1, 2))
    return rows + [jnp.zeros_like(mass)] * (16 - len(rows))


def moment_rows(quad, v):
    rows = paired(list(quad) + list(v), (0, 1, 2))
    return rows + [jnp.zeros_like(v[0])] * (32 - len(rows))


def target_rows(x, y, z):
    one = jnp.ones_like(x)
    zero = jnp.zeros_like(x)
    q = [one] * 3 + paired([x, y, z, x * x, y * y, z * z, x * y, x * z, y * z], A_PART)
    q += [zero] * (QROWS - len(q))
    s = [one] * 3 + paired([x, y, z], A_PART) + list(split3(x * x + y * y + z * z))
    s += [zero] * (SROWS - len(s))
    return q, s


def stage_rows(feat, rows, sub):
    for k, value in enumerate(rows):
        feat[k * sub : (k + 1) * sub, :] = value


def cell_features(read, sub, feat, lhs, fw, fu, base):
    mass, center, quad = read
    q, v = quad_rows(mass, center, quad)
    rows = q + dist_rows(mass, center) + mass_rows(mass, center) + moment_rows(quad, v)
    stage_rows(feat, rows, sub)
    wide = QROWS + SROWS
    for r in range(sub):
        at = slice(base + r * LANES, base + (r + 1) * LANES)
        left = feat[pl.ds(r, wide, stride=sub), :]
        lhs[at, 0:wide] = left.T.astype(bf16)
        right = feat[pl.ds(wide * sub + r, FROWS, stride=sub), :]
        fw[:, at] = right[0:16].astype(bf16)
        fu[:, at] = right[16:FROWS].astype(bf16)


def body_features(mass, center, sub, feat, lhs, fw, base):
    rows = dist_rows(mass, center) + mass_rows(mass, center)
    stage_rows(feat, rows, sub)
    for r in range(sub):
        at = slice(base + r * LANES, base + (r + 1) * LANES)
        left = feat[pl.ds(r, SROWS, stride=sub), :]
        lhs[at, 0:SROWS] = left.T.astype(bf16)
        right = feat[pl.ds(SROWS * sub + r, 16, stride=sub), :]
        fw[:, at] = right.astype(bf16)


def twice(left, high, low):
    return dot(jnp.concatenate([left, left], 1), jnp.concatenate([high, low], 0))


def pair_sums(cells, bodies, at_q, at_s, lhs, fw, fu, blhs, bfw, aw, au):
    targets = at_q.shape[1]
    wide = math.gcd(targets, UNIT)
    units = []
    for count, is_cell in ((bodies, False), (cells, True)):
        deep = math.gcd(count, UNIT) if count else 1
        for b in range(count // deep):
            for t in range(targets // wide):
                units.append((slice(b * deep, (b + 1) * deep), slice(t * wide, (t + 1) * wide), is_cell))
    aw[...] = jnp.zeros_like(aw)
    au[...] = jnp.zeros_like(au)

    def first(src, tgt, is_cell):
        if not is_cell:
            return dot(blhs[src, 0:SROWS], at_s[QROWS : QROWS + SROWS, tgt]), None
        s = dot(lhs[src, 0 : QROWS + SROWS], at_s[:, tgt])
        return s, dot(lhs[src, 0:QROWS], at_q[:, tgt])

    def second(src, tgt, is_cell, s, q):
        y = lax.rsqrt(s)
        y2 = y * y
        y3 = y * y2
        if not is_cell:
            aw[:, tgt] += twice(bfw[:, src], *halves(y3))
            return
        y5 = y3 * y2
        w = y3 + (q * y2) * y5
        aw[:, tgt] += twice(fw[:, src], *halves(w))
        au[:, tgt] += twice(fu[:, src], *halves(y5))

    ready = first(*units[0])
    for k, unit in enumerate(units):
        coming = first(*units[k + 1]) if k + 1 < len(units) else None
        second(*unit, *ready)
        ready = coming


def from_sums(x, y, z, aw, au):
    w = aw[0:4, :] + aw[4:8, :] + aw[8:12, :]
    u = au[0:9, :] + au[9:18, :] + au[18:27, :]

    def g(k):
        return u[k : k + 1, :]

    return (
        g(0) * x + g(3) * y + g(4) * z - g(6) - (w[0:1] * x - w[1:2]),
        g(3) * x + g(1) * y + g(5) * z - g(7) - (w[0:1] * y - w[2:3]),
        g(4) * x + g(5) * y + g(2) * z - g(8) - (w[0:1] * z - w[3:4]),
    )


def slot_place(lists, masks, level):
    at = slice(level * SUBS, (level + 1) * SUBS)
    index = lists[at, :]
    return jnp.where(masks[at, :] > 0, index >> 7, -1), index & (LANES - 1)


def picked(row, lane, lines, base, count, out):
    out = list(out)
    for k in range(count):
        hit = row == base + k
        for f in range(10):
            line = jnp.broadcast_to(lines(f, k), row.shape)
            got = jnp.take_along_axis(line, lane, axis=1, mode="promise_in_bounds")
            out[f] = jnp.where(hit, got, out[f])
    return out


def table_lines(table):
    rows = table.shape[0] // 10

    def line(f, k):
        return table[f * rows + k : f * rows + k + 1, :]

    return rows, line


def picked_tables(row, lane, tables):
    out = [jnp.zeros(row.shape, f32)] * 10
    base = 0
    for table in tables:
        rows, line = table_lines(table)
        out = picked(row, lane, line, base, rows, out)
        base += rows
    return out


def store_rows(to, values, count):
    for f, value in enumerate(values):
        to[f * count : (f + 1) * count, :] = value[0:count, :]


def open_kernel(count, *refs):
    sources, pick, here, sems = refs[:count], refs[count], refs[count + 1 : -1], refs[-1]
    moves = [pltpu.make_async_copy(a, b, sems.at[k]) for k, (a, b) in enumerate(zip(sources, here))]
    for move in moves:
        move.start()
    mass, center, quad, lists, masks = here[:5]
    for move in moves[:5]:
        move.wait()
    row, lane = slot_place(lists, masks, 0)

    def line(f, k):
        at = slice(k * LANES, (k + 1) * LANES)
        if f == 0:
            return mass[k : k + 1, :]
        return center[f - 1 : f, at] if f < 4 else quad[f - 4 : f - 3, at]

    zeros = [jnp.zeros(row.shape, f32)] * 10
    store_rows(pick, picked(row, lane, line, 0, mass.shape[0], zeros), row.shape[0])
    for move in moves[5:]:
        move.wait()


def packed(live, value, bits):
    subs = live.shape[0]
    at_row = lax.broadcasted_iota(jnp.int32, live.shape, 0)
    at_lane = lax.broadcasted_iota(jnp.int32, live.shape, 1)
    upper = lax.broadcasted_iota(jnp.int32, (LANES, LANES), 0) < lax.broadcasted_iota(jnp.int32, (LANES, LANES), 1)
    dead = jnp.where(live, 0.0, 1.0).astype(bf16)
    before = dot(dead, jnp.where(upper, 1.0, 0.0).astype(bf16))
    whole = dot(dead, jnp.ones((LANES, LANES), bf16))
    run = whole
    step = 1
    while step < subs:
        run = run + jnp.where(at_row >= step, pltpu.roll(run, step, axis=0), 0.0)
        step *= 2
    move = (before + run - whole).astype(jnp.int32)
    word = jnp.where(live, ((move + subs * LANES) << bits) + value, 0)
    step = 1
    shift = bits
    while step < subs * LANES:
        if step < LANES:
            turned = pltpu.roll(word, LANES - step, axis=1)
            come = jnp.where(at_lane < LANES - step, turned, pltpu.roll(turned, subs - 1, axis=0))
        else:
            come = pltpu.roll(word, subs - step // LANES, axis=0)
        stay = jnp.where((word >> shift) & 1 == 0, word, 0)
        word = jnp.where((come >> shift) & 1 == 1, come, stay)
        step *= 2
        shift += 1
    return word > 0, word & ((1 << bits) - 1)


def packed_place(row, lane, live):
    found, value = packed(live, row * LANES + lane, 13)
    return jnp.where(found, value >> 7, -1), value & (LANES - 1)


def packed_table(table, to, count):
    shape = (SUBS, LANES)
    index = lax.broadcasted_iota(jnp.int32, shape, 0) * LANES + lax.broadcasted_iota(jnp.int32, shape, 1)
    found, value = packed(table[0:SUBS, :] > 0.0, index, 10)
    row = jnp.where(found, value >> 7, -1)
    store_rows(to, picked_tables(row, value & (LANES - 1), [table]), count)


def read_cells(table, first, count, mid):
    rows, unused = table_lines(table)

    def row(f):
        return table[f * rows + first : f * rows + first + count, :]

    center = [row(1 + k) - mid[k : k + 1, :] for k in range(3)]
    return row(0), center, [row(4 + k) for k in range(6)]


def read_bodies(table, mid):
    blocks = table.shape[0] // 4
    center = [table[(1 + k) * blocks : (2 + k) * blocks, :] - mid[k : k + 1, :] for k in range(3)]
    return table[0:blocks, :], center, blocks


def span_features(spans, mid, feat, lhs, fw, fu):
    base = 0
    for table, first, count in spans:
        done = 0
        while done < count:
            sub = min(SUBS, count - done)
            cell_features(read_cells(table, first + done, sub, mid), sub, feat, lhs, fw, fu, base)
            base += sub * LANES
            done += sub
    return base


def store_sums(out, shifted, aw, au, parts=()):
    total = list(from_sums(shifted[0:1], shifted[1:2], shifted[2:3], aw, au))
    for part in parts:
        total = [t + part[k : k + 1, :] for k, t in enumerate(total)]
    for k in range(3):
        out[k : k + 1, :] = total[k]


def start_kernel(
    one_side, some, mass, center, quad, lists, masks, pos, weight, faces, counts,
    own, place, part, at_q, at_s, shifted, mid, face, out,
    tab, bod, feat, lhs, fw, fu, blhs, bfw, aw, au,
):
    slots = SUBS
    levels = lists.shape[0] // slots
    for level in range(levels):
        row, lane = slot_place(lists, masks, level)
        if level == levels - 1:
            row, lane = packed_place(row, lane, row >= 0)
        place[2 * level * slots : (2 * level + 1) * slots, :] = row
        place[(2 * level + 1) * slots : (2 * level + 2) * slots, :] = lane
    rows = mass.shape[0]
    for k in range(rows):
        at = slice(k * LANES, (k + 1) * LANES)
        tab[k * 16 : k * 16 + 1, :] = mass[k : k + 1, :]
        tab[k * 16 + 1 : k * 16 + 4, :] = center[:, at]
        tab[k * 16 + 4 : k * 16 + 10, :] = quad[:, at]
    for f in range(10):
        own[f * rows : (f + 1) * rows, :] = tab[pl.ds(f, rows, stride=16), :]

    targets = pos.shape[1]
    blocks = targets // LANES
    low = jnp.min(pos[...], axis=1, keepdims=True)
    high = jnp.max(pos[...], axis=1, keepdims=True)
    middle = jnp.broadcast_to(0.5 * (low + high), (3, LANES))
    mid[0:3, :] = middle
    bod[0:blocks, :] = weight[...]
    for k in range(blocks):
        at = slice(k * LANES, (k + 1) * LANES)
        here = pos[:, at]
        bod[pl.ds(blocks + k, 3, stride=blocks), :] = here
        shifted[0:3, at] = here - middle
    own_mass, own_center, unused = read_bodies(bod, mid)
    q, s = target_rows(*own_center)
    stage_rows(feat, q + s, blocks)
    for k in range(blocks):
        at = slice(k * LANES, (k + 1) * LANES)
        rows_here = feat[pl.ds(k, QROWS + SROWS, stride=blocks), :]
        at_q[:, at] = rows_here[0:QROWS].astype(bf16)
        at_s[0:QROWS, at] = jnp.zeros((QROWS, LANES), bf16)
        at_s[QROWS : QROWS + SROWS, at] = rows_here[QROWS : QROWS + SROWS].astype(bf16)
    body_features(own_mass, own_center, blocks, feat, blhs, bfw, 0)
    span_features([(own, 0, some)], mid, feat, lhs, fw, fu)

    lower = lax.axis_index("gz") > 0
    for k in range(1 if one_side else 2):
        order = jnp.where(lower, faces[0:1, :], faces[1:2, :]) if one_side else faces[k : k + 1, :]
        many = jnp.where(lower, counts[:, 0:1], counts[:, 1:2]) if one_side else counts[:, k : k + 1]
        for j in range(blocks):
            take = jnp.where(j < many, order[:, j : j + 1], -1)
            got = jnp.zeros((4, LANES), f32)
            for b in range(blocks):
                got = jnp.where(take == b, bod[pl.ds(b, 4, stride=blocks), :], got)
            face[pl.ds(k * 4 * blocks + j, 4, stride=blocks), :] = got
    row, lane = place[2 * slots : 3 * slots, :], place[3 * slots : 4 * slots, :]
    store_rows(part, picked_tables(row, lane, [own]), slots)
    pair_sums(some * LANES, targets, at_q, at_s, lhs, fw, fu, blhs, bfw, aw, au)
    store_sums(out, shifted, aw, au)


def placed(place, level):
    row = place[2 * level * SUBS : (2 * level + 1) * SUBS, :]
    return row, place[(2 * level + 1) * SUBS : (2 * level + 2) * SUBS, :]


def window_kernel(spans, ahead, dense, inside, count, parts, at_q, at_s, shifted, mid, place, *refs):
    tables, sums = list(refs[:count]), refs[count : count + parts]
    refs = list(refs[count + parts :])
    out = refs.pop(0)
    for level, ids in ahead:
        row, lane = placed(place, level)
        store_rows(refs.pop(0), picked_tables(row, lane, [tables[k] for k in ids]), SUBS)
    if dense is not None:
        to = refs.pop(0)
        packed_table(tables[dense], to, to.shape[0] // 10)
    au, aw = refs.pop(), refs.pop()
    room = refs.pop() if inside is not None else None
    feat, lhs, fw, fu = refs
    if inside is not None:
        packed_table(tables[inside], room, room.shape[0] // 10)
        tables[inside] = room
    base = span_features([(tables[k], first, many) for k, first, many in spans], mid, feat, lhs, fw, fu)
    pair_sums(base, 0, at_q, at_s, lhs, fw, fu, None, None, aw, au)
    store_sums(out, shifted, aw, au, sums)


def pick_kernel(level, base, live, faces, place, part, table, *refs):
    row, lane = placed(place, level)
    rows, line = table_lines(table)
    out = [part[f * SUBS : (f + 1) * SUBS, :] for f in range(10)]
    store_rows(refs[-1], picked(row, lane, line, base, rows, out), live)
    if faces:
        refs[-1][10 * live :, :] = refs[0][...]


def last_kernel(merged, faces, parts, live, *refs):
    at_q, at_s, shifted, mid, table = refs[:5]
    sides = list(refs[5 : 5 + faces])
    sums = refs[5 + faces : 5 + faces + parts]
    out, feat, lhs, fw, fu, blhs, bfw, aw, au = refs[5 + faces + parts :]
    if merged:
        sides.append(table.at[10 * live :])
        table = table.at[: 10 * live]
    base = 0
    for side in sides:
        mass, center, blocks = read_bodies(side, mid)
        body_features(mass, center, blocks, feat, blhs, bfw, base)
        base += blocks * LANES
    count = span_features([(table, 0, live)], mid, feat, lhs, fw, fu)
    pair_sums(count, base, at_q, at_s, lhs, fw, fu, blhs, bfw, aw, au)
    store_sums(out, shifted, aw, au, sums)


def call(kernel, out_shape, args, scratch=(), in_specs=None, flops=0):
    specs = in_specs or [pl.BlockSpec(memory_space=pltpu.VMEM)] * len(args)
    many = isinstance(out_shape, (list, tuple))
    vmem = pl.BlockSpec(memory_space=pltpu.VMEM)
    return pl.pallas_call(
        kernel,
        out_shape=out_shape,
        in_specs=specs,
        out_specs=[vmem] * len(out_shape) if many else vmem,
        scratch_shapes=list(scratch),
        compiler_params=pltpu.CompilerParams(vmem_limit_bytes=32 * 2**20),
        cost_estimate=pl.CostEstimate(flops=flops * 64, bytes_accessed=2**18, transcendentals=0),
    )(*args)


def shaped(*shape, dtype=f32):
    return jax.ShapeDtypeStruct(shape, dtype)


def sum_scratch(targets, cells, bodies):
    got = [pltpu.VMEM(((QROWS + SROWS + FROWS) * SUBS, LANES), f32)]
    if cells:
        got += [pltpu.VMEM((cells, LANES), bf16), pltpu.VMEM((16, cells), bf16), pltpu.VMEM((32, cells), bf16)]
    if bodies:
        got += [pltpu.VMEM((bodies, LANES), bf16), pltpu.VMEM((16, bodies), bf16)]
    return got + [pltpu.VMEM((16, targets), f32), pltpu.VMEM((32, targets), f32)]


def swapped(value, apart):
    mask = 2**apart
    return lax.ppermute(value, AXES, [(k, k ^ mask) for k in range(lax.axis_size(AXES))])


def shards(body_pos, body_mass, cell_mass, cell_center, cell_quad, cell_lists, slot_masks, face_lists, face_counts):
    bits = lax.axis_size(AXES).bit_length() - 1
    levels, slots = cell_lists.shape[1:]
    targets = body_mass.shape[0]
    blocks = targets // LANES
    rows = cell_mass.shape[0] // LANES
    wide = slots // LANES
    live = LIVE // LANES
    near_by = lax.axis_size("gz")
    merged = near_by == 2 and bits == levels
    given = [cell_mass.reshape(rows, LANES), cell_center, cell_quad]
    given += [cell_lists.reshape(levels * wide, LANES), slot_masks.reshape(levels * wide, LANES)]
    given += [body_pos, body_mass.reshape(blocks, LANES), face_lists[0], face_counts]
    pick, *given = call(
        functools.partial(open_kernel, len(given)),
        [shaped(10 * wide, LANES)] + [shaped(*g.shape, dtype=g.dtype) for g in given],
        [pltpu.with_memory_space_constraint(g, pltpu.HBM) for g in given],
        [pltpu.SemaphoreType.DMA((len(given),))],
        [pl.BlockSpec(memory_space=pltpu.HBM)] * len(given),
    )
    arrived = swapped(pick, bits - 1)

    some = 3 * rows // 8
    own, place, part, at_q, at_s, shifted, mid, face, near = call(
        functools.partial(start_kernel, merged, some),
        [
            shaped(10 * rows, LANES),
            shaped(2 * levels * wide, LANES, dtype=jnp.int32),
            shaped(10 * wide, LANES),
            shaped(QROWS, targets, dtype=bf16),
            shaped(QROWS + SROWS, targets, dtype=bf16),
            shaped(SUBS, targets),
            shaped(SUBS, LANES),
            shaped((1 if merged else 2) * 4 * blocks, LANES),
            shaped(3, targets),
        ],
        given,
        [pltpu.VMEM((16 * rows, LANES), f32), pltpu.VMEM((4 * blocks, LANES), f32)]
        + sum_scratch(targets, some * LANES, targets),
        flops=targets * (some * LANES * 50 + targets * 20),
    )
    common = [at_q, at_s, shifted, mid]

    def window(spans, ahead=(), dense=None, inside=None, parts=()):
        tables = []
        for table in [span[0] for span in spans] + [t for item in ahead for t in item[1]] + [dense]:
            if table is not None and not any(table is known for known in tables):
                tables.append(table)

        def at(table):
            return None if table is None else [table is known for known in tables].index(True)

        count = sum(many for table, first, many in spans) * LANES
        kernel = functools.partial(
            window_kernel,
            [(at(table), first, many) for table, first, many in spans],
            [(level, [at(t) for t in some_tables]) for level, some_tables in ahead],
            at(dense),
            at(inside),
            len(tables),
            len(parts),
        )
        outs = [shaped(3, targets)] + [shaped(10 * wide, LANES)] * len(ahead)
        outs += [shaped(10 * live, LANES)] if dense is not None else []
        scratch = sum_scratch(targets, count, 0)
        if inside is not None:
            scratch.insert(-2, pltpu.VMEM((10 * live, LANES), f32))
        args = common + [place] + tables + list(parts)
        return call(kernel, outs, args, scratch, flops=targets * count * 50)

    sides = []
    if not merged:
        lower, upper = face[: 4 * blocks], face[4 * blocks :]
        sides = [
            lax.ppermute(upper, "gz", [(k, k + 1) for k in range(near_by - 1)]),
            lax.ppermute(lower, "gz", [(k + 1, k) for k in range(near_by - 1)]),
        ]

    def cut(start, stop):
        return (own, start * rows // 8, (stop - start) * rows // 8)

    tables = [own]
    dense = []
    sums = []
    tied = [near, part]
    for level in range(1, levels):
        tied = list(lax.optimization_barrier((arrived, *tied)))
        arrived = tied.pop(0)
        sums.append(tied.pop(0))
        part = tied.pop(0)
        dense += tied
        last = level == levels - 1
        extra = [face] if merged and last else []
        many = live if last else wide
        pick = call(
            functools.partial(pick_kernel, level, rows + (level - 1) * wide, many, len(extra)),
            shaped(10 * many + len(extra) * 4 * blocks, LANES),
            [place, part, arrived] + extra,
        )
        tables.append(arrived)
        newest = arrived
        arrived = swapped(pick, bits - 1 - level)
        if level == 1:
            spans = [cut(3, 5)]
        elif level == 2:
            spans = [cut(5, 7), (dense[0], 0, live)]
        elif level == 3:
            spans = [cut(7, 8), (dense[1], 0, live)]
        else:
            spans = [(dense[2], 0, live), (newest, 0, live)]
        ahead = [] if last else [(level + 1, list(tables))]
        tied = window(spans, ahead, None if last else newest, newest if last else None, sums if last else ())

    sums = list(tied)
    return call(
        functools.partial(last_kernel, merged, len(sides), len(sums), live),
        shaped(3, targets),
        common + [arrived] + sides + sums,
        sum_scratch(targets, live * LANES, targets * (len(sides) + merged)),
        flops=targets * LIVE * 50,
    )


def solution(mesh):
    in_specs = (
        P(None, AXES),
        P(AXES),
        P(AXES),
        P(None, AXES),
        P(None, AXES),
        P(AXES, None, None),
        P(AXES, None, None),
        P(AXES, None, None),
        P(AXES, None),
    )
    out_specs = P(None, AXES)
    return jax.shard_map(shards, mesh=mesh, in_specs=in_specs, out_specs=out_specs, check_vma=False)
```

```python
import functools
import math

import jax
import jax.numpy as jnp
from jax import lax
from jax.experimental import pallas as pl
from jax.experimental.pallas import tpu as pltpu
from jax.sharding import PartitionSpec as P

AXES = ("gx", "gy", "gz")
LANES = 128
SUBS = 8
LIVE = 768
SOFT = 0.01
QROWS = 64
SROWS = 32
FROWS = 48
UNIT = 256
A_PART = (0, 0, 1, 1, 0, 2)
B_PART = (0, 1, 0, 1, 2, 0)

f32 = jnp.float32
bf16 = jnp.bfloat16
dot = functools.partial(jnp.dot, preferred_element_type=f32)


def split3(value):
    one = value.astype(bf16).astype(f32)
    rest = value - one
    two = rest.astype(bf16).astype(f32)
    three = (rest - two).astype(bf16).astype(f32)
    return one, two, three


def halves(value):
    high = value.astype(bf16)
    return high, (value - high.astype(f32)).astype(bf16)


def paired(values, parts):
    pieces = [split3(v) for v in values]
    return [p[k] for k in parts for p in pieces]


def quad_rows(mass, center, quad):
    cx, cy, cz = center
    qxx, qyy, qzz, qxy, qxz, qyz = quad
    vx = qxx * cx + qxy * cy + qxz * cz
    vy = qxy * cx + qyy * cy + qyz * cz
    vz = qxz * cx + qyz * cy + qzz * cz
    h = 2.5 / jnp.maximum(mass, 1e-3)
    linear = [-2.0 * h * vx, -2.0 * h * vy, -2.0 * h * vz]
    square = [h * qxx, h * qyy, h * qzz, 2.0 * h * qxy, 2.0 * h * qxz, 2.0 * h * qyz]
    rows = list(split3(h * (cx * vx + cy * vy + cz * vz)))
    rows += paired(linear + square, B_PART)
    rows += [jnp.zeros_like(mass)] * (QROWS - len(rows))
    return rows, (vx, vy, vz)


def dist_rows(mass, center):
    cx, cy, cz = center
    rows = list(split3(cx * cx + cy * cy + cz * cz + SOFT))
    rows += paired([-2.0 * cx, -2.0 * cy, -2.0 * cz], B_PART)
    rows += [jnp.ones_like(mass)] * 3
    rows += [jnp.zeros_like(mass)] * (SROWS - len(rows))
    return rows


def mass_rows(mass, center):
    cx, cy, cz = center
    rows = paired([mass, mass * cx, mass * cy, mass * cz], (0, 1, 2))
    return rows + [jnp.zeros_like(mass)] * (16 - len(rows))


def moment_rows(quad, v):
    rows = paired(list(quad) + list(v), (0, 1, 2))
    return rows + [jnp.zeros_like(v[0])] * (32 - len(rows))


def target_rows(x, y, z):
    one = jnp.ones_like(x)
    zero = jnp.zeros_like(x)
    q = [one] * 3 + paired([x, y, z, x * x, y * y, z * z, x * y, x * z, y * z], A_PART)
    q += [zero] * (QROWS - len(q))
    s = [one] * 3 + paired([x, y, z], A_PART) + list(split3(x * x + y * y + z * z))
    s += [zero] * (SROWS - len(s))
    return q, s


def stage_rows(feat, rows, sub):
    for k, value in enumerate(rows):
        feat[k * sub : (k + 1) * sub, :] = value


def cell_features(read, sub, feat, lhs, fw, fu, base):
    mass, center, quad = read
    q, v = quad_rows(mass, center, quad)
    rows = q + dist_rows(mass, center) + mass_rows(mass, center) + moment_rows(quad, v)
    stage_rows(feat, rows, sub)
    wide = QROWS + SROWS
    for r in range(sub):
        at = slice(base + r * LANES, base + (r + 1) * LANES)
        left = feat[pl.ds(r, wide, stride=sub), :]
        lhs[at, 0:wide] = left.T.astype(bf16)
        right = feat[pl.ds(wide * sub + r, FROWS, stride=sub), :]
        fw[:, at] = right[0:16].astype(bf16)
        fu[:, at] = right[16:FROWS].astype(bf16)


def body_features(mass, center, sub, feat, lhs, fw, base):
    rows = dist_rows(mass, center) + mass_rows(mass, center)
    stage_rows(feat, rows, sub)
    for r in range(sub):
        at = slice(base + r * LANES, base + (r + 1) * LANES)
        left = feat[pl.ds(r, SROWS, stride=sub), :]
        lhs[at, 0:SROWS] = left.T.astype(bf16)
        right = feat[pl.ds(SROWS * sub + r, 16, stride=sub), :]
        fw[:, at] = right.astype(bf16)


def twice(left, high, low):
    return dot(jnp.concatenate([left, left], 1), jnp.concatenate([high, low], 0))


def pair_sums(cells, bodies, at_q, at_s, lhs, fw, fu, blhs, bfw, aw, au):
    targets = at_q.shape[1]
    wide = math.gcd(targets, UNIT)
    units = []
    for count, is_cell in ((bodies, False), (cells, True)):
        deep = math.gcd(count, UNIT) if count else 1
        for b in range(count // deep):
            for t in range(targets // wide):
                units.append((slice(b * deep, (b + 1) * deep), slice(t * wide, (t + 1) * wide), is_cell))
    aw[...] = jnp.zeros_like(aw)
    au[...] = jnp.zeros_like(au)

    def first(src, tgt, is_cell):
        if not is_cell:
            return dot(blhs[src, 0:SROWS], at_s[QROWS : QROWS + SROWS, tgt]), None
        s = dot(lhs[src, 0 : QROWS + SROWS], at_s[:, tgt])
        return s, dot(lhs[src, 0:QROWS], at_q[:, tgt])

    def second(src, tgt, is_cell, s, q):
        y = lax.rsqrt(s)
        y2 = y * y
        y3 = y * y2
        if not is_cell:
            aw[:, tgt] += twice(bfw[:, src], *halves(y3))
            return
        y5 = y3 * y2
        w = y3 + (q * y2) * y5
        aw[:, tgt] += twice(fw[:, src], *halves(w))
        au[:, tgt] += twice(fu[:, src], *halves(y5))

    ready = first(*units[0])
    for k, unit in enumerate(units):
        coming = first(*units[k + 1]) if k + 1 < len(units) else None
        second(*unit, *ready)
        ready = coming


def from_sums(x, y, z, aw, au):
    w = aw[0:4, :] + aw[4:8, :] + aw[8:12, :]
    u = au[0:9, :] + au[9:18, :] + au[18:27, :]

    def g(k):
        return u[k : k + 1, :]

    return (
        g(0) * x + g(3) * y + g(4) * z - g(6) - (w[0:1] * x - w[1:2]),
        g(3) * x + g(1) * y + g(5) * z - g(7) - (w[0:1] * y - w[2:3]),
        g(4) * x + g(5) * y + g(2) * z - g(8) - (w[0:1] * z - w[3:4]),
    )


def slot_place(lists, masks, level):
    rows, lanes = [], []
    for r in range(lists.shape[1] // LANES):
        at = slice(r * LANES, (r + 1) * LANES)
        index = lists[level : level + 1, at]
        rows.append(jnp.where(masks[level : level + 1, at] > 0, index >> 7, -1))
        lanes.append(index & (LANES - 1))
    return jnp.concatenate(rows, 0), jnp.concatenate(lanes, 0)


def picked(row, lane, lines, base, count, out):
    out = list(out)
    for k in range(count):
        hit = row == base + k
        for f in range(10):
            line = jnp.broadcast_to(lines(f, k), row.shape)
            got = jnp.take_along_axis(line, lane, axis=1, mode="promise_in_bounds")
            out[f] = jnp.where(hit, got, out[f])
    return out


def table_lines(table):
    rows = table.shape[0] // 10

    def line(f, k):
        return table[f * rows + k : f * rows + k + 1, :]

    return rows, line


def picked_tables(row, lane, tables):
    out = [jnp.zeros(row.shape, f32)] * 10
    base = 0
    for table in tables:
        rows, line = table_lines(table)
        out = picked(row, lane, line, base, rows, out)
        base += rows
    return out


def store_rows(to, values, count):
    for f, value in enumerate(values):
        to[f * count : (f + 1) * count, :] = value[0:count, :]


def open_kernel(mass, center, quad, lists, masks, pick):
    row, lane = slot_place(lists, masks, 0)

    def line(f, k):
        at = slice(k * LANES, (k + 1) * LANES)
        if f == 0:
            return mass[k : k + 1, :]
        return center[f - 1 : f, at] if f < 4 else quad[f - 4 : f - 3, at]

    zeros = [jnp.zeros(row.shape, f32)] * 10
    store_rows(pick, picked(row, lane, line, 0, mass.shape[0], zeros), row.shape[0])


def packed(live, value, bits):
    subs = live.shape[0]
    at_row = lax.broadcasted_iota(jnp.int32, live.shape, 0)
    at_lane = lax.broadcasted_iota(jnp.int32, live.shape, 1)
    upper = lax.broadcasted_iota(jnp.int32, (LANES, LANES), 0) < lax.broadcasted_iota(jnp.int32, (LANES, LANES), 1)
    dead = jnp.where(live, 0.0, 1.0).astype(bf16)
    before = dot(dead, jnp.where(upper, 1.0, 0.0).astype(bf16))
    whole = dot(dead, jnp.ones((LANES, LANES), bf16))
    run = whole
    step = 1
    while step < subs:
        run = run + jnp.where(at_row >= step, pltpu.roll(run, step, axis=0), 0.0)
        step *= 2
    move = (before + run - whole).astype(jnp.int32)
    word = jnp.where(live, ((move + subs * LANES) << bits) + value, 0)
    step = 1
    shift = bits
    while step < subs * LANES:
        if step < LANES:
            turned = pltpu.roll(word, LANES - step, axis=1)
            come = jnp.where(at_lane < LANES - step, turned, pltpu.roll(turned, subs - 1, axis=0))
        else:
            come = pltpu.roll(word, subs - step // LANES, axis=0)
        stay = jnp.where((word >> shift) & 1 == 0, word, 0)
        word = jnp.where((come >> shift) & 1 == 1, come, stay)
        step *= 2
        shift += 1
    return word > 0, word & ((1 << bits) - 1)


def packed_place(row, lane, live):
    found, value = packed(live, row * LANES + lane, 13)
    return jnp.where(found, value >> 7, -1), value & (LANES - 1)


def packed_table(table, to, count):
    shape = (SUBS, LANES)
    index = lax.broadcasted_iota(jnp.int32, shape, 0) * LANES + lax.broadcasted_iota(jnp.int32, shape, 1)
    found, value = packed(table[0:SUBS, :] > 0.0, index, 10)
    row = jnp.where(found, value >> 7, -1)
    store_rows(to, picked_tables(row, value & (LANES - 1), [table]), count)


def read_cells(table, first, count, mid):
    rows, unused = table_lines(table)

    def row(f):
        return table[f * rows + first : f * rows + first + count, :]

    center = [row(1 + k) - mid[k : k + 1, :] for k in range(3)]
    return row(0), center, [row(4 + k) for k in range(6)]


def read_bodies(table, mid):
    blocks = table.shape[0] // 4
    center = [table[(1 + k) * blocks : (2 + k) * blocks, :] - mid[k : k + 1, :] for k in range(3)]
    return table[0:blocks, :], center, blocks


def span_features(spans, mid, feat, lhs, fw, fu):
    base = 0
    for table, first, count in spans:
        done = 0
        while done < count:
            sub = min(SUBS, count - done)
            cell_features(read_cells(table, first + done, sub, mid), sub, feat, lhs, fw, fu, base)
            base += sub * LANES
            done += sub
    return base


def store_sums(out, shifted, aw, au, parts=()):
    total = list(from_sums(shifted[0:1], shifted[1:2], shifted[2:3], aw, au))
    for part in parts:
        total = [t + part[k : k + 1, :] for k, t in enumerate(total)]
    for k in range(3):
        out[k : k + 1, :] = total[k]


def face_blocks(one_side, bod, faces, counts, face):
    blocks = bod.shape[0] // 4
    lower = lax.axis_index("gz") > 0
    for k in range(1 if one_side else 2):
        order = jnp.where(lower, faces[0:1, :], faces[1:2, :]) if one_side else faces[k : k + 1, :]
        many = jnp.where(lower, counts[:, 0:1], counts[:, 1:2]) if one_side else counts[:, k : k + 1]
        for j in range(blocks):
            take = jnp.where(j < many, order[:, j : j + 1], -1)
            got = jnp.zeros((4, LANES), f32)
            for b in range(blocks):
                got = jnp.where(take == b, bod[pl.ds(b, 4, stride=blocks), :], got)
            face[pl.ds(k * 4 * blocks + j, 4, stride=blocks), :] = got


def start_kernel(
    some, mass, center, quad, lists, masks, pos, weight,
    own, place, part, at_q, at_s, shifted, mid, bod, out,
    tab, feat, lhs, fw, fu, blhs, bfw, aw, au,
):
    slots = SUBS
    levels = lists.shape[0]
    for level in range(levels):
        row, lane = slot_place(lists, masks, level)
        if level == levels - 1:
            row, lane = packed_place(row, lane, row >= 0)
        place[2 * level * slots : (2 * level + 1) * slots, :] = row
        place[(2 * level + 1) * slots : (2 * level + 2) * slots, :] = lane
    rows = mass.shape[0]
    for k in range(rows):
        at = slice(k * LANES, (k + 1) * LANES)
        tab[k * 16 : k * 16 + 1, :] = mass[k : k + 1, :]
        tab[k * 16 + 1 : k * 16 + 4, :] = center[:, at]
        tab[k * 16 + 4 : k * 16 + 10, :] = quad[:, at]
    for f in range(10):
        own[f * rows : (f + 1) * rows, :] = tab[pl.ds(f, rows, stride=16), :]

    targets = pos.shape[1]
    blocks = targets // LANES
    low = jnp.min(pos[...], axis=1, keepdims=True)
    high = jnp.max(pos[...], axis=1, keepdims=True)
    middle = jnp.broadcast_to(0.5 * (low + high), (3, LANES))
    mid[0:3, :] = middle
    bod[0:blocks, :] = weight[...]
    for k in range(blocks):
        at = slice(k * LANES, (k + 1) * LANES)
        here = pos[:, at]
        bod[pl.ds(blocks + k, 3, stride=blocks), :] = here
        shifted[0:3, at] = here - middle
    own_mass, own_center, unused = read_bodies(bod, mid)
    q, s = target_rows(*own_center)
    stage_rows(feat, q + s, blocks)
    for k in range(blocks):
        at = slice(k * LANES, (k + 1) * LANES)
        rows_here = feat[pl.ds(k, QROWS + SROWS, stride=blocks), :]
        at_q[:, at] = rows_here[0:QROWS].astype(bf16)
        at_s[0:QROWS, at] = jnp.zeros((QROWS, LANES), bf16)
        at_s[QROWS : QROWS + SROWS, at] = rows_here[QROWS : QROWS + SROWS].astype(bf16)
    body_features(own_mass, own_center, blocks, feat, blhs, bfw, 0)
    span_features([(own, 0, some)], mid, feat, lhs, fw, fu)

    row, lane = place[2 * slots : 3 * slots, :], place[3 * slots : 4 * slots, :]
    store_rows(part, picked_tables(row, lane, [own]), slots)
    pair_sums(some * LANES, targets, at_q, at_s, lhs, fw, fu, blhs, bfw, aw, au)
    store_sums(out, shifted, aw, au)


def placed(place, level):
    row = place[2 * level * SUBS : (2 * level + 1) * SUBS, :]
    return row, place[(2 * level + 1) * SUBS : (2 * level + 2) * SUBS, :]


def window_kernel(spans, ahead, dense, inside, count, parts, sided, at_q, at_s, shifted, mid, place, *refs):
    if sided:
        bod, far, near, sems = refs[0], refs[1:3], refs[-3:-1], refs[-1]
        spot = 4 + count + parts + len(ahead) + (dense is not None)
        face = refs[spot]
        moves = [pltpu.make_async_copy(a, b, sems.at[k]) for k, (a, b) in enumerate(zip(far, near))]
        for move in moves:
            move.start()
        refs = refs[3:spot] + refs[spot + 1 : -3]
    tables, sums = list(refs[:count]), refs[count : count + parts]
    refs = list(refs[count + parts :])
    out = refs.pop(0)
    for level, ids in ahead:
        row, lane = placed(place, level)
        store_rows(refs.pop(0), picked_tables(row, lane, [tables[k] for k in ids]), SUBS)
    if dense is not None:
        to = refs.pop(0)
        packed_table(tables[dense], to, to.shape[0] // 10)
    au, aw = refs.pop(), refs.pop()
    room = refs.pop() if inside is not None else None
    feat, lhs, fw, fu = refs
    if inside is not None:
        packed_table(tables[inside], room, room.shape[0] // 10)
        tables[inside] = room
    base = span_features([(tables[k], first, many) for k, first, many in spans], mid, feat, lhs, fw, fu)
    pair_sums(base, 0, at_q, at_s, lhs, fw, fu, None, None, aw, au)
    store_sums(out, shifted, aw, au, sums)
    if sided:
        for move in moves:
            move.wait()
        face_blocks(sided == 1, bod, *near, face)


def pick_kernel(level, base, live, faces, place, part, table, *refs):
    row, lane = placed(place, level)
    rows, line = table_lines(table)
    out = [part[f * SUBS : (f + 1) * SUBS, :] for f in range(10)]
    store_rows(refs[-1], picked(row, lane, line, base, rows, out), live)
    if faces:
        refs[-1][10 * live :, :] = refs[0][...]


def last_kernel(merged, faces, parts, live, *refs):
    at_q, at_s, shifted, mid, table = refs[:5]
    sides = list(refs[5 : 5 + faces])
    sums = refs[5 + faces : 5 + faces + parts]
    out, feat, lhs, fw, fu, blhs, bfw, aw, au = refs[5 + faces + parts :]
    if merged:
        sides.append(table.at[10 * live :])
        table = table.at[: 10 * live]
    base = 0
    for side in sides:
        mass, center, blocks = read_bodies(side, mid)
        body_features(mass, center, blocks, feat, blhs, bfw, base)
        base += blocks * LANES
    count = span_features([(table, 0, live)], mid, feat, lhs, fw, fu)
    pair_sums(count, base, at_q, at_s, lhs, fw, fu, blhs, bfw, aw, au)
    store_sums(out, shifted, aw, au, sums)


def call(kernel, out_shape, args, scratch=(), in_specs=None, flops=0):
    specs = in_specs or [pl.BlockSpec(memory_space=pltpu.VMEM)] * len(args)
    many = isinstance(out_shape, (list, tuple))
    vmem = pl.BlockSpec(memory_space=pltpu.VMEM)
    return pl.pallas_call(
        kernel,
        out_shape=out_shape,
        in_specs=specs,
        out_specs=[vmem] * len(out_shape) if many else vmem,
        scratch_shapes=list(scratch),
        compiler_params=pltpu.CompilerParams(vmem_limit_bytes=32 * 2**20),
        cost_estimate=pl.CostEstimate(flops=flops * 64, bytes_accessed=2**18, transcendentals=0),
    )(*args)


def shaped(*shape, dtype=f32):
    return jax.ShapeDtypeStruct(shape, dtype)


def sum_scratch(targets, cells, bodies):
    got = [pltpu.VMEM(((QROWS + SROWS + FROWS) * SUBS, LANES), f32)]
    if cells:
        got += [pltpu.VMEM((cells, LANES), bf16), pltpu.VMEM((16, cells), bf16), pltpu.VMEM((32, cells), bf16)]
    if bodies:
        got += [pltpu.VMEM((bodies, LANES), bf16), pltpu.VMEM((16, bodies), bf16)]
    return got + [pltpu.VMEM((16, targets), f32), pltpu.VMEM((32, targets), f32)]


def swapped(value, apart):
    mask = 2**apart
    return lax.ppermute(value, AXES, [(k, k ^ mask) for k in range(lax.axis_size(AXES))])


def shards(body_pos, body_mass, cell_mass, cell_center, cell_quad, cell_lists, slot_masks, face_lists, face_counts):
    bits = lax.axis_size(AXES).bit_length() - 1
    levels, slots = cell_lists.shape[1:]
    targets = body_mass.shape[0]
    blocks = targets // LANES
    rows = cell_mass.shape[0] // LANES
    wide = slots // LANES
    live = LIVE // LANES
    near_by = lax.axis_size("gz")
    merged = near_by == 2 and bits == levels
    given = [cell_mass.reshape(rows, LANES), cell_center, cell_quad]
    given += [cell_lists[0], slot_masks[0]]
    pick = call(open_kernel, shaped(10 * wide, LANES), given)
    given += [body_pos, body_mass.reshape(blocks, LANES)]
    notes = [face_lists[0], face_counts]
    arrived = swapped(pick, bits - 1)

    some = 3 * rows // 8
    own, place, part, at_q, at_s, shifted, mid, bod, near = call(
        functools.partial(start_kernel, some),
        [
            shaped(10 * rows, LANES),
            shaped(2 * levels * wide, LANES, dtype=jnp.int32),
            shaped(10 * wide, LANES),
            shaped(QROWS, targets, dtype=bf16),
            shaped(QROWS + SROWS, targets, dtype=bf16),
            shaped(SUBS, targets),
            shaped(SUBS, LANES),
            shaped(4 * blocks, LANES),
            shaped(3, targets),
        ],
        given,
        [pltpu.VMEM((16 * rows, LANES), f32)]
        + sum_scratch(targets, some * LANES, targets),
        flops=targets * (some * LANES * 50 + targets * 20),
    )
    common = [at_q, at_s, shifted, mid]

    def window(spans, ahead=(), dense=None, inside=None, parts=(), sided=()):
        tables = []
        for table in [span[0] for span in spans] + [t for item in ahead for t in item[1]] + [dense]:
            if table is not None and not any(table is known for known in tables):
                tables.append(table)

        def at(table):
            return None if table is None else [table is known for known in tables].index(True)

        count = sum(many for table, first, many in spans) * LANES
        kernel = functools.partial(
            window_kernel,
            [(at(table), first, many) for table, first, many in spans],
            [(level, [at(t) for t in some_tables]) for level, some_tables in ahead],
            at(dense),
            at(inside),
            len(tables),
            len(parts),
            (1 if merged else 2) if sided else 0,
        )
        outs = [shaped(3, targets)] + [shaped(10 * wide, LANES)] * len(ahead)
        outs += [shaped(10 * live, LANES)] if dense is not None else []
        scratch = sum_scratch(targets, count, 0)
        if inside is not None:
            scratch.insert(-2, pltpu.VMEM((10 * live, LANES), f32))
        args = common + [place] + list(sided) + tables + list(parts)
        specs = [pl.BlockSpec(memory_space=pltpu.VMEM)] * len(args)
        if sided:
            for k in range(len(common) + 2, len(common) + 4):
                args[k] = pltpu.with_memory_space_constraint(args[k], pltpu.HBM)
                specs[k] = pl.BlockSpec(memory_space=pltpu.HBM)
            outs += [shaped((1 if merged else 2) * 4 * blocks, LANES)]
            scratch += [pltpu.VMEM(n.shape, n.dtype) for n in notes] + [pltpu.SemaphoreType.DMA((2,))]
        return call(kernel, outs, args, scratch, specs, flops=targets * count * 50)

    def cut(start, stop):
        return (own, start * rows // 8, (stop - start) * rows // 8)

    tables = [own]
    dense = []
    sums = []
    tied = [near, part]
    for level in range(1, levels):
        tied = list(lax.optimization_barrier((arrived, *tied)))
        arrived = tied.pop(0)
        sums.append(tied.pop(0))
        part = tied.pop(0)
        last = level == levels - 1
        if last:
            face = tied.pop()
        dense += tied
        extra = [face] if merged and last else []
        many = live if last else wide
        pick = call(
            functools.partial(pick_kernel, level, rows + (level - 1) * wide, many, len(extra)),
            shaped(10 * many + len(extra) * 4 * blocks, LANES),
            [place, part, arrived] + extra,
        )
        tables.append(arrived)
        newest = arrived
        arrived = swapped(pick, bits - 1 - level)
        if level == 1:
            spans = [cut(3, 5)]
        elif level == 2:
            spans = [cut(5, 7), (dense[0], 0, live)]
        elif level == 3:
            spans = [cut(7, 8), (dense[1], 0, live)]
        else:
            spans = [(dense[2], 0, live), (newest, 0, live)]
        sided = [bod, *notes] if level == levels - 2 else ()
        ahead = [] if last else [(level + 1, list(tables))]
        tied = window(spans, ahead, None if last else newest, newest if last else None, sums if last else (), sided)

    sides = []
    if not merged:
        lower, upper = face[: 4 * blocks], face[4 * blocks :]
        sides = [
            lax.ppermute(upper, "gz", [(k, k + 1) for k in range(near_by - 1)]),
            lax.ppermute(lower, "gz", [(k + 1, k) for k in range(near_by - 1)]),
        ]

    sums = list(tied)
    return call(
        functools.partial(last_kernel, merged, len(sides), len(sums), live),
        shaped(3, targets),
        common + [arrived] + sides + sums,
        sum_scratch(targets, live * LANES, targets * (len(sides) + merged)),
        flops=targets * LIVE * 50,
    )


def solution(mesh):
    in_specs = (
        P(None, AXES),
        P(AXES),
        P(AXES),
        P(None, AXES),
        P(None, AXES),
        P(AXES, None, None),
        P(AXES, None, None),
        P(AXES, None, None),
        P(AXES, None),
    )
    out_specs = P(None, AXES)
    return jax.shard_map(shards, mesh=mesh, in_specs=in_specs, out_specs=out_specs, check_vma=False)
```

```python
import functools
import math

import jax
import jax.numpy as jnp
from jax import lax
from jax.experimental import pallas as pl
from jax.experimental.pallas import tpu as pltpu
from jax.sharding import PartitionSpec as P

AXES = ("gx", "gy", "gz")
LANES = 128
SUBS = 8
LIVE = 768
SOFT = 0.01
QROWS = 64
SROWS = 32
FROWS = 48
UNIT = 256
A_PART = (0, 0, 1, 1, 0, 2)
B_PART = (0, 1, 0, 1, 2, 0)

f32 = jnp.float32
bf16 = jnp.bfloat16
dot = functools.partial(jnp.dot, preferred_element_type=f32)


def split3(value):
    one = value.astype(bf16).astype(f32)
    rest = value - one
    two = rest.astype(bf16).astype(f32)
    three = (rest - two).astype(bf16).astype(f32)
    return one, two, three


def halves(value):
    high = value.astype(bf16)
    return high, (value - high.astype(f32)).astype(bf16)


def paired(values, parts):
    pieces = [split3(v) for v in values]
    return [p[k] for k in parts for p in pieces]


def quad_rows(mass, center, quad):
    cx, cy, cz = center
    qxx, qyy, qzz, qxy, qxz, qyz = quad
    vx = qxx * cx + qxy * cy + qxz * cz
    vy = qxy * cx + qyy * cy + qyz * cz
    vz = qxz * cx + qyz * cy + qzz * cz
    h = 2.5 / jnp.maximum(mass, 1e-3)
    linear = [-2.0 * h * vx, -2.0 * h * vy, -2.0 * h * vz]
    square = [h * qxx, h * qyy, h * qzz, 2.0 * h * qxy, 2.0 * h * qxz, 2.0 * h * qyz]
    rows = list(split3(h * (cx * vx + cy * vy + cz * vz)))
    rows += paired(linear + square, B_PART)
    rows += [jnp.zeros_like(mass)] * (QROWS - len(rows))
    return rows, (vx, vy, vz)


def dist_rows(mass, center):
    cx, cy, cz = center
    rows = list(split3(cx * cx + cy * cy + cz * cz + SOFT))
    rows += paired([-2.0 * cx, -2.0 * cy, -2.0 * cz], B_PART)
    rows += [jnp.ones_like(mass)] * 3
    rows += [jnp.zeros_like(mass)] * (SROWS - len(rows))
    return rows


def mass_rows(mass, center):
    cx, cy, cz = center
    rows = paired([mass, mass * cx, mass * cy, mass * cz], (0, 1, 2))
    return rows + [jnp.zeros_like(mass)] * (16 - len(rows))


def moment_rows(quad, v):
    rows = paired(list(quad) + list(v), (0, 1, 2))
    return rows + [jnp.zeros_like(v[0])] * (32 - len(rows))


def target_rows(x, y, z):
    one = jnp.ones_like(x)
    zero = jnp.zeros_like(x)
    q = [one] * 3 + paired([x, y, z, x * x, y * y, z * z, x * y, x * z, y * z], A_PART)
    q += [zero] * (QROWS - len(q))
    s = [one] * 3 + paired([x, y, z], A_PART) + list(split3(x * x + y * y + z * z))
    s += [zero] * (SROWS - len(s))
    return q, s


def stage_rows(feat, rows, sub):
    for k, value in enumerate(rows):
        feat[k * sub : (k + 1) * sub, :] = value


def cell_features(read, sub, feat, lhs, fw, fu, base):
    mass, center, quad = read
    q, v = quad_rows(mass, center, quad)
    rows = q + dist_rows(mass, center) + mass_rows(mass, center) + moment_rows(quad, v)
    stage_rows(feat, rows, sub)
    wide = QROWS + SROWS
    for r in range(sub):
        at = slice(base + r * LANES, base + (r + 1) * LANES)
        left = feat[pl.ds(r, wide, stride=sub), :]
        lhs[at, 0:wide] = left.T.astype(bf16)
        right = feat[pl.ds(wide * sub + r, FROWS, stride=sub), :]
        fw[:, at] = right[0:16].astype(bf16)
        fu[:, at] = right[16:FROWS].astype(bf16)


def body_features(mass, center, sub, feat, lhs, fw, base):
    rows = dist_rows(mass, center) + mass_rows(mass, center)
    stage_rows(feat, rows, sub)
    for r in range(sub):
        at = slice(base + r * LANES, base + (r + 1) * LANES)
        left = feat[pl.ds(r, SROWS, stride=sub), :]
        lhs[at, 0:SROWS] = left.T.astype(bf16)
        right = feat[pl.ds(SROWS * sub + r, 16, stride=sub), :]
        fw[:, at] = right.astype(bf16)


def twice(left, high, low):
    return dot(jnp.concatenate([left, left], 1), jnp.concatenate([high, low], 0))


def pair_sums(cells, bodies, at_q, at_s, lhs, fw, fu, blhs, bfw, aw, au):
    targets = at_q.shape[1]
    wide = math.gcd(targets, UNIT)
    units = []
    for count, is_cell in ((bodies, False), (cells, True)):
        deep = math.gcd(count, UNIT) if count else 1
        for b in range(count // deep):
            for t in range(targets // wide):
                units.append((slice(b * deep, (b + 1) * deep), slice(t * wide, (t + 1) * wide), is_cell))
    aw[...] = jnp.zeros_like(aw)
    au[...] = jnp.zeros_like(au)

    def first(src, tgt, is_cell):
        if not is_cell:
            return dot(blhs[src, 0:SROWS], at_s[QROWS : QROWS + SROWS, tgt]), None
        s = dot(lhs[src, 0 : QROWS + SROWS], at_s[:, tgt])
        return s, dot(lhs[src, 0:QROWS], at_q[:, tgt])

    def second(src, tgt, is_cell, s, q):
        y = lax.rsqrt(s)
        y2 = y * y
        y3 = y * y2
        if not is_cell:
            aw[:, tgt] += twice(bfw[:, src], *halves(y3))
            return
        y5 = y3 * y2
        w = y3 + (q * y2) * y5
        aw[:, tgt] += twice(fw[:, src], *halves(w))
        au[:, tgt] += twice(fu[:, src], *halves(y5))

    ready = first(*units[0])
    for k, unit in enumerate(units):
        coming = first(*units[k + 1]) if k + 1 < len(units) else None
        second(*unit, *ready)
        ready = coming


def from_sums(x, y, z, aw, au):
    w = aw[0:4, :] + aw[4:8, :] + aw[8:12, :]
    u = au[0:9, :] + au[9:18, :] + au[18:27, :]

    def g(k):
        return u[k : k + 1, :]

    return (
        g(0) * x + g(3) * y + g(4) * z - g(6) - (w[0:1] * x - w[1:2]),
        g(3) * x + g(1) * y + g(5) * z - g(7) - (w[0:1] * y - w[2:3]),
        g(4) * x + g(5) * y + g(2) * z - g(8) - (w[0:1] * z - w[3:4]),
    )


def slot_place(lists, masks, level):
    rows, lanes = [], []
    for r in range(lists.shape[1] // LANES):
        at = slice(r * LANES, (r + 1) * LANES)
        index = lists[level : level + 1, at]
        rows.append(jnp.where(masks[level : level + 1, at] > 0, index >> 7, -1))
        lanes.append(index & (LANES - 1))
    return jnp.concatenate(rows, 0), jnp.concatenate(lanes, 0)


def picked(row, lane, lines, base, count, out):
    out = list(out)
    for k in range(count):
        hit = row == base + k
        for f in range(10):
            line = jnp.broadcast_to(lines(f, k), row.shape)
            got = jnp.take_along_axis(line, lane, axis=1, mode="promise_in_bounds")
            out[f] = jnp.where(hit, got, out[f])
    return out


def table_lines(table):
    rows = table.shape[0] // 10

    def line(f, k):
        return table[f * rows + k : f * rows + k + 1, :]

    return rows, line


def picked_tables(row, lane, tables):
    out = [jnp.zeros(row.shape, f32)] * 10
    base = 0
    for table in tables:
        rows, line = table_lines(table)
        out = picked(row, lane, line, base, rows, out)
        base += rows
    return out


def store_rows(to, values, count):
    for f, value in enumerate(values):
        to[f * count : (f + 1) * count, :] = value[0:count, :]


def open_kernel(mass, center, quad, lists, masks, pick):
    row, lane = slot_place(lists, masks, 0)

    def line(f, k):
        at = slice(k * LANES, (k + 1) * LANES)
        if f == 0:
            return mass[k : k + 1, :]
        return center[f - 1 : f, at] if f < 4 else quad[f - 4 : f - 3, at]

    zeros = [jnp.zeros(row.shape, f32)] * 10
    store_rows(pick, picked(row, lane, line, 0, mass.shape[0], zeros), row.shape[0])


def packed(live, value, bits):
    subs = live.shape[0]
    at_row = lax.broadcasted_iota(jnp.int32, live.shape, 0)
    at_lane = lax.broadcasted_iota(jnp.int32, live.shape, 1)
    upper = lax.broadcasted_iota(jnp.int32, (LANES, LANES), 0) < lax.broadcasted_iota(jnp.int32, (LANES, LANES), 1)
    dead = jnp.where(live, 0.0, 1.0).astype(bf16)
    before = dot(dead, jnp.where(upper, 1.0, 0.0).astype(bf16))
    whole = dot(dead, jnp.ones((LANES, LANES), bf16))
    run = whole
    step = 1
    while step < subs:
        run = run + jnp.where(at_row >= step, pltpu.roll(run, step, axis=0), 0.0)
        step *= 2
    move = (before + run - whole).astype(jnp.int32)
    word = jnp.where(live, ((move + subs * LANES) << bits) + value, 0)
    step = 1
    shift = bits
    while step < subs * LANES:
        if step < LANES:
            turned = pltpu.roll(word, LANES - step, axis=1)
            come = jnp.where(at_lane < LANES - step, turned, pltpu.roll(turned, subs - 1, axis=0))
        else:
            come = pltpu.roll(word, subs - step // LANES, axis=0)
        stay = jnp.where((word >> shift) & 1 == 0, word, 0)
        word = jnp.where((come >> shift) & 1 == 1, come, stay)
        step *= 2
        shift += 1
    return word > 0, word & ((1 << bits) - 1)


def packed_place(row, lane, live):
    found, value = packed(live, row * LANES + lane, 13)
    return jnp.where(found, value >> 7, -1), value & (LANES - 1)


def packed_table(table, to, count):
    shape = (SUBS, LANES)
    index = lax.broadcasted_iota(jnp.int32, shape, 0) * LANES + lax.broadcasted_iota(jnp.int32, shape, 1)
    found, value = packed(table[0:SUBS, :] > 0.0, index, 10)
    row = jnp.where(found, value >> 7, -1)
    store_rows(to, picked_tables(row, value & (LANES - 1), [table]), count)


def read_cells(table, first, count, mid):
    rows, unused = table_lines(table)

    def row(f):
        return table[f * rows + first : f * rows + first + count, :]

    center = [row(1 + k) - mid[k : k + 1, :] for k in range(3)]
    return row(0), center, [row(4 + k) for k in range(6)]


def read_bodies(table, mid):
    blocks = table.shape[0] // 4
    center = [table[(1 + k) * blocks : (2 + k) * blocks, :] - mid[k : k + 1, :] for k in range(3)]
    return table[0:blocks, :], center, blocks


def span_features(spans, mid, feat, lhs, fw, fu):
    base = 0
    for table, first, count in spans:
        done = 0
        while done < count:
            sub = min(SUBS, count - done)
            cell_features(read_cells(table, first + done, sub, mid), sub, feat, lhs, fw, fu, base)
            base += sub * LANES
            done += sub
    return base


def store_sums(out, shifted, aw, au, parts=()):
    total = list(from_sums(shifted[0:1], shifted[1:2], shifted[2:3], aw, au))
    for part in parts:
        total = [t + part[k : k + 1, :] for k, t in enumerate(total)]
    for k in range(3):
        out[k : k + 1, :] = total[k]


def face_blocks(one_side, bod, faces, counts, face):
    blocks = bod.shape[0] // 4
    lower = lax.axis_index("gz") > 0
    for k in range(1 if one_side else 2):
        order = jnp.where(lower, faces[0:1, :], faces[1:2, :]) if one_side else faces[k : k + 1, :]
        many = jnp.where(lower, counts[:, 0:1], counts[:, 1:2]) if one_side else counts[:, k : k + 1]
        for j in range(blocks):
            take = jnp.where(j < many, order[:, j : j + 1], -1)
            got = jnp.zeros((4, LANES), f32)
            for b in range(blocks):
                got = jnp.where(take == b, bod[pl.ds(b, 4, stride=blocks), :], got)
            face[pl.ds(k * 4 * blocks + j, 4, stride=blocks), :] = got


def start_kernel(
    some, mass, center, quad, lists, masks, pos, weight,
    own, place, part, at_q, at_s, shifted, mid, bod, out,
    tab, feat, lhs, fw, fu, blhs, bfw, aw, au,
):
    slots = SUBS
    levels = lists.shape[0]
    for level in range(levels):
        row, lane = slot_place(lists, masks, level)
        if level == levels - 1:
            row, lane = packed_place(row, lane, row >= 0)
        place[2 * level * slots : (2 * level + 1) * slots, :] = row
        place[(2 * level + 1) * slots : (2 * level + 2) * slots, :] = lane
    rows = mass.shape[0]
    for k in range(rows):
        at = slice(k * LANES, (k + 1) * LANES)
        tab[k * 16 : k * 16 + 1, :] = mass[k : k + 1, :]
        tab[k * 16 + 1 : k * 16 + 4, :] = center[:, at]
        tab[k * 16 + 4 : k * 16 + 10, :] = quad[:, at]
    for f in range(10):
        own[f * rows : (f + 1) * rows, :] = tab[pl.ds(f, rows, stride=16), :]

    targets = pos.shape[1]
    blocks = targets // LANES
    low = jnp.min(pos[...], axis=1, keepdims=True)
    high = jnp.max(pos[...], axis=1, keepdims=True)
    middle = jnp.broadcast_to(0.5 * (low + high), (3, LANES))
    mid[0:3, :] = middle
    bod[0:blocks, :] = weight[...]
    for k in range(blocks):
        at = slice(k * LANES, (k + 1) * LANES)
        here = pos[:, at]
        bod[pl.ds(blocks + k, 3, stride=blocks), :] = here
        shifted[0:3, at] = here - middle
    own_mass, own_center, unused = read_bodies(bod, mid)
    q, s = target_rows(*own_center)
    stage_rows(feat, q + s, blocks)
    for k in range(blocks):
        at = slice(k * LANES, (k + 1) * LANES)
        rows_here = feat[pl.ds(k, QROWS + SROWS, stride=blocks), :]
        at_q[:, at] = rows_here[0:QROWS].astype(bf16)
        at_s[0:QROWS, at] = jnp.zeros((QROWS, LANES), bf16)
        at_s[QROWS : QROWS + SROWS, at] = rows_here[QROWS : QROWS + SROWS].astype(bf16)
    body_features(own_mass, own_center, blocks, feat, blhs, bfw, 0)
    span_features([(own, 0, some)], mid, feat, lhs, fw, fu)

    row, lane = place[2 * slots : 3 * slots, :], place[3 * slots : 4 * slots, :]
    store_rows(part, picked_tables(row, lane, [own]), slots)
    pair_sums(some * LANES, targets, at_q, at_s, lhs, fw, fu, blhs, bfw, aw, au)
    store_sums(out, shifted, aw, au)


def placed(place, level):
    row = place[2 * level * SUBS : (2 * level + 1) * SUBS, :]
    return row, place[(2 * level + 1) * SUBS : (2 * level + 2) * SUBS, :]


def window_kernel(spans, ahead, dense, inside, count, parts, sided, at_q, at_s, shifted, mid, place, *refs):
    if sided:
        bod, far, near, sems = refs[0], refs[1:3], refs[-3:-1], refs[-1]
        spot = 4 + count + parts + len(ahead) + (dense is not None)
        face = refs[spot]
        moves = [pltpu.make_async_copy(a, b, sems.at[k]) for k, (a, b) in enumerate(zip(far, near))]
        for move in moves:
            move.start()
        refs = refs[3:spot] + refs[spot + 1 : -3]
    tables, sums = list(refs[:count]), refs[count : count + parts]
    refs = list(refs[count + parts :])
    out = refs.pop(0)
    for level, ids in ahead:
        row, lane = placed(place, level)
        store_rows(refs.pop(0), picked_tables(row, lane, [tables[k] for k in ids]), SUBS)
    if dense is not None:
        to = refs.pop(0)
        packed_table(tables[dense], to, to.shape[0] // 10)
    au, aw = refs.pop(), refs.pop()
    room = refs.pop() if inside is not None else None
    feat, lhs, fw, fu = refs
    if inside is not None:
        packed_table(tables[inside], room, room.shape[0] // 10)
        tables[inside] = room
    base = span_features([(tables[k], first, many) for k, first, many in spans], mid, feat, lhs, fw, fu)
    pair_sums(base, 0, at_q, at_s, lhs, fw, fu, None, None, aw, au)
    store_sums(out, shifted, aw, au, sums)
    if sided:
        for move in moves:
            move.wait()
        face_blocks(sided == 1, bod, *near, face)


def pick_kernel(level, base, live, faces, place, part, table, *refs):
    row, lane = placed(place, level)
    rows, line = table_lines(table)
    out = [part[f * SUBS : (f + 1) * SUBS, :] for f in range(10)]
    store_rows(refs[-1], picked(row, lane, line, base, rows, out), live)
    if faces:
        refs[-1][10 * live :, :] = refs[0][...]


def last_kernel(merged, faces, parts, live, *refs):
    at_q, at_s, shifted, mid, table = refs[:5]
    sides = list(refs[5 : 5 + faces])
    sums = refs[5 + faces : 5 + faces + parts]
    out, feat, lhs, fw, fu, blhs, bfw, aw, au = refs[5 + faces + parts :]
    if merged:
        sides.append(table.at[10 * live :])
        table = table.at[: 10 * live]
    base = 0
    for side in sides:
        mass, center, blocks = read_bodies(side, mid)
        body_features(mass, center, blocks, feat, blhs, bfw, base)
        base += blocks * LANES
    count = span_features([(table, 0, live)], mid, feat, lhs, fw, fu)
    pair_sums(count, base, at_q, at_s, lhs, fw, fu, blhs, bfw, aw, au)
    store_sums(out, shifted, aw, au, sums)


def call(kernel, out_shape, args, scratch=(), in_specs=None, flops=0):
    specs = in_specs or [pl.BlockSpec(memory_space=pltpu.VMEM)] * len(args)
    many = isinstance(out_shape, (list, tuple))
    vmem = pl.BlockSpec(memory_space=pltpu.VMEM)
    return pl.pallas_call(
        kernel,
        out_shape=out_shape,
        in_specs=specs,
        out_specs=[vmem] * len(out_shape) if many else vmem,
        scratch_shapes=list(scratch),
        compiler_params=pltpu.CompilerParams(vmem_limit_bytes=32 * 2**20),
        cost_estimate=pl.CostEstimate(flops=flops * 64, bytes_accessed=2**18, transcendentals=0),
    )(*args)


def shaped(*shape, dtype=f32):
    return jax.ShapeDtypeStruct(shape, dtype)


def sum_scratch(targets, cells, bodies):
    got = [pltpu.VMEM(((QROWS + SROWS + FROWS) * SUBS, LANES), f32)]
    if cells:
        got += [pltpu.VMEM((cells, LANES), bf16), pltpu.VMEM((16, cells), bf16), pltpu.VMEM((32, cells), bf16)]
    if bodies:
        got += [pltpu.VMEM((bodies, LANES), bf16), pltpu.VMEM((16, bodies), bf16)]
    return got + [pltpu.VMEM((16, targets), f32), pltpu.VMEM((32, targets), f32)]


def swapped(value, apart):
    mask = 2**apart
    return lax.ppermute(value, AXES, [(k, k ^ mask) for k in range(lax.axis_size(AXES))])


def shards(body_pos, body_mass, cell_mass, cell_center, cell_quad, cell_lists, slot_masks, face_lists, face_counts):
    bits = lax.axis_size(AXES).bit_length() - 1
    levels, slots = cell_lists.shape[1:]
    targets = body_mass.shape[0]
    blocks = targets // LANES
    rows = cell_mass.shape[0] // LANES
    wide = slots // LANES
    live = LIVE // LANES
    near_by = lax.axis_size("gz")
    merged = near_by == 2 and bits == levels
    given = [cell_mass.reshape(rows, LANES), cell_center, cell_quad]
    given += [cell_lists[0], slot_masks[0]]
    pick = call(open_kernel, shaped(10 * wide, LANES), given)
    given += [body_pos, body_mass.reshape(blocks, LANES)]
    notes = [face_lists[0], face_counts]
    arrived = swapped(pick, bits - 1)

    some = rows // 2
    own, place, part, at_q, at_s, shifted, mid, bod, near = call(
        functools.partial(start_kernel, some),
        [
            shaped(10 * rows, LANES),
            shaped(2 * levels * wide, LANES, dtype=jnp.int32),
            shaped(10 * wide, LANES),
            shaped(QROWS, targets, dtype=bf16),
            shaped(QROWS + SROWS, targets, dtype=bf16),
            shaped(SUBS, targets),
            shaped(SUBS, LANES),
            shaped(4 * blocks, LANES),
            shaped(3, targets),
        ],
        given,
        [pltpu.VMEM((16 * rows, LANES), f32)]
        + sum_scratch(targets, some * LANES, targets),
        flops=targets * (some * LANES * 50 + targets * 20),
    )
    common = [at_q, at_s, shifted, mid]

    def window(spans, ahead=(), dense=None, inside=None, parts=(), sided=()):
        tables = []
        for table in [span[0] for span in spans] + [t for item in ahead for t in item[1]] + [dense]:
            if table is not None and not any(table is known for known in tables):
                tables.append(table)

        def at(table):
            return None if table is None else [table is known for known in tables].index(True)

        count = sum(many for table, first, many in spans) * LANES
        kernel = functools.partial(
            window_kernel,
            [(at(table), first, many) for table, first, many in spans],
            [(level, [at(t) for t in some_tables]) for level, some_tables in ahead],
            at(dense),
            at(inside),
            len(tables),
            len(parts),
            (1 if merged else 2) if sided else 0,
        )
        outs = [shaped(3, targets)] + [shaped(10 * wide, LANES)] * len(ahead)
        outs += [shaped(10 * live, LANES)] if dense is not None else []
        scratch = sum_scratch(targets, count, 0)
        if inside is not None:
            scratch.insert(-2, pltpu.VMEM((10 * live, LANES), f32))
        args = common + [place] + list(sided) + tables + list(parts)
        specs = [pl.BlockSpec(memory_space=pltpu.VMEM)] * len(args)
        if sided:
            for k in range(len(common) + 2, len(common) + 4):
                args[k] = pltpu.with_memory_space_constraint(args[k], pltpu.HBM)
                specs[k] = pl.BlockSpec(memory_space=pltpu.HBM)
            outs += [shaped((1 if merged else 2) * 4 * blocks, LANES)]
            scratch += [pltpu.VMEM(n.shape, n.dtype) for n in notes] + [pltpu.SemaphoreType.DMA((2,))]
        return call(kernel, outs, args, scratch, specs, flops=targets * count * 50)

    def cut(start, stop):
        return (own, start * rows // 8, (stop - start) * rows // 8)

    tables = [own]
    dense = []
    sums = []
    tied = [near, part]
    for level in range(1, levels):
        tied = list(lax.optimization_barrier((arrived, *tied)))
        arrived = tied.pop(0)
        sums.append(tied.pop(0))
        part = tied.pop(0)
        last = level == levels - 1
        if last:
            face = tied.pop()
        dense += tied
        extra = [face] if merged and last else []
        many = live if last else wide
        pick = call(
            functools.partial(pick_kernel, level, rows + (level - 1) * wide, many, len(extra)),
            shaped(10 * many + len(extra) * 4 * blocks, LANES),
            [place, part, arrived] + extra,
        )
        tables.append(arrived)
        newest = arrived
        arrived = swapped(pick, bits - 1 - level)
        if level == 1:
            spans = [cut(4, 6)]
        elif level == 2:
            spans = [cut(6, 8), (dense[0], 0, live)]
        elif level == 3:
            spans = [(dense[1], 0, live)]
        else:
            spans = [(dense[2], 0, live), (newest, 0, live)]
        sided = [bod, *notes] if level == levels - 2 else ()
        ahead = [] if last else [(level + 1, list(tables))]
        tied = window(spans, ahead, None if last else newest, newest if last else None, sums if last else (), sided)

    sides = []
    if not merged:
        lower, upper = face[: 4 * blocks], face[4 * blocks :]
        sides = [
            lax.ppermute(upper, "gz", [(k, k + 1) for k in range(near_by - 1)]),
            lax.ppermute(lower, "gz", [(k + 1, k) for k in range(near_by - 1)]),
        ]

    sums = list(tied)
    return call(
        functools.partial(last_kernel, merged, len(sides), len(sums), live),
        shaped(3, targets),
        common + [arrived] + sides + sums,
        sum_scratch(targets, live * LANES, targets * (len(sides) + merged)),
        flops=targets * LIVE * 50,
    )


def solution(mesh):
    in_specs = (
        P(None, AXES),
        P(AXES),
        P(AXES),
        P(None, AXES),
        P(None, AXES),
        P(AXES, None, None),
        P(AXES, None, None),
        P(AXES, None, None),
        P(AXES, None),
    )
    out_specs = P(None, AXES)
    return jax.shard_map(shards, mesh=mesh, in_specs=in_specs, out_specs=out_specs, check_vma=False)
```
